128 devices in a mesh: clip: 32 (over x, z, y_lo), head: 4 (over y_hi, core).
Axes of the slice: x: 4, y: 4 (y_hi: 2, y_lo: 2; y = y_hi * 2 + y_lo), z: 4, core: 2. Of those that a mesh axis runs over, the one named last changes fastest.
Arguments:
- tokens: bfloat16 [50176, 768], P(('clip', 'head')), may hold values from -6 to 6
- cube_mask: int32 [32, 196], P('clip'), may hold values 0 or 1
- mask_token: bfloat16 [768], P(('clip', 'head')), may hold values from -4 to 4
- norm1_gain: bfloat16 [768], P(('clip', 'head')), may hold values from 0.099609375 to 1.8984375
- norm1_bias: bfloat16 [768], P(('clip', 'head')), may hold values from -3 to 3
- w_qkv: bfloat16 [768, 2304], P(None, 'head'), may hold values from -0.21875 to 0.21875
- qv_bias: bfloat16 [2, 768], P(None, 'head'), may hold values from -3 to 3
- w_out: bfloat16 [768, 768], P('head'), may hold values from -3.5 to 3.5
- proj_bias: bfloat16 [768], P(('clip', 'head')), may hold values from -3 to 3
- norm2_gain: bfloat16 [768], P(('clip', 'head')), may hold values from 0.099609375 to 1.8984375
- norm2_bias: bfloat16 [768], P(('clip', 'head')), may hold values from -3 to 3
- w_fc1: bfloat16 [768, 3072], P(None, ('clip', 'head')), may hold values from -0.21875 to 0.21875
- fc1_bias: bfloat16 [3072], P(('clip', 'head')), may hold values from -3 to 3
- w_fc2: bfloat16 [3072, 768], P(('clip', 'head')), may hold values from -0.109375 to 0.109375
- fc2_bias: bfloat16 [768], P(('clip', 'head')), may hold values from -3 to 3
- cotangent: bfloat16 [50176, 768], P(('clip', 'head')), may hold values from -6 to 6
Outputs:
- block_out: float32 [50176, 768], P(('clip', 'head'))
- tokens_grad: float32 [50176, 768], P(('clip', 'head'))
- mask_token_grad: float32 [768], P(('clip', 'head'))
- norm1_gain_grad: float32 [768], P(('clip', 'head'))
- norm1_bias_grad: float32 [768], P(('clip', 'head'))
- w_qkv_grad: float32 [768, 2304], P(None, 'head')
- qv_bias_grad: float32 [2, 768], P(None, 'head')
- w_out_grad: float32 [768, 768], P('head')
- proj_bias_grad: float32 [768], P(('clip', 'head'))
- norm2_gain_grad: float32 [768], P(('clip', 'head'))
- norm2_bias_grad: float32 [768], P(('clip', 'head'))
- w_fc1_grad: float32 [768, 3072], P(None, ('clip', 'head'))
- fc1_bias_grad: float32 [3072], P(('clip', 'head'))
- w_fc2_grad: float32 [3072, 768], P(('clip', 'head'))
- fc2_bias_grad: float32 [768], P(('clip', 'head'))
The draws below stay inside these ranges and needn't reach their ends.
Inputs may be any that keep to these rules, and one draw needn't show every extreme that they name: `cube_mask`: 1 marks a masked cube of 2 x 2 x 2 tubes.
All inputs are finite; a program needn't handle non-finite values. No bound on the sum of `cube_mask` on one device may be relied on, other than what follows from the above.
Results may differ from the reference program's by a relative error of at most 0.025.
Values may be sent and summed in bfloat16 or wider, within the bound.
A program may use at most 256 MiB of HBM per device.

```python
import math
import jax
import jax.numpy as jnp
from jax import lax

D = 768
HEADS = 12
HEAD_DIM = 64
FF = 3072
GRID = 14
TGRID = 8
TOK = 1568
CUBES = 196
CLIPS = 32
ROWS = 50176


def set_ends(values, rng, least, largest):
    longest = values.shape.index(max(values.shape))
    spots = []
    for shift in (0, 1):
        where = [jax.random.randint(jax.random.fold_in(rng, axis), (), 0, length) for axis, length in enumerate(values.shape)]
        where[longest] = (where[longest] + shift) % values.shape[longest]
        spots.append(tuple(where))
    return values.at[spots[0]].set(least).at[spots[1]].set(largest)


def levels(rng, shape, pieces, least, top_value):
    def one(axis_at, blocks):
        heights = jax.random.uniform(jax.random.fold_in(jax.random.fold_in(rng, 6), axis_at), (blocks,), jnp.float32, least / len(pieces), top_value / len(pieces))
        return jnp.repeat(jnp.exp(heights), shape[axis_at] // blocks).reshape((-1,) + (1,) * (len(shape) - axis_at - 1))

    loudness = one(*pieces[0])
    for cut in pieces[1:]:
        loudness = loudness * one(*cut)
    return loudness


def normal_values(key, dims, scale, most, cuts=(), kind=jnp.bfloat16):
    level = levels(key, dims, cuts, -0.22, 0.18) if cuts else 1.0
    result = jax.random.normal(key, dims, jnp.float32) * scale * level
    return jnp.minimum(jnp.maximum(result, -most), most).astype(kind)


def setup_inputs(seed: int = 0) -> dict:
    key_of = jax.random.split(jax.random.key(seed), 17)
    return {
        "tokens": normal_values(key_of[0], (ROWS, D), 1.0, 6.0, ((0, 128),)),
        "cube_mask": set_ends((jax.random.randint(key_of[1], (CLIPS, CUBES), 0, 5) < 2).astype(jnp.int32), jax.random.fold_in(key_of[1], 1), 0, 1),
        "mask_token": normal_values(key_of[2], (D,), 1.0, 4.0, ((0, 128),)),
        "norm1_gain": jnp.clip(1.0 + 0.18 * jax.random.normal(key_of[3], (D,), jnp.float32), 0.099609375, 1.8984375).astype(jnp.bfloat16),
        "norm1_bias": normal_values(key_of[4], (D,), 0.5, 3.0, ((0, 128),)),
        "w_qkv": normal_values(key_of[5], (D, 3 * D), D ** -0.5, 0.21875, ((1, 4),)),
        "qv_bias": normal_values(key_of[6], (2, D), 0.5, 3.0, ((1, 4),)),
        "w_out": normal_values(key_of[7], (D, D), (max(D // 256, 1)) ** -0.5, 3.5, ((0, 4),)),
        "proj_bias": normal_values(key_of[8], (D,), 0.5, 3.0, ((0, 128),)),
        "norm2_gain": jnp.clip(1.0 + 0.18 * jax.random.normal(key_of[9], (D,), jnp.float32), 0.099609375, 1.8984375).astype(jnp.bfloat16),
        "norm2_bias": normal_values(key_of[10], (D,), 0.5, 3.0, ((0, 128),)),
        "w_fc1": normal_values(key_of[11], (D, FF), D ** -0.5, 0.21875, ((1, 128),)),
        "fc1_bias": normal_values(key_of[12], (FF,), 0.5, 3.0, ((0, 128),)),
        "w_fc2": normal_values(key_of[13], (FF, D), FF ** -0.5, 0.109375, ((0, 128),)),
        "fc2_bias": normal_values(key_of[14], (D,), 0.5, 3.0, ((0, 128),)),
        "cotangent": normal_values(key_of[15], (ROWS, D), 1.0, 6.0, ((0, 128),)),
    }


@jax.custom_vjp
def low(v):
    return lax.optimization_barrier(v.astype(jnp.bfloat16)).astype(jnp.float32)

@jax.custom_vjp
def low_back(v):
    return v

def low_keep(v):
    return (low(v), None)

def low_pass(kept, grad):
    return (grad,)

def back_keep(v):
    return (v, None)

def back_low(kept, grad):
    return (low(grad),)
low.defvjp(low_keep, low_pass)
low_back.defvjp(back_keep, back_low)
highest = lax.Precision.HIGHEST
epsilon = 1e-06

def layer_norm(values, gain_vec, shift_vec):
    average = lax.optimization_barrier(jnp.mean(values, axis=-1, keepdims=True))
    centered = values - average
    variance = lax.optimization_barrier(jnp.mean(centered * centered, axis=-1, keepdims=True))
    return centered * lax.rsqrt(variance + epsilon) * gain_vec + shift_vec

def token_mask(cube_mask):
    half_grid = GRID // 2
    cubes = cube_mask.reshape(CLIPS, TGRID // 2, 1, half_grid, 1, half_grid, 1)
    spread = jnp.broadcast_to(cubes, (CLIPS, TGRID // 2, 2, half_grid, 2, half_grid, 2))
    return spread.reshape(CLIPS * TOK)

def attend(block):
    query = block[:, :, 0]
    keys = block[:, :, 1]
    values = block[:, :, 2]
    scores = jnp.einsum('qhe,khe->hqk', query, keys, precision=highest) * (1.0 / math.sqrt(HEAD_DIM))
    scores = low_back(scores)
    weights = low(jax.nn.softmax(scores, axis=-1))
    return jnp.einsum('hqk,khe->qhe', weights, values, precision=highest)

def forward(params, masked):
    tokens, mask_token, norm1_gain, norm1_bias, w_qkv, qv_bias, w_out, proj_bias, norm2_gain, norm2_bias, w_fc1, fc1_bias, w_fc2, fc2_bias = params
    start = jnp.where(masked[:, None] > 0, mask_token[None, :], tokens)
    normed1 = low(layer_norm(start, norm1_gain, norm1_bias))
    packed = jnp.dot(normed1, w_qkv, precision=highest).reshape(ROWS, HEADS, 3, HEAD_DIM)
    zero_row = jnp.zeros_like(qv_bias[0])
    bias_full = jnp.stack([qv_bias[0], zero_row, qv_bias[1]], axis=0).reshape(3, HEADS, HEAD_DIM)
    bias_full = jnp.transpose(bias_full, (1, 0, 2))
    packed = low_back(low(packed + bias_full[None]))
    mixed = lax.map(jax.checkpoint(attend), packed.reshape(CLIPS, TOK, HEADS, 3, HEAD_DIM))
    mixed = low_back(low(mixed.reshape(ROWS, D)))
    branch = low_back(jnp.dot(mixed, w_out, precision=highest))
    middle = start + branch + proj_bias
    normed2 = low(layer_norm(middle, norm2_gain, norm2_bias))
    inner = low_back(jnp.dot(normed2, w_fc1, precision=highest) + fc1_bias)
    active = low(jax.nn.gelu(inner, approximate=False))
    outer = low_back(jnp.dot(active, w_fc2, precision=highest))
    return middle + outer + fc2_bias

def reference(tokens, cube_mask, mask_token, norm1_gain, norm1_bias, w_qkv, qv_bias, w_out, proj_bias, norm2_gain, norm2_bias, w_fc1, fc1_bias, w_fc2, fc2_bias, cotangent):
    masked = token_mask(cube_mask)
    floats = tuple((item.astype(jnp.float32) for item in (tokens, mask_token, norm1_gain, norm1_bias, w_qkv, qv_bias, w_out, proj_bias, norm2_gain, norm2_bias, w_fc1, fc1_bias, w_fc2, fc2_bias)))

    def wrapped(params):
        return forward(params, masked)
    block_out, pullback = jax.vjp(wrapped, floats)
    grads = pullback(cotangent.astype(jnp.float32))[0]
    return (block_out, grads[0], grads[1], grads[2], grads[3], grads[4], grads[5], grads[6], grads[7], grads[8], grads[9], grads[10], grads[11], grads[12], grads[13])
```

```python
from functools import partial

import jax
import jax.numpy as jnp
import numpy as np
from jax import lax
from jax.experimental import pallas as pl
from jax.experimental.pallas import tpu as pltpu
from jax.sharding import PartitionSpec as P

HEAD_DIM = 64
GRID = 14
TOK = 1568
ROWS = 392
D = 768
HEADS_HERE = 3
QCHUNK = 224
CHUNKS = TOK // QCHUNK
UNITS = 384
BLOCKS = 8
epsilon = 1e-06
MESH = pl.DeviceIdType.MESH
VMEM_LIMIT = 60 * 2**20
f32 = jnp.float32
bf16 = jnp.bfloat16
GATHER = (("z", "x", "y"), ("y", "x", "z"), ("y", "z", "x"))
REDUCE = (("x", "z", "y"), ("z", "x", "y"))
RING = ("x", "y", "z")


def dot_nn(left, right):
    return jnp.dot(left, right, preferred_element_type=f32)


def dot_nt(left, right):
    return lax.dot_general(left, right, (((1,), (1,)), ((), ())), preferred_element_type=f32)


def dot_tn(left, right):
    return lax.dot_general(left, right, (((0,), (0,)), ((), ())), preferred_element_type=f32)


class Place:
    def __init__(self):
        clip = lax.axis_index("clip")
        head = lax.axis_index("head")
        self.head = head
        self.index = clip * 4 + head
        self.at = {"x": clip // 8, "y": (head // 2) * 2 + clip % 2, "z": (clip // 2) % 4}
        self.core = head % 2

    def device(self, at, core):
        return {
            "clip": at["x"] * 8 + at["z"] * 2 + at["y"] % 2,
            "head": (at["y"] // 2) * 2 + core,
        }

    def along(self, axis, step):
        at = dict(self.at)
        at[axis] = (at[axis] + step) % 4
        return self.device(at, self.core)

    def partner(self):
        return self.device(self.at, 1 - self.core)

    def across(self):
        at = dict(self.at)
        at["y"] = (at["y"] + 2) % 4
        return self.device(at, 1 - self.core)


def slot_of(axis, value):
    return (value % 2) * 2 + value // 2 if axis == "y" else value


def greet(here):
    barrier = pltpu.get_barrier_semaphore()
    peers = [here.partner(), here.across()]
    peers += [here.along(axis, step) for axis in RING for step in (1, 2, 3)]
    for device in peers:
        pl.semaphore_signal(barrier, inc=1, device_id=device, device_id_type=MESH)
    pl.semaphore_wait(barrier, len(peers))


def remote(src, dst, send, recv, device):
    return pltpu.make_async_remote_copy(
        src_ref=src, dst_ref=dst, send_sem=send, recv_sem=recv, device_id=device, device_id_type=MESH
    )


def ring_total(own, first, second, third):
    return (own + second) + (first + third)


class SmallSum:
    def __init__(self, here, held, arrived, send, recv):
        self.phases = []
        count = 0
        for phase, axis in enumerate(("core", "y", "x", "z")):
            devices = [here.partner()] if axis == "core" else [here.along(axis, k) for k in (1, 2, 3)]
            copies = []
            for device in devices:
                copies.append(
                    remote(held.at[phase], arrived.at[count], send.at[count], recv.at[count], device)
                )
                count += 1
            self.phases.append((copies, list(range(count - len(devices), count))))
        self.held, self.arrived = held, arrived

    def start(self, phase):
        for copy in self.phases[phase][0]:
            copy.start()

    def finish(self, phase):
        copies, slots = self.phases[phase]
        for copy in copies:
            copy.wait_recv()
        total = self.held[phase]
        if len(slots) == 1:
            total = total + self.arrived[slots[0]]
        else:
            total = ring_total(total, *[self.arrived[slot] for slot in slots])
        if phase < 3:
            self.held[phase + 1] = total
        return total

    def drain(self):
        for copies, _ in self.phases:
            for copy in copies:
                copy.wait_send()


def region(fixed):
    return tuple(fixed.get(axis, slice(None)) for axis in ("x", "z", "y"))


def row_mask(cubes, which):
    row = lax.broadcasted_iota(jnp.int32, (ROWS, 196), 0)
    spot = jnp.where(row >= GRID * GRID, row - GRID * GRID, row)
    line = (spot * 1171) >> 14
    cube = (line >> 1) * (GRID // 2) + ((spot - line * GRID) >> 1)
    here = lax.broadcasted_iota(jnp.int32, (ROWS, 196), 1) == cube + which * 49
    return jnp.sum(jnp.where(here, cubes[...].astype(f32), 0.0), axis=1, keepdims=True)


def unit_of(values):
    average = jnp.mean(values, axis=-1, keepdims=True)
    centered = values - average
    inverse = lax.rsqrt(jnp.mean(centered * centered, axis=-1, keepdims=True) + epsilon)
    return centered * inverse, inverse


def unit_back(scaled, unit, inverse):
    return inverse * (
        scaled
        - jnp.mean(scaled, axis=-1, keepdims=True)
        - unit * jnp.mean(scaled * unit, axis=-1, keepdims=True)
    )


MASK, GAIN1, SHIFT1, PROJ, GAIN2, SHIFT2, FC2B = range(7)


def forward_kernel(
    small, cubes, tokens, w_qkv, qv_bias, w_out, w_fc1, w_fc2,
    params, normed_out, qkv_out, lse_out, mixed_keep, mixed_out_keep, mixed_in_out, w_out_all_out, gathered,
    normed, qkv, lse, mixed, mixed_out, mixed_in, w_out_all,
    rows, held, arrived, own_half, their_half, chip_block, block, values_t,
    tok_send, tok_recv, sum_send, sum_recv, half_sem, ff_send, ff_recv, fwd_send, fwd_recv,
    out_send, out_recv, mix_send, mix_recv, local_sem,
):
    here = Place()
    core, head = here.core, here.head
    at = here.at
    mate = head + 1 - 2 * core
    far = (head + 2) % 4
    far_mate = far + 1 - 2 * core

    own_half[0] = w_fc1[...].astype(f32)
    own_half[1] = w_fc2[...].astype(f32)
    column = lax.broadcasted_iota(jnp.int32, (1, D), 1) - here.index * 6
    lines = []
    for k in range(7):
        placed = jnp.zeros((1, D), f32)
        for j in range(6):
            placed = jnp.where(column == j, small[k * 6 + j], placed)
        lines.append(placed)
    held[0, :, 0:D] = jnp.concatenate(lines + [jnp.zeros((1, D), f32)], axis=0)
    line = lax.broadcasted_iota(jnp.int32, (8, UNITS), 0)
    unit = lax.broadcasted_iota(jnp.int32, (8, UNITS), 1) - (here.index % 16) * 24
    shifted = jnp.zeros((8, UNITS), f32)
    for j in range(24):
        shifted = jnp.where(unit == j, small[42 + j], shifted)
    held[0, :, D : D + UNITS] = jnp.where(line == here.index // 16, shifted, 0.0)
    sums = SmallSum(here, held, arrived, sum_send, sum_recv)

    greet(here)
    sums.start(0)

    def tok_copy(way, k):
        lanes = pl.ds(k * 384, 384)
        src = rows.at[far, :, lanes] if way == 2 else tokens.at[:, lanes]
        dst = rows.at[far if way == 2 else head, :, lanes]
        device = here.along("y", 2) if way == 1 else here.partner()
        return remote(src, dst, tok_send.at[way, k], tok_recv.at[way, k], device)

    half_copy = remote(
        own_half.at[:, :, pl.ds(pl.multiple_of((1 - core) * UNITS, UNITS), UNITS)],
        their_half, half_sem.at[0], half_sem.at[1], here.partner(),
    )
    half_copy.start()
    sums.finish(0)
    sums.start(1)
    for way in (1, 0):
        for k in (0, 1):
            tok_copy(way, k).start()

    half_copy.wait_recv()
    mine = pl.ds(pl.multiple_of(core * 24, 8), 24)
    theirs = pl.ds(pl.multiple_of((1 - core) * 24, 8), 24)
    for kind in (0, 1):
        chip_block[kind, mine, :] = own_half[kind, :, pl.ds(pl.multiple_of(core * UNITS, UNITS), UNITS)]
        chip_block[kind, theirs, :] = their_half[kind]
    for part in range(3):
        for kind in (0, 1):
            block[part, kind * 48 : kind * 48 + 48, :] = chip_block[
                kind, :, part * 128 : part * 128 + 128
            ].astype(bf16)

    slots = {axis: slot_of(axis, at[axis]) for axis in RING}
    ours = pl.ds(core * 3, 3)
    block_copy = pltpu.make_async_copy(block, gathered.at[(ours,) + region(slots)], local_sem.at[0])

    def ff_copy(part, phase, step):
        order = GATHER[part]
        spot = gathered.at[(core * 3 + part,) + region({a: slots[a] for a in order[phase:]})]
        return remote(
            block.at[part] if phase == 0 else spot, spot,
            ff_send.at[part, phase, step - 1], ff_recv.at[part, phase, step - 1],
            here.along(order[phase], step),
        )

    def pass_copy(part, step):
        last = GATHER[part][2]
        plane = region({last: slot_of(last, (at[last] + 4 - step) % 4)})
        spot = gathered.at[(core * 3 + part,) + plane]
        return remote(spot, spot, fwd_send.at[part, step], fwd_recv.at[part, step], here.partner())

    def ff_start(part, phase):
        for step in (1, 2, 3):
            ff_copy(part, phase, step).start()

    def ff_on(part, phase):
        for step in (1, 2, 3):
            ff_copy(part, phase, step).wait_recv()
        ff_start(part, phase + 1)
        if phase == 1:
            pass_copy(part, 0).start()

    for part in range(3):
        ff_start(part, 0)
    block_copy.start()

    def out_copy(way):
        src = w_out_all.at[far] if way == 2 else w_out
        dst = w_out_all.at[far if way == 2 else head]
        device = here.along("y", 2) if way == 1 else here.partner()
        return remote(src, dst, out_send.at[way], out_recv.at[way], device)

    out_copy(0).start()
    w_out_all[head] = w_out[...]
    rows[head] = tokens[...]
    sums.finish(1)
    sums.start(2)
    block_copy.wait()
    ff_on(0, 0)
    sums.finish(2)
    sums.start(3)
    for k in (0, 1):
        tok_copy(0, k).wait_recv()
    params[...] = sums.finish(3)

    gain = params[GAIN1 : GAIN1 + 1, 0:D]
    shift = params[SHIFT1 : SHIFT1 + 1, 0:D]
    mask_token = params[MASK : MASK + 1, 0:D]
    biases = qv_bias[...].astype(f32)
    q_bias = biases[0:1, :]
    v_bias = biases[1:2, :]

    def project(half):
        parts = []
        for j in range(2):
            which = half * 2 + j
            masked = row_mask(cubes, which)
            start = jnp.where(masked > 0.5, mask_token, rows[which].astype(f32))
            unit1, _ = unit_of(start)
            parts.append(unit1 * gain + shift)
        normed[half] = jnp.concatenate(parts, axis=0).astype(bf16)

        def some(i, carry):
            part_rows = normed[half, pl.ds(pl.multiple_of(i * 112, 16), 112), :]
            to = pl.ds(pl.multiple_of(half * 784 + i * 112, 16), 112)
            packed = dot_nt(part_rows, w_qkv[...])
            for h in range(HEADS_HERE):
                lanes = slice(h * 64, h * 64 + 64)
                query = packed[:, h * 192 : h * 192 + 64] + q_bias[:, lanes]
                key = packed[:, h * 192 + 64 : h * 192 + 128]
                value = packed[:, h * 192 + 128 : h * 192 + 192] + v_bias[:, lanes]
                qkv[h * 3, to, :] = query.astype(bf16) * bf16(0.125)
                qkv[h * 3 + 1, to, :] = key.astype(bf16)
                qkv[h * 3 + 2, to, :] = value.astype(bf16)
            return carry

        lax.fori_loop(0, 7, some, 0)

    chip_half = head // 2
    project(chip_half)
    ff_on(0, 1)
    for k in (0, 1):
        tok_copy(1, k).wait_recv()
        tok_copy(2, k).start()
    for part in (1, 2):
        ff_on(part, 0)
    out_copy(1).start()
    for k in (0, 1):
        tok_copy(2, k).wait_recv()
    project(1 - chip_half)
    early = [
        pltpu.make_async_copy(normed, normed_out, local_sem.at[1]),
        pltpu.make_async_copy(qkv, qkv_out, local_sem.at[2]),
    ]
    for copy in early:
        copy.start()

    ones_row = (lax.broadcasted_iota(jnp.int32, (16, TOK), 0) == 0).astype(f32)
    for h in range(HEADS_HERE):
        values_t[h] = jnp.concatenate([qkv[h * 3 + 2].astype(f32).T, ones_row], axis=0).astype(bf16)

    def mix_copy(h, way):
        other, device = (
            (mate, here.partner()), (far, here.along("y", 2)), (far_mate, here.across()),
        )[way]
        return remote(
            mixed_out.at[h, other], mixed_in.at[h, head], mix_send.at[h, way], mix_recv.at[h, way], device
        )

    def mix_start(h):
        for j in range(4):
            mixed_out[h, j] = mixed[h, j * ROWS : j * ROWS + ROWS, :].astype(bf16)
        for way in (1, 2, 0):
            mix_copy(h, way).start()
        mixed_in[h, head] = mixed_out[h, head]

    def ff_pass(part, step):
        ff_copy(part, 2, step).wait_recv()
        pass_copy(part, step).start()

    def out_on():
        out_copy(1).wait_recv()
        out_copy(2).start()

    plan = [(CHUNKS - 1, partial(mix_start, 0)), (2 * CHUNKS - 1, partial(mix_start, 1))]
    plan += [(10, out_on), (3, partial(ff_on, 1, 1)), (4, partial(ff_on, 2, 1))]
    plan += [(12 + 3 * k + part, partial(ff_pass, part, k + 1)) for k in range(3) for part in range(3)]

    def attend(i, carry):
        h = i // CHUNKS
        chunk = pl.ds(pl.multiple_of((i % CHUNKS) * QCHUNK, 16), QCHUNK)
        scores = dot_nt(qkv[h * 3 + 1], qkv[h * 3, chunk, :])
        top = jnp.max(scores, axis=0, keepdims=True)
        weights = jnp.exp(scores - top).astype(bf16)
        outcome = dot_nn(values_t[h], weights)
        total = outcome[64:65, :]
        mixed[h, chunk, :] = (outcome[0:64, :] / total).T
        lse[i] = jnp.broadcast_to(top + jnp.log(total), (8, QCHUNK))
        for when, action in plan:
            pl.when(i == when)(action)
        return carry

    lax.fori_loop(0, HEADS_HERE * CHUNKS, attend, 0)

    mix_start(HEADS_HERE - 1)
    out_copy(0).wait_recv()
    out_copy(2).wait_recv()
    late = [
        pltpu.make_async_copy(lse, lse_out, local_sem.at[3]),
        pltpu.make_async_copy(mixed, mixed_keep, local_sem.at[4]),
        pltpu.make_async_copy(mixed_out, mixed_out_keep, local_sem.at[5]),
        pltpu.make_async_copy(w_out_all, w_out_all_out, local_sem.at[6]),
    ]
    for copy in late:
        copy.start()
    for part in range(3):
        for step in range(4):
            pass_copy(part, step).wait_recv()
    for h in range(HEADS_HERE):
        for way in range(3):
            mix_copy(h, way).wait_recv()
    last_copy = pltpu.make_async_copy(mixed_in, mixed_in_out, local_sem.at[7])
    last_copy.start()
    sums.drain()
    half_copy.wait_send()
    for way in range(3):
        out_copy(way).wait_send()
        for k in (0, 1):
            tok_copy(way, k).wait_send()
        for h in range(HEADS_HERE):
            mix_copy(h, way).wait_send()
    for part in range(3):
        for phase in range(3):
            for step in (1, 2, 3):
                ff_copy(part, phase, step).wait_send()
        for step in range(4):
            pass_copy(part, step).wait_send()
    for copy in early + late + [last_copy]:
        copy.wait()


VM = pl.BlockSpec(memory_space=pltpu.VMEM)
SM = pl.BlockSpec(memory_space=pltpu.SMEM)
ANY = pl.BlockSpec(memory_space=pl.ANY)
DMA = pltpu.SemaphoreType.DMA


def shape(dims, kind=bf16):
    return jax.ShapeDtypeStruct(dims, kind)


def forward_call(*args):
    kept = (
        ((2, 784, D), bf16),
        ((9, TOK, 64), bf16),
        ((HEADS_HERE * CHUNKS, 8, QCHUNK), f32),
        ((HEADS_HERE, TOK, 64), f32),
        ((HEADS_HERE, 4, ROWS, 64), bf16),
        ((HEADS_HERE, 4, ROWS, 64), bf16),
        ((4, 192, D), bf16),
    )
    return pl.pallas_call(
        forward_kernel,
        out_shape=(shape((8, D + UNITS), f32),)
        + tuple(shape(*k) for k in kept)
        + (shape((6, 4, 4, 4, 96, 128)),),
        in_specs=[SM] + [VM] * 7,
        out_specs=(VM,) + (ANY,) * 8,
        scratch_shapes=[pltpu.VMEM(*k) for k in kept]
        + [
            pltpu.VMEM((4, ROWS, D), bf16),
            pltpu.VMEM((4, 8, D + UNITS), f32),
            pltpu.VMEM((10, 8, D + UNITS), f32),
            pltpu.VMEM((2, 24, D), f32),
            pltpu.VMEM((2, 24, UNITS), f32),
            pltpu.VMEM((2, 48, UNITS), f32),
            pltpu.VMEM((3, 96, 128), bf16),
            pltpu.VMEM((HEADS_HERE, 80, TOK), bf16),
            DMA((3, 2)), DMA((3, 2)), DMA((10,)), DMA((10,)), DMA((2,)),
            DMA((3, 3, 3)), DMA((3, 3, 3)), DMA((3, 4)), DMA((3, 4)),
            DMA((3,)), DMA((3,)), DMA((HEADS_HERE, 3)), DMA((HEADS_HERE, 3)), DMA((8,)),
        ],
        name="attention_forward",
        compiler_params=pltpu.CompilerParams(
            collective_id=0, has_side_effects=True, vmem_limit_bytes=VMEM_LIMIT
        ),
    )(*args)


SQRT_HALF = 0.7071067811865476
INV_SQRT_2PI = 0.3989422804014327


def feed_forward_kernel(
    cubes, params, tokens, cotangent, mixed_in, w_out_all, weights,
    block_out, grad_middle, grad_branch, grad_mixed, small_grads, reduced_out,
    held, grads, arrived, reduced, normed2, outer, grad_normed2,
    load_sem, pair_send, pair_recv, keep_sem,
):
    here = Place()
    core, head = here.core, here.head

    def load(b):
        chips = pl.ds(b * 8, 8)
        return pltpu.make_async_copy(weights.at[:, chips], held.at[:, chips], load_sem.at[b])

    for b in range(BLOCKS):
        load(b).start()
    barrier = pltpu.get_barrier_semaphore()
    pl.semaphore_signal(barrier, inc=1, device_id=here.partner(), device_id_type=MESH)

    masked = row_mask(cubes, head)
    start = jnp.where(masked > 0.5, params[MASK : MASK + 1, 0:D], tokens[...].astype(f32))
    branch = jnp.zeros((ROWS, D), f32)
    for j in range(4):
        some = jnp.concatenate([mixed_in[h, j] for h in range(HEADS_HERE)], axis=1)
        branch = branch + dot_nn(some, w_out_all[j])
    middle = start + branch + params[PROJ : PROJ + 1, 0:D]
    gain2 = params[GAIN2 : GAIN2 + 1, 0:D]
    unit2, _ = unit_of(middle)
    normed2[...] = (unit2 * gain2 + params[SHIFT2 : SHIFT2 + 1, 0:D]).astype(bf16)
    block_out[...] = middle
    outer[...] = jnp.zeros((ROWS, D), f32)
    grad_normed2[...] = jnp.zeros((ROWS, D), f32)
    pl.semaphore_wait(barrier, 1)
    mates = pl.ds((1 - core) * 3, 3)

    def pair_copy(b):
        chips = pl.ds(b * 8, 8)
        return remote(
            grads.at[mates, chips], arrived.at[:, chips], pair_send.at[b], pair_recv.at[b], here.partner()
        )

    def keep_copy(b):
        chips = pl.ds(b * 8, 8)
        return pltpu.make_async_copy(reduced.at[:, chips], reduced_out.at[:, chips], keep_sem.at[b])

    def add_pair(b):
        chips = pl.ds(b * 8, 8)
        pair_copy(b).wait_recv()
        for part in range(3):
            reduced[part, chips] = (
                grads[core * 3 + part, chips].astype(f32) + arrived[part, chips].astype(f32)
            ).astype(bf16)
        keep_copy(b).start()

    def some_units(b, carry):
        chips = pl.ds(b * 8, 8)
        load(b).wait()

        def weight(kind):
            return jnp.concatenate(
                [
                    held[s, chips, kind * 48 : kind * 48 + 48, :].reshape(UNITS, 128)
                    for s in range(6)
                ],
                axis=1,
            )

        def keep(kind, grad):
            grad = grad.astype(bf16)
            for s in range(6):
                grads[s, chips, kind * 48 : kind * 48 + 48, :] = grad[
                    :, s * 128 : s * 128 + 128
                ].reshape(8, 48, 128)

        inner = dot_nt(normed2[...], weight(0)) + params[pl.ds(b, 1), D : D + UNITS]
        below = 0.5 + 0.5 * lax.erf(inner * SQRT_HALF)
        active = (inner * below).astype(bf16)
        slope = below + inner * (INV_SQRT_2PI * jnp.exp(-0.5 * inner * inner))
        grad_active = dot_nt(cotangent[...], weight(1))
        grad_inner = (grad_active * slope).astype(bf16)
        small_grads[pl.ds(b, 1), D : D + UNITS] = jnp.sum(
            grad_inner.astype(f32), axis=0, keepdims=True
        )
        outer[...] += dot_nn(active, weight(1))
        grad_normed2[...] += dot_nn(grad_inner, weight(0))
        keep(1, dot_tn(active, cotangent[...]))
        keep(0, dot_tn(grad_inner, normed2[...]))
        pair_copy(b).start()

        @pl.when(b > 0)
        def _():
            add_pair(b - 1)

        return carry

    lax.fori_loop(0, BLOCKS, some_units, 0)

    middle = block_out[...]
    block_out[...] = middle + outer[...] + params[FC2B : FC2B + 1, 0:D]
    unit2, inverse2 = unit_of(middle)
    grad_out = cotangent[...].astype(f32)
    back = grad_normed2[...]
    grad_mid = grad_out + unit_back(back * gain2, unit2, inverse2)
    grad_middle[...] = grad_mid
    low = grad_mid.astype(bf16)
    grad_branch[...] = low
    for j in range(4):
        some = dot_nt(low, w_out_all[j]).astype(bf16)
        for h in range(HEADS_HERE):
            grad_mixed[h, j] = some[:, h * 64 : h * 64 + 64]
    sums = [
        jnp.sum(v, axis=0, keepdims=True)
        for v in (grad_mid, back * unit2, back, grad_out)
    ]
    small_grads[:, 0:D] = jnp.concatenate(sums + [jnp.zeros((4, D), f32)], axis=0)
    add_pair(BLOCKS - 1)
    for b in range(BLOCKS):
        pair_copy(b).wait_send()
        keep_copy(b).wait()


def feed_forward_call(*args):
    return pl.pallas_call(
        feed_forward_kernel,
        out_shape=(
            shape((ROWS, D), f32),
            shape((ROWS, D), f32),
            shape((ROWS, D)),
            shape((HEADS_HERE, 4, ROWS, 64)),
            shape((8, D + UNITS), f32),
            shape((3, 64, 96, 128)),
        ),
        in_specs=[VM] * 6 + [ANY],
        out_specs=(VM,) * 5 + (ANY,),
        scratch_shapes=[
            pltpu.VMEM((6, 64, 96, 128), bf16),
            pltpu.VMEM((6, 64, 96, 128), bf16),
            pltpu.VMEM((3, 64, 96, 128), bf16),
            pltpu.VMEM((3, 64, 96, 128), bf16),
            pltpu.VMEM((ROWS, D), bf16),
            pltpu.VMEM((ROWS, D), f32),
            pltpu.VMEM((ROWS, D), f32),
            DMA((BLOCKS,)), DMA((BLOCKS,)), DMA((BLOCKS,)), DMA((BLOCKS,)),
        ],
        name="feed_forward",
        compiler_params=pltpu.CompilerParams(
            collective_id=1, has_side_effects=True, vmem_limit_bytes=VMEM_LIMIT
        ),
    )(*args)


def without(axes, axis):
    return tuple(a for a in axes if a != axis)


def backward_kernel(
    cubes, params, grad_mixed, grad_branch, small_grads, reduced,
    grad_middle_in, tokens_in, normed_in, qkv_in, lse_in, mixed_in, mixed_out_in, w_qkv_in,
    tokens_grad, small_first, small_last, w_grads, w_fc1_grad, w_fc2_grad,
    grad_middle, tokens, normed, qkv, lse, mixed, mixed_out, w_qkv, own_reduced,
    mixed_back, mixed_wide, outer_back, queries, keys_t, grad_q, grad_kv, packed_back,
    branch_in, input_back, pair_out, pair_in, far_out, far_in,
    held, arrived, held_last, arrived_last,
    ff_in0, ff_sum1, ff_in1, ff_sum2, ff_in2, ff_last, ff_mate,
    w_src, w_in, w_z, w_z_in, w_y, w_y_in, w_all, column_sums,
    mix_send, mix_recv, br_send, br_recv, in_send, in_recv, sum_send, sum_recv, last_send, last_recv,
    ff_send, ff_recv, mate_sem, wx_send, wx_recv, wz_send, wz_recv, wy_send, wy_recv, wg_send, wg_recv,
    load_sem,
):
    here = Place()
    core, head, at = here.core, here.head, here.at
    mate = head + 1 - 2 * core
    far = (head + 2) % 4
    far_mate = far + 1 - 2 * core
    slots = {axis: slot_of(axis, at[axis]) for axis in RING}

    def own_share(kind):
        axis = REDUCE[kind][0]
        return reduced.at[(slice(None),) + region({axis: slots[axis]}) + (pl.ds(kind * 48, 48),)]

    pairs = (
        (qkv_in, qkv), (lse_in, lse), (mixed_in, mixed), (tokens_in, tokens), (w_qkv_in, w_qkv),
        (normed_in, normed), (mixed_out_in, mixed_out), (grad_middle_in, grad_middle),
        (own_share(0), own_reduced.at[0]), (own_share(1), own_reduced.at[1]),
    )
    loads = [pltpu.make_async_copy(src, dst, load_sem.at[k]) for k, (src, dst) in enumerate(pairs)]
    for copy in loads:
        copy.start()
    greet(here)

    def mix_copy(h, way):
        other, device = (
            (mate, here.partner()), (far, here.along("y", 2)), (far_mate, here.across()),
        )[way]
        return remote(
            grad_mixed.at[h, other], mixed_back.at[h, head], mix_send.at[h, way], mix_recv.at[h, way], device
        )

    for h in range(HEADS_HERE):
        for way in (1, 2, 0):
            mix_copy(h, way).start()

    def peer_slot(axis, step):
        return slot_of(axis, (at[axis] + step) % 4)

    def ff_left(kind, phase):
        left = ("x", "z", "y")
        for done in REDUCE[kind][:phase]:
            left = without(left, done)
        return left

    def ff_copy(kind, phase, step):
        axis = REDUCE[kind][phase]
        where = tuple(
            peer_slot(axis, step) if a == axis else slice(None) for a in ff_left(kind, phase)
        )
        where = (slice(None),) + where
        if phase == 0:
            src = reduced.at[where + (pl.ds(kind * 48, 48),)]
        else:
            src = (ff_sum1, ff_sum2)[phase - 1].at[(kind,) + where]
        dst = (ff_in0, ff_in1, ff_in2)[phase]
        return remote(
            src, dst.at[kind, step - 1],
            ff_send.at[kind, phase, step - 1], ff_recv.at[kind, phase, step - 1],
            here.along(axis, step),
        )

    def ff_start(kind, phase):
        for step in (1, 2, 3):
            ff_copy(kind, phase, step).start()

    def ff_add(kind, phase):
        axis = REDUCE[kind][phase]
        where = tuple(slots[axis] if a == axis else slice(None) for a in ff_left(kind, phase))
        arrived_in = (ff_in0, ff_in1, ff_in2)[phase]
        for step in (1, 2, 3):
            ff_copy(kind, phase, step).wait_recv()
        if phase == 0:
            loads[8 + kind].wait()

        def some(part):
            if phase == 0:
                own = own_reduced[kind, part]
            else:
                own = (ff_sum1, ff_sum2)[phase - 1][(kind, part) + where]
            return ring_total(
                own.astype(f32), *[arrived_in[kind, k, part].astype(f32) for k in range(3)]
            )

        if phase == 0:
            @pl.loop(0, 3)
            def _(part):
                ff_sum1[kind, part] = some(part).astype(bf16)
        else:
            for part in range(3):
                total = some(part)
                if phase == 1:
                    ff_sum2[kind, part] = total.astype(bf16)
                else:
                    ff_last[kind, :, part * 128 : part * 128 + 128] = total

    for kind in (0, 1):
        ff_start(kind, 0)

    held[0] = small_grads[...]
    sums = SmallSum(here, held, arrived, sum_send, sum_recv)
    sums.start(0)

    beside = dict(at)
    beside["y"] = at["y"] + 1 - 2 * (at["y"] % 2)
    beside = here.device(beside, core)

    def wx_copy(n, step):
        return remote(
            w_src.at[n, (at["x"] + step) % 4], w_in.at[n, step - 1],
            wx_send.at[n, step - 1], wx_recv.at[n, step - 1], here.along("x", step),
        )

    def wz_copy(n, step):
        return remote(
            w_z.at[n], w_z_in.at[n, step - 1], wz_send.at[n, step - 1], wz_recv.at[n, step - 1],
            here.along("z", step),
        )

    def wy_copy(n):
        return remote(w_y.at[n], w_y_in.at[n], wy_send.at[n], wy_recv.at[n], beside)

    def wg_copy(n, step):
        return remote(
            w_all.at[n, at["x"]], w_all.at[n, at["x"]], wg_send.at[n, step - 1], wg_recv.at[n, step - 1],
            here.along("x", step),
        )

    def w_begin(n, grad):
        grad = grad.astype(bf16)
        for s in range(6):
            lanes = slice(s * 128, s * 128 + 128)
            first = s * 192
            for chunk in range(4):
                low, high = max(first, chunk * 288), min(first + 192, chunk * 288 + 288)
                if low < high:
                    w_src[n, chunk, low - chunk * 288 : high - chunk * 288, :] = grad[
                        low - first : high - first, lanes
                    ]
        for step in (1, 2, 3):
            wx_copy(n, step).start()

    def w_second(n):
        for step in (1, 2, 3):
            wx_copy(n, step).wait_recv()
        w_z[n] = ring_total(
            w_src[n, at["x"]].astype(f32), *[w_in[n, k].astype(f32) for k in range(3)]
        ).astype(bf16)
        for step in (1, 2, 3):
            wz_copy(n, step).start()

    def w_third(n):
        for step in (1, 2, 3):
            wz_copy(n, step).wait_recv()
        w_y[n] = ring_total(
            w_z[n].astype(f32), *[w_z_in[n, k].astype(f32) for k in range(3)]
        ).astype(bf16)
        wy_copy(n).start()

    def w_fourth(n):
        wy_copy(n).wait_recv()
        w_all[n, at["x"]] = (w_y[n].astype(f32) + w_y_in[n].astype(f32)).astype(bf16)
        for step in (1, 2, 3):
            wg_copy(n, step).start()

    def w_end(n):
        for step in (1, 2, 3):
            wg_copy(n, step).wait_recv()
        w_grads[n] = w_all[n]

    br_near = remote(grad_branch, branch_in.at[head], br_send.at[0], br_recv.at[0], here.partner())
    br_far = remote(grad_branch, branch_in.at[head], br_send.at[1], br_recv.at[1], here.along("y", 2))
    br_pass = remote(branch_in.at[far], branch_in.at[far], br_send.at[2], br_recv.at[2], here.partner())
    branch_in[head] = grad_branch[...]
    for h in range(HEADS_HERE):
        mixed_back[h, head] = grad_mixed[h, head]

    zeros = jnp.zeros((TOK, 64), bf16)
    loads[0].wait()
    for h in range(HEADS_HERE):
        query = qkv[h * 3]
        queries[h] = jnp.concatenate([zeros, query], axis=1)
        keys_t[h] = qkv[h * 3 + 1].astype(f32).T.astype(bf16)

    def outer_in(h):
        for way in range(3):
            mix_copy(h, way).wait_recv()
        for j in range(4):
            mixed_wide[j * ROWS : j * ROWS + ROWS, :] = mixed_back[h, j].astype(f32)
        outer_back[h] = jnp.concatenate([mixed_wide[...].astype(bf16), zeros], axis=1)

    outer_in(0)
    br_far.start()
    br_near.start()
    for k in (1, 2, 3, 4, 5, 6, 7):
        loads[k].wait()

    def steps(i, plan):
        for when, action in plan:
            pl.when(i == when)(action)

    def branch_on():
        br_far.wait_recv()
        br_pass.start()

    def branch_end():
        br_near.wait_recv()
        br_pass.wait_recv()
        grad = jnp.zeros((192, D), f32)
        for j in range(4):
            some = jnp.concatenate([mixed_out[h, j] for h in range(HEADS_HERE)], axis=1)
            grad = grad + dot_tn(some, branch_in[j])
        w_begin(0, grad)

    def sum_on(phase):
        def action():
            total = sums.finish(phase)
            if phase < 3:
                sums.start(phase + 1)
            else:
                small_first[...] = total
        return action

    def ff_on(part, phase):
        def action():
            ff_add(part, phase)
            if phase < 2:
                ff_start(part, phase + 1)
        return action

    plan = [(1, sum_on(0)), (3, sum_on(1)), (5, sum_on(2)), (7, sum_on(3))]
    plan += [(4, partial(outer_in, 1)), (10, partial(outer_in, 2))]
    plan += [(6, branch_on), (9, branch_end)]
    plan += [(11, partial(w_second, 0)), (13, partial(w_third, 0)), (15, partial(w_fourth, 0)), (17, partial(w_end, 0))]
    plan += [(9, partial(w_second, 1)), (11, partial(w_third, 1)), (13, partial(w_fourth, 1)), (15, partial(w_end, 1))]
    plan += [(16, partial(w_second, 2)), (18, partial(w_third, 2)), (20, partial(w_fourth, 2))]
    plan += [(12, ff_on(0, 0)), (13, ff_on(1, 0))]
    plan += [(16, ff_on(0, 1)), (17, ff_on(1, 1))]
    plan += [(19, ff_on(0, 2)), (20, ff_on(1, 2))]
    lane = lax.broadcasted_iota(jnp.int32, (TOK, 128), 1)

    def attend(i, carry):
        h = i // CHUNKS
        chunk = pl.ds(pl.multiple_of((i % CHUNKS) * QCHUNK, 16), QCHUNK)

        @pl.when(i % CHUNKS == 0)
        def _():
            grad_kv[...] = jnp.zeros((TOK, 128), f32)

        given = outer_back[h, chunk, :]
        given_mixed = given[:, 0:64]
        scores = dot_nt(qkv[h * 3 + 1], qkv[h * 3, chunk, :])
        weights = jnp.exp(scores - lse[i, 0:1, :])
        delta = jnp.sum((given_mixed.astype(f32) * mixed[h, chunk, :]).T, axis=0, keepdims=True)
        grad_weights = dot_nt(qkv[h * 3 + 2], given_mixed)
        grad_scores = (weights * (grad_weights - delta)).astype(bf16)
        grad_kv[...] += dot_nn(weights.astype(bf16), given) + dot_nn(grad_scores, queries[h, chunk, :])
        grad_q[chunk, 0:64] = dot_nn(keys_t[h], grad_scores).T * 0.125

        @pl.when(i % CHUNKS == CHUNKS - 1)
        def _():
            both = grad_kv[...]
            packed_back[:, 0:128] = jnp.where(lane < 64, grad_q[...], both).astype(bf16)
            packed_back[:, 128:192] = both[:, 0:64].astype(bf16)
            column_sums[pl.ds(h, 1), :] = jnp.sum(packed_back[...].astype(f32), axis=0, keepdims=True)
            for half in (0, 1):
                share = dot_nn(
                    packed_back[half * 784 : half * 784 + 784, :],
                    w_qkv[pl.ds(pl.multiple_of(h * 192, 16), 192), :],
                )
                for j in (0, 1):
                    some = share[j * ROWS : j * ROWS + ROWS]

                    @pl.when(h == 0)
                    def _():
                        input_back[half, j] = some

                    @pl.when(h > 0)
                    def _():
                        input_back[half, j] += some

            for n in range(HEADS_HERE):
                @pl.when(h == n)
                def _():
                    w_begin(n + 1, dot_tn(packed_back[...], normed[...]))

        steps(i, plan)
        return carry

    lax.fori_loop(0, HEADS_HERE * CHUNKS, attend, 0)

    chip = head // 2
    pair_out[0] = input_back[1 - chip, 1 - core].astype(bf16)
    pair_out[1] = input_back[chip, 1 - core].astype(bf16)
    pair_copies = [
        remote(pair_out.at[k], pair_in.at[k], in_send.at[k], in_recv.at[k], here.partner()) for k in (0, 1)
    ]
    for copy in pair_copies:
        copy.start()
    far_copy = remote(far_out, far_in, in_send.at[2], in_recv.at[2], here.along("y", 2))
    pair_copies[0].wait_recv()
    far_out[...] = (input_back[1 - chip, core] + pair_in[0].astype(f32)).astype(bf16)
    far_copy.start()
    w_second(3)

    mate_copy = remote(
        ff_last.at[:, pl.ds(pl.multiple_of((1 - core) * 24, 8), 24), :], ff_mate,
        mate_sem.at[0], mate_sem.at[1], here.partner(),
    )
    mate_copy.start()
    w_third(3)

    masked = row_mask(cubes, head)
    start = jnp.where(masked > 0.5, params[MASK : MASK + 1, 0:D], tokens[...].astype(f32))
    unit1, inverse1 = unit_of(start)
    mate_copy.wait_recv()
    for kind, target in ((0, w_fc1_grad), (1, w_fc2_grad)):
        target[:, pl.ds(pl.multiple_of(core * UNITS, UNITS), UNITS)] = ff_last[
            kind, pl.ds(pl.multiple_of(core * 24, 8), 24), :
        ]
        target[:, pl.ds(pl.multiple_of((1 - core) * UNITS, UNITS), UNITS)] = ff_mate[kind]
    w_end(2)
    w_fourth(3)
    pair_copies[1].wait_recv()
    near = input_back[chip, core] + pair_in[1].astype(f32)
    far_copy.wait_recv()
    back = near + far_in[...].astype(f32)
    grad_start = grad_middle[...] + unit_back(
        back * params[GAIN1 : GAIN1 + 1, 0:D], unit1, inverse1
    )
    tokens_grad[...] = jnp.where(masked > 0.5, 0.0, grad_start)
    totals = [
        jnp.sum(v, axis=0, keepdims=True)
        for v in (back * unit1, back, jnp.where(masked > 0.5, grad_start, 0.0))
    ]
    held_last[0, :, 0:384] = jnp.concatenate(
        [v[:, k * 384 : k * 384 + 384] for v in totals for k in (0, 1)] + [jnp.zeros((2, 384), f32)],
        axis=0,
    )
    line = lax.broadcasted_iota(jnp.int32, (8, 192), 0)
    of_query = jnp.concatenate([column_sums[h : h + 1, 0:64] for h in range(HEADS_HERE)], axis=1)
    of_value = jnp.concatenate([column_sums[h : h + 1, 128:192] for h in range(HEADS_HERE)], axis=1)
    held_last[0, :, 384:576] = jnp.where(
        line == 2 * head, of_query, jnp.where(line == 2 * head + 1, of_value, 0.0)
    )
    held_last[0, :, 576:640] = jnp.zeros((8, 64), f32)
    last = SmallSum(here, held_last, arrived_last, last_send, last_recv)
    last.start(0)
    w_end(3)
    for phase in range(3):
        last.finish(phase)
        last.start(phase + 1)
    small_last[...] = last.finish(3)

    sums.drain()
    last.drain()
    for copy in [br_near, br_far, br_pass, far_copy, mate_copy] + pair_copies:
        copy.wait_send()
    for h in range(HEADS_HERE):
        for way in range(3):
            mix_copy(h, way).wait_send()
    for kind in (0, 1):
        for phase in range(3):
            for step in (1, 2, 3):
                ff_copy(kind, phase, step).wait_send()
    for n in range(4):
        for step in (1, 2, 3):
            wx_copy(n, step).wait_send()
            wz_copy(n, step).wait_send()
            wg_copy(n, step).wait_send()
        wy_copy(n).wait_send()


def backward_call(*args):
    loaded = (
        ((ROWS, D), f32),
        ((ROWS, D), bf16),
        ((TOK, D), bf16),
        ((9, TOK, 64), bf16),
        ((HEADS_HERE * CHUNKS, 8, QCHUNK), f32),
        ((HEADS_HERE, TOK, 64), f32),
        ((HEADS_HERE, 4, ROWS, 64), bf16),
        ((576, D), bf16),
    )
    return pl.pallas_call(
        backward_kernel,
        out_shape=(
            shape((ROWS, D), f32),
            shape((8, D + UNITS), f32),
            shape((8, 640), f32),
            shape((4, 4, 288, 128)),
            shape((24, D), f32),
            shape((24, D), f32),
        ),
        in_specs=[VM] * 5 + [ANY] * 9,
        out_specs=(VM,) * 6,
        scratch_shapes=[pltpu.VMEM(*k) for k in loaded]
        + [
            pltpu.VMEM((2, 3, 4, 4, 48, 128), bf16),
            pltpu.VMEM((HEADS_HERE, 4, ROWS, 64), bf16),
            pltpu.VMEM((TOK, 64), f32),
            pltpu.VMEM((HEADS_HERE, TOK, 128), bf16),
            pltpu.VMEM((HEADS_HERE, TOK, 128), bf16),
            pltpu.VMEM((HEADS_HERE, 64, TOK), bf16),
            pltpu.VMEM((TOK, 128), f32),
            pltpu.VMEM((TOK, 128), f32),
            pltpu.VMEM((TOK, 192), bf16),
            pltpu.VMEM((4, ROWS, D), bf16),
            pltpu.VMEM((2, 2, ROWS, D), f32),
            pltpu.VMEM((2, ROWS, D), bf16),
            pltpu.VMEM((2, ROWS, D), bf16),
            pltpu.VMEM((ROWS, D), bf16),
            pltpu.VMEM((ROWS, D), bf16),
            pltpu.VMEM((4, 8, D + UNITS), f32),
            pltpu.VMEM((10, 8, D + UNITS), f32),
            pltpu.VMEM((4, 8, 640), f32),
            pltpu.VMEM((10, 8, 640), f32),
            pltpu.VMEM((2, 3, 3, 4, 4, 48, 128), bf16),
            pltpu.VMEM((2, 3, 4, 4, 48, 128), bf16),
            pltpu.VMEM((2, 3, 3, 4, 48, 128), bf16),
            pltpu.VMEM((2, 3, 4, 48, 128), bf16),
            pltpu.VMEM((2, 3, 3, 48, 128), bf16),
            pltpu.VMEM((2, 48, UNITS), f32),
            pltpu.VMEM((2, 24, UNITS), f32),
            pltpu.VMEM((4, 4, 288, 128), bf16),
            pltpu.VMEM((4, 3, 288, 128), bf16),
            pltpu.VMEM((4, 288, 128), bf16),
            pltpu.VMEM((4, 3, 288, 128), bf16),
            pltpu.VMEM((4, 288, 128), bf16),
            pltpu.VMEM((4, 288, 128), bf16),
            pltpu.VMEM((4, 4, 288, 128), bf16),
            pltpu.VMEM((8, 192), f32),
            DMA((HEADS_HERE, 3)), DMA((HEADS_HERE, 3)), DMA((3,)), DMA((3,)), DMA((3,)), DMA((3,)),
            DMA((10,)), DMA((10,)), DMA((10,)), DMA((10,)),
            DMA((2, 3, 3)), DMA((2, 3, 3)), DMA((2,)),
            DMA((4, 3)), DMA((4, 3)), DMA((4, 3)), DMA((4, 3)), DMA((4,)), DMA((4,)), DMA((4, 3)), DMA((4, 3)),
            DMA((10,)),
        ],
        name="attention_backward",
        compiler_params=pltpu.CompilerParams(
            collective_id=2, has_side_effects=True, vmem_limit_bytes=VMEM_LIMIT
        ),
    )(*args)


def results_kernel(
    block_in, tokens_in, w_grads, w_fc1_in, w_fc2_in, first, last,
    block_out, tokens_grad, mask_grad, gain1_grad, shift1_grad, w_qkv_grad, qv_grad, w_out_grad,
    proj_grad, gain2_grad, shift2_grad, w_fc1_grad, fc1_grad, w_fc2_grad, fc2_grad,
):
    here = Place()
    pairs = (
        (block_in, block_out), (tokens_in, tokens_grad), (w_fc1_in, w_fc1_grad), (w_fc2_in, w_fc2_grad)
    )
    for src, dst in pairs:
        dst[...] = src[...]

    def pick(line, offset, count):
        column = lax.broadcasted_iota(jnp.int32, line.shape, 1) - offset
        spot = lax.broadcasted_iota(jnp.int32, (1, count), 1)
        out = jnp.zeros((1, count), f32)
        for j in range(count):
            one = jnp.sum(jnp.where(column == j, line, 0.0), axis=1, keepdims=True)
            out = jnp.where(spot == j, one, out)
        return out

    index = here.index
    for row, target in ((0, proj_grad), (1, gain2_grad), (2, shift2_grad), (3, fc2_grad)):
        target[...] = pick(first[row : row + 1, 0:D], index * 6, 6)
    fc1_grad[...] = pick(first[pl.ds(index // 16, 1), D : D + UNITS], (index % 16) * 24, 24)
    for k, target in enumerate((gain1_grad, shift1_grad, mask_grad)):
        target[...] = pick(last[pl.ds(2 * k + index // 64, 1), 0:384], (index % 64) * 6, 6)
    for k in (0, 1):
        qv_grad[k : k + 1, :] = last[pl.ds(2 * here.head + k, 1), 384:576]
    for n in range(4):
        for s in range(6):
            lanes = slice(s * 128, s * 128 + 128)
            start = s * 192
            for chunk in range(4):
                low, high = max(start, chunk * 288), min(start + 192, chunk * 288 + 288)
                if low < high:
                    got = w_grads[n, chunk, low - chunk * 288 : high - chunk * 288, :].astype(f32)
                    if n == 0:
                        w_out_grad[low - start : high - start, lanes] = got
                    else:
                        base = (n - 1) * 192 - start
                        w_qkv_grad[base + low : base + high, lanes] = got


def results_call(*args):
    six = shape((1, 6), f32)
    return pl.pallas_call(
        results_kernel,
        out_shape=(
            shape((ROWS, D), f32), shape((ROWS, D), f32), six, six, six, shape((576, D), f32),
            shape((2, 192), f32), shape((192, D), f32), six, six, six,
            shape((24, D), f32), shape((1, 24), f32), shape((24, D), f32), six,
        ),
        in_specs=[VM] * 7,
        out_specs=(VM,) * 15,
        name="results",
        compiler_params=pltpu.CompilerParams(vmem_limit_bytes=VMEM_LIMIT),
    )(*args)


def body(
    tokens, cube_mask, mask_token, norm1_gain, norm1_bias, w_qkv, qv_bias, w_out, proj_bias,
    norm2_gain, norm2_bias, w_fc1, fc1_bias, w_fc2, fc2_bias, cotangent,
):
    small = jnp.concatenate(
        [mask_token, norm1_gain, norm1_bias, proj_bias, norm2_gain, norm2_bias, fc2_bias, fc1_bias]
    ).astype(f32)
    w_qkv_t = w_qkv.T
    params, normed, qkv, lse, mixed, mixed_out, mixed_in, w_out_all, weights = forward_call(
        small, cube_mask, tokens, w_qkv_t, qv_bias, w_out, w_fc1.T, w_fc2,
    )
    block_out, grad_middle, grad_branch, grad_mixed, small_grads, reduced = feed_forward_call(
        cube_mask, params, tokens, cotangent, mixed_in, w_out_all, weights.reshape(6, 64, 96, 128),
    )
    tokens_grad, small_first, small_last, w_grads, w_fc1_grad, w_fc2_grad = backward_call(
        cube_mask, params, grad_mixed, grad_branch, small_grads, reduced.reshape(3, 4, 4, 4, 96, 128),
        grad_middle, tokens, normed.reshape(TOK, D), qkv, lse, mixed, mixed_out, w_qkv_t,
    )
    outs = list(
        results_call(block_out, tokens_grad, w_grads, w_fc1_grad, w_fc2_grad, small_first, small_last)
    )
    for k in (2, 3, 4, 8, 9, 10, 12, 14):
        outs[k] = outs[k].reshape(-1)
    outs[5] = outs[5].T
    outs[11] = outs[11].T
    return tuple(outs)


def solution(mesh):
    every = P(("clip", "head"))
    rows = P(("clip", "head"), None)
    columns = P(None, ("clip", "head"))
    in_specs = (
        rows, P("clip", None), every, every, every, P(None, "head"), P(None, "head"),
        P("head", None), every, every, every, columns, every, rows, every, rows,
    )
    out_specs = (
        rows, rows, every, every, every, P(None, "head"), P(None, "head"), P("head", None),
        every, every, every, columns, every, rows, every,
    )
    return jax.shard_map(body, mesh=mesh, in_specs=in_specs, out_specs=out_specs, check_vma=False)
```

```python
from functools import partial

import jax
import jax.numpy as jnp
import numpy as np
from jax import lax
from jax.experimental import pallas as pl
from jax.experimental.pallas import tpu as pltpu
from jax.sharding import PartitionSpec as P

HEAD_DIM = 64
GRID = 14
TOK = 1568
ROWS = 392
D = 768
HEADS_HERE = 3
QCHUNK = 224
CHUNKS = TOK // QCHUNK
UNITS = 384
BLOCKS = 4
epsilon = 1e-06
MESH = pl.DeviceIdType.MESH
VMEM_LIMIT = 60 * 2**20
f32 = jnp.float32
bf16 = jnp.bfloat16
GATHER = (("y", "x", "z"), ("y", "z", "x"))
REDUCE = (("x", "z", "y"), ("z", "x", "y"))
RING = ("x", "y", "z")


def dot_nn(left, right):
    return jnp.dot(left, right, preferred_element_type=f32)


def dot_nt(left, right):
    return lax.dot_general(left, right, (((1,), (1,)), ((), ())), preferred_element_type=f32)


def dot_tn(left, right):
    return lax.dot_general(left, right, (((0,), (0,)), ((), ())), preferred_element_type=f32)


class Place:
    def __init__(self):
        clip = lax.axis_index("clip")
        head = lax.axis_index("head")
        self.head = head
        self.index = clip * 4 + head
        self.at = {"x": clip // 8, "y": (head // 2) * 2 + clip % 2, "z": (clip // 2) % 4}
        self.core = head % 2

    def device(self, at, core):
        return {
            "clip": at["x"] * 8 + at["z"] * 2 + at["y"] % 2,
            "head": (at["y"] // 2) * 2 + core,
        }

    def along(self, axis, step):
        at = dict(self.at)
        at[axis] = (at[axis] + step) % 4
        return self.device(at, self.core)

    def partner(self):
        return self.device(self.at, 1 - self.core)

    def across(self):
        at = dict(self.at)
        at["y"] = (at["y"] + 2) % 4
        return self.device(at, 1 - self.core)


def slot_of(axis, value):
    return (value % 2) * 2 + value // 2 if axis == "y" else value


def greet(here):
    barrier = pltpu.get_barrier_semaphore()
    peers = [here.partner(), here.across()]
    peers += [here.along(axis, step) for axis in RING for step in (1, 2, 3)]
    for device in peers:
        pl.semaphore_signal(barrier, inc=1, device_id=device, device_id_type=MESH)
    pl.semaphore_wait(barrier, len(peers))


def remote(src, dst, send, recv, device):
    return pltpu.make_async_remote_copy(
        src_ref=src, dst_ref=dst, send_sem=send, recv_sem=recv, device_id=device, device_id_type=MESH
    )


def ring_total(own, first, second, third):
    return (own + second) + (first + third)


class SmallSum:
    def __init__(self, here, held, arrived, send, recv):
        self.phases = []
        count = 0
        for phase, axis in enumerate(("core", "y", "x", "z")):
            devices = [here.partner()] if axis == "core" else [here.along(axis, k) for k in (1, 2, 3)]
            copies = []
            for device in devices:
                copies.append(
                    remote(held.at[phase], arrived.at[count], send.at[count], recv.at[count], device)
                )
                count += 1
            self.phases.append((copies, list(range(count - len(devices), count))))
        self.held, self.arrived = held, arrived

    def start(self, phase):
        for copy in self.phases[phase][0]:
            copy.start()

    def finish(self, phase):
        copies, slots = self.phases[phase]
        for copy in copies:
            copy.wait_recv()
        total = self.held[phase]
        if len(slots) == 1:
            total = total + self.arrived[slots[0]]
        else:
            total = ring_total(total, *[self.arrived[slot] for slot in slots])
        if phase < 3:
            self.held[phase + 1] = total
        return total

    def drain(self):
        for copies, _ in self.phases:
            for copy in copies:
                copy.wait_send()


def region(fixed):
    return tuple(fixed.get(axis, slice(None)) for axis in ("x", "z", "y"))


def row_mask(cubes, which):
    row = lax.broadcasted_iota(jnp.int32, (ROWS, 196), 0)
    spot = jnp.where(row >= GRID * GRID, row - GRID * GRID, row)
    line = (spot * 1171) >> 14
    cube = (line >> 1) * (GRID // 2) + ((spot - line * GRID) >> 1)
    here = lax.broadcasted_iota(jnp.int32, (ROWS, 196), 1) == cube + which * 49
    return jnp.sum(jnp.where(here, cubes[...].astype(f32), 0.0), axis=1, keepdims=True)


def unit_of(values):
    average = jnp.mean(values, axis=-1, keepdims=True)
    centered = values - average
    inverse = lax.rsqrt(jnp.mean(centered * centered, axis=-1, keepdims=True) + epsilon)
    return centered * inverse, inverse


def unit_back(scaled, unit, inverse):
    return inverse * (
        scaled
        - jnp.mean(scaled, axis=-1, keepdims=True)
        - unit * jnp.mean(scaled * unit, axis=-1, keepdims=True)
    )


MASK, GAIN1, SHIFT1, PROJ, GAIN2, SHIFT2, FC2B = range(7)


def forward_kernel(
    small, cubes, tokens, w_qkv, qv_bias, w_out, w_fc1, w_fc2,
    params, normed_out, qkv_out, lse_out, mixed_keep, mixed_out_keep, mixed_in_out, w_out_all_out, gathered,
    normed, qkv, lse, mixed, mixed_out, mixed_in, w_out_all,
    rows, held, arrived, own_half, their_half, chip_block, block, values_t,
    tok_send, tok_recv, sum_send, sum_recv, half_sem, ff_send, ff_recv, fwd_send, fwd_recv,
    out_send, out_recv, mix_send, mix_recv, local_sem,
):
    here = Place()
    core, head = here.core, here.head
    at = here.at
    mate = head + 1 - 2 * core
    far = (head + 2) % 4
    far_mate = far + 1 - 2 * core

    own_half[0] = w_fc1[...].astype(f32)
    own_half[1] = w_fc2[...].astype(f32)
    column = lax.broadcasted_iota(jnp.int32, (1, D), 1) - here.index * 6
    lines = []
    for k in range(7):
        placed = jnp.zeros((1, D), f32)
        for j in range(6):
            placed = jnp.where(column == j, small[k * 6 + j], placed)
        lines.append(placed)
    held[0, :, 0:D] = jnp.concatenate(lines + [jnp.zeros((1, D), f32)], axis=0)
    line = lax.broadcasted_iota(jnp.int32, (8, UNITS), 0)
    unit = lax.broadcasted_iota(jnp.int32, (8, UNITS), 1) - (here.index % 16) * 24
    shifted = jnp.zeros((8, UNITS), f32)
    for j in range(24):
        shifted = jnp.where(unit == j, small[42 + j], shifted)
    held[0, :, D : D + UNITS] = jnp.where(line == here.index // 16, shifted, 0.0)
    sums = SmallSum(here, held, arrived, sum_send, sum_recv)

    greet(here)

    def tok_copy(way, k):
        lanes = pl.ds(k * 384, 384)
        src = rows.at[far, :, lanes] if way == 2 else tokens.at[:, lanes]
        dst = rows.at[far if way == 2 else head, :, lanes]
        device = here.along("y", 2) if way == 1 else here.partner()
        return remote(src, dst, tok_send.at[way, k], tok_recv.at[way, k], device)

    half_copy = remote(
        own_half.at[:, :, pl.ds(pl.multiple_of((1 - core) * UNITS, UNITS), UNITS)],
        their_half, half_sem.at[0], half_sem.at[1], here.partner(),
    )
    half_copy.start()
    sums.start(0)
    sums.finish(0)
    sums.start(1)

    half_copy.wait_recv()
    mine = pl.ds(pl.multiple_of(core * 24, 8), 24)
    theirs = pl.ds(pl.multiple_of((1 - core) * 24, 8), 24)
    for kind in (0, 1):
        chip_block[kind, mine, :] = own_half[kind, :, pl.ds(pl.multiple_of(core * UNITS, UNITS), UNITS)]
        chip_block[kind, theirs, :] = their_half[kind]
    for part in range(3):
        for kind in (0, 1):
            block[part, kind * 48 : kind * 48 + 48, :] = chip_block[
                kind, :, part * 128 : part * 128 + 128
            ].astype(bf16)

    slots = {axis: slot_of(axis, at[axis]) for axis in RING}
    ours = pl.ds(core * 3, 3)
    block_copy = pltpu.make_async_copy(block, gathered.at[(ours,) + region(slots)], local_sem.at[0])

    def ff_copy(kind, phase, step):
        order = GATHER[kind]
        of_kind = pl.ds(kind * 48, 48)
        spot = gathered.at[(ours,) + region({a: slots[a] for a in order[phase:]}) + (of_kind,)]
        return remote(
            block.at[:, of_kind] if phase == 0 else spot, spot,
            ff_send.at[kind, phase, step - 1], ff_recv.at[kind, phase, step - 1],
            here.along(order[phase], step),
        )

    def pass_copy(kind, step):
        last = GATHER[kind][2]
        of_kind = pl.ds(kind * 48, 48)
        plane = region({last: slot_of(last, (at[last] + 4 - step) % 4)})
        spot = gathered.at[(ours,) + plane + (of_kind,)]
        return remote(spot, spot, fwd_send.at[kind, step], fwd_recv.at[kind, step], here.partner())

    def ff_start(phase):
        for step in (1, 2, 3):
            for kind in (0, 1):
                ff_copy(kind, phase, step).start()

    def ff_on(phase):
        for step in (1, 2, 3):
            for kind in (0, 1):
                ff_copy(kind, phase, step).wait_recv()
        ff_start(phase + 1)

    ff_start(0)
    block_copy.start()
    for way in (1, 0):
        for k in (0, 1):
            tok_copy(way, k).start()

    def out_copy(way):
        src = w_out_all.at[far] if way == 2 else w_out
        dst = w_out_all.at[far if way == 2 else head]
        device = here.along("y", 2) if way == 1 else here.partner()
        return remote(src, dst, out_send.at[way], out_recv.at[way], device)

    out_copy(0).start()
    w_out_all[head] = w_out[...]
    rows[head] = tokens[...]
    sums.finish(1)
    sums.start(2)
    block_copy.wait()
    ff_on(0)
    sums.finish(2)
    sums.start(3)
    for k in (0, 1):
        tok_copy(0, k).wait_recv()
    params[...] = sums.finish(3)

    gain = params[GAIN1 : GAIN1 + 1, 0:D]
    shift = params[SHIFT1 : SHIFT1 + 1, 0:D]
    mask_token = params[MASK : MASK + 1, 0:D]
    biases = qv_bias[...].astype(f32)
    q_bias = biases[0:1, :]
    v_bias = biases[1:2, :]

    def project(half):
        parts = []
        for j in range(2):
            which = half * 2 + j
            masked = row_mask(cubes, which)
            start = jnp.where(masked > 0.5, mask_token, rows[which].astype(f32))
            unit1, _ = unit_of(start)
            parts.append(unit1 * gain + shift)
        normed[half] = jnp.concatenate(parts, axis=0).astype(bf16)

        to = pl.ds(pl.multiple_of(half * 784, 16), 784)
        for h in range(HEADS_HERE):
            packed = dot_nt(normed[half], w_qkv[h * 192 : h * 192 + 192, :])
            lanes = slice(h * 64, h * 64 + 64)
            query = packed[:, 0:64] + q_bias[:, lanes]
            value = packed[:, 128:192] + v_bias[:, lanes]
            qkv[h * 3, to, :] = query.astype(bf16) * bf16(0.125)
            qkv[h * 3 + 1, to, :] = packed[:, 64:128].astype(bf16)
            qkv[h * 3 + 2, to, :] = value.astype(bf16)

    chip_half = head // 2
    project(chip_half)
    ff_on(1)
    for kind in (0, 1):
        pass_copy(kind, 0).start()
    for k in (0, 1):
        tok_copy(1, k).wait_recv()
        tok_copy(2, k).start()
    out_copy(1).start()
    for k in (0, 1):
        tok_copy(2, k).wait_recv()
    project(1 - chip_half)
    early = [
        pltpu.make_async_copy(normed, normed_out, local_sem.at[1]),
        pltpu.make_async_copy(qkv, qkv_out, local_sem.at[2]),
    ]
    for copy in early:
        copy.start()

    ones_row = (lax.broadcasted_iota(jnp.int32, (16, TOK), 0) == 0).astype(f32)
    for h in range(HEADS_HERE):
        values_t[h] = jnp.concatenate([qkv[h * 3 + 2].astype(f32).T, ones_row], axis=0).astype(bf16)

    def mix_copy(h, way):
        other, device = (
            (mate, here.partner()), (far, here.along("y", 2)), (far_mate, here.across()),
        )[way]
        return remote(
            mixed_out.at[h, other], mixed_in.at[h, head], mix_send.at[h, way], mix_recv.at[h, way], device
        )

    def mix_start(h):
        for j in range(4):
            mixed_out[h, j] = mixed[h, j * ROWS : j * ROWS + ROWS, :].astype(bf16)
        for way in (1, 2, 0):
            mix_copy(h, way).start()
        mixed_in[h, head] = mixed_out[h, head]

    def ff_pass(step):
        for kind in (0, 1):
            ff_copy(kind, 2, step).wait_recv()
            pass_copy(kind, step).start()

    def out_on():
        out_copy(1).wait_recv()
        out_copy(2).start()

    def attend(h, carry):
        def score(k):
            scores = dot_nt(qkv[h * 3 + 1], qkv[h * 3, k * QCHUNK : k * QCHUNK + QCHUNK, :])
            return scores, jnp.max(scores, axis=0, keepdims=True)

        ready = score(0)
        for k in range(CHUNKS):
            scores, top = ready
            if k + 1 < CHUNKS:
                ready = score(k + 1)
            weights = jnp.exp(scores - top).astype(bf16)
            outcome = dot_nn(values_t[h], weights)
            total = outcome[64:65, :]
            mixed[h, k * QCHUNK : k * QCHUNK + QCHUNK, :] = (outcome[0:64, :] / total).T
            lse[h * CHUNKS + k] = jnp.broadcast_to(top + jnp.log(total), (8, QCHUNK))
        for n in range(HEADS_HERE - 1):
            pl.when(h == n)(partial(mix_start, n))
        pl.when(h == 1)(out_on)
        return carry

    lax.fori_loop(0, HEADS_HERE, attend, 0)

    mix_start(HEADS_HERE - 1)
    for step in (1, 2, 3):
        ff_pass(step)
    out_copy(0).wait_recv()
    out_copy(2).wait_recv()
    late = [
        pltpu.make_async_copy(lse, lse_out, local_sem.at[3]),
        pltpu.make_async_copy(mixed, mixed_keep, local_sem.at[4]),
        pltpu.make_async_copy(mixed_out, mixed_out_keep, local_sem.at[5]),
        pltpu.make_async_copy(w_out_all, w_out_all_out, local_sem.at[6]),
    ]
    for copy in late:
        copy.start()
    for kind in (0, 1):
        for step in range(4):
            pass_copy(kind, step).wait_recv()
    for h in range(HEADS_HERE):
        for way in range(3):
            mix_copy(h, way).wait_recv()
    last_copy = pltpu.make_async_copy(mixed_in, mixed_in_out, local_sem.at[7])
    last_copy.start()
    sums.drain()
    half_copy.wait_send()
    for way in range(3):
        out_copy(way).wait_send()
        for k in (0, 1):
            tok_copy(way, k).wait_send()
        for h in range(HEADS_HERE):
            mix_copy(h, way).wait_send()
    for kind in (0, 1):
        for phase in range(3):
            for step in (1, 2, 3):
                ff_copy(kind, phase, step).wait_send()
        for step in range(4):
            pass_copy(kind, step).wait_send()
    for copy in early + late + [last_copy]:
        copy.wait()


VM = pl.BlockSpec(memory_space=pltpu.VMEM)
SM = pl.BlockSpec(memory_space=pltpu.SMEM)
ANY = pl.BlockSpec(memory_space=pl.ANY)
DMA = pltpu.SemaphoreType.DMA


def shape(dims, kind=bf16):
    return jax.ShapeDtypeStruct(dims, kind)


def forward_call(*args):
    kept = (
        ((2, 784, D), bf16),
        ((9, TOK, 64), bf16),
        ((HEADS_HERE * CHUNKS, 8, QCHUNK), f32),
        ((HEADS_HERE, TOK, 64), f32),
        ((HEADS_HERE, 4, ROWS, 64), bf16),
        ((HEADS_HERE, 4, ROWS, 64), bf16),
        ((4, 192, D), bf16),
    )
    return pl.pallas_call(
        forward_kernel,
        out_shape=(shape((8, D + UNITS), f32),)
        + tuple(shape(*k) for k in kept)
        + (shape((6, 4, 4, 4, 96, 128)),),
        in_specs=[SM] + [VM] * 7,
        out_specs=(VM,) + (ANY,) * 8,
        scratch_shapes=[pltpu.VMEM(*k) for k in kept]
        + [
            pltpu.VMEM((4, ROWS, D), bf16),
            pltpu.VMEM((4, 8, D + UNITS), f32),
            pltpu.VMEM((10, 8, D + UNITS), f32),
            pltpu.VMEM((2, 24, D), f32),
            pltpu.VMEM((2, 24, UNITS), f32),
            pltpu.VMEM((2, 48, UNITS), f32),
            pltpu.VMEM((3, 96, 128), bf16),
            pltpu.VMEM((HEADS_HERE, 80, TOK), bf16),
            DMA((3, 2)), DMA((3, 2)), DMA((10,)), DMA((10,)), DMA((2,)),
            DMA((2, 3, 3)), DMA((2, 3, 3)), DMA((2, 4)), DMA((2, 4)),
            DMA((3,)), DMA((3,)), DMA((HEADS_HERE, 3)), DMA((HEADS_HERE, 3)), DMA((8,)),
        ],
        name="attention_forward",
        compiler_params=pltpu.CompilerParams(
            collective_id=0, has_side_effects=True, vmem_limit_bytes=VMEM_LIMIT
        ),
    )(*args)


SQRT_HALF = 0.7071067811865476
INV_SQRT_2PI = 0.3989422804014327


def feed_forward_kernel(
    cubes, params, tokens, cotangent, mixed_in, w_out_all, weights,
    block_out, grad_middle, grad_branch, grad_mixed, small_grads, reduced_out,
    held, grads, arrived, reduced, normed2, outer, grad_normed2,
    load_sem, pair_send, pair_recv, keep_sem,
):
    here = Place()
    core, head = here.core, here.head

    def load(b):
        chips = pl.ds(b * 16, 16)
        return pltpu.make_async_copy(weights.at[:, chips], held.at[:, chips], load_sem.at[b])

    for b in range(BLOCKS):
        load(b).start()
    barrier = pltpu.get_barrier_semaphore()
    pl.semaphore_signal(barrier, inc=1, device_id=here.partner(), device_id_type=MESH)

    masked = row_mask(cubes, head)
    start = jnp.where(masked > 0.5, params[MASK : MASK + 1, 0:D], tokens[...].astype(f32))
    branch = jnp.zeros((ROWS, D), f32)
    for j in range(4):
        some = jnp.concatenate([mixed_in[h, j] for h in range(HEADS_HERE)], axis=1)
        branch = branch + dot_nn(some, w_out_all[j])
    middle = start + branch + params[PROJ : PROJ + 1, 0:D]
    gain2 = params[GAIN2 : GAIN2 + 1, 0:D]
    unit2, _ = unit_of(middle)
    normed2[...] = (unit2 * gain2 + params[SHIFT2 : SHIFT2 + 1, 0:D]).astype(bf16)
    block_out[...] = middle
    outer[...] = jnp.zeros((ROWS, D), f32)
    grad_normed2[...] = jnp.zeros((ROWS, D), f32)
    pl.semaphore_wait(barrier, 1)
    mates = pl.ds((1 - core) * 3, 3)

    def pair_copy(b):
        chips = pl.ds(b * 16, 16)
        return remote(
            grads.at[mates, chips], arrived.at[:, chips], pair_send.at[b], pair_recv.at[b], here.partner()
        )

    def keep_copy(b):
        chips = pl.ds(b * 16, 16)
        return pltpu.make_async_copy(reduced.at[:, chips], reduced_out.at[:, chips], keep_sem.at[b])

    def add_pair(b):
        chips = pl.ds(b * 16, 16)
        pair_copy(b).wait_recv()
        for part in range(3):
            reduced[part, chips] = (
                grads[core * 3 + part, chips].astype(f32) + arrived[part, chips].astype(f32)
            ).astype(bf16)
        keep_copy(b).start()

    def some_units(b, carry):
        load(b).wait()
        chips = pl.ds(b * 16, 16)

        def weight(kind):
            return jnp.concatenate(
                [
                    held[s, chips, kind * 48 : kind * 48 + 48, :].reshape(2 * UNITS, 128)
                    for s in range(6)
                ],
                axis=1,
            )

        def keep(kind, grad):
            grad = grad.astype(bf16)
            for s in range(6):
                grads[s, chips, kind * 48 : kind * 48 + 48, :] = grad[
                    :, s * 128 : s * 128 + 128
                ].reshape(16, 48, 128)

        bias = jnp.concatenate(
            [params[pl.ds(2 * b + k, 1), D : D + UNITS] for k in (0, 1)], axis=1
        )
        inner = dot_nt(normed2[...], weight(0)) + bias
        below = 0.5 + 0.5 * lax.erf(inner * SQRT_HALF)
        active = (inner * below).astype(bf16)
        slope = below + inner * (INV_SQRT_2PI * jnp.exp(-0.5 * inner * inner))
        grad_active = dot_nt(cotangent[...], weight(1))
        grad_inner = (grad_active * slope).astype(bf16)
        bias_grad = jnp.sum(grad_inner.astype(f32), axis=0, keepdims=True)
        for k in (0, 1):
            small_grads[pl.ds(2 * b + k, 1), D : D + UNITS] = bias_grad[:, k * UNITS : k * UNITS + UNITS]
        outer[...] += dot_nn(active, weight(1))
        grad_normed2[...] += dot_nn(grad_inner, weight(0))
        keep(1, dot_tn(active, cotangent[...]))
        keep(0, dot_tn(grad_inner, normed2[...]))
        pair_copy(b).start()

        @pl.when(b > 0)
        def _():
            add_pair(b - 1)

        return carry

    lax.fori_loop(0, BLOCKS, some_units, 0)

    middle = block_out[...]
    block_out[...] = middle + outer[...] + params[FC2B : FC2B + 1, 0:D]
    unit2, inverse2 = unit_of(middle)
    grad_out = cotangent[...].astype(f32)
    back = grad_normed2[...]
    grad_mid = grad_out + unit_back(back * gain2, unit2, inverse2)
    grad_middle[...] = grad_mid
    low = grad_mid.astype(bf16)
    grad_branch[...] = low
    for j in range(4):
        some = dot_nt(low, w_out_all[j]).astype(bf16)
        for h in range(HEADS_HERE):
            grad_mixed[h, j] = some[:, h * 64 : h * 64 + 64]
    sums = [
        jnp.sum(v, axis=0, keepdims=True)
        for v in (grad_mid, back * unit2, back, grad_out)
    ]
    small_grads[:, 0:D] = jnp.concatenate(sums + [jnp.zeros((4, D), f32)], axis=0)
    add_pair(BLOCKS - 1)
    for b in range(BLOCKS):
        pair_copy(b).wait_send()
        keep_copy(b).wait()


def feed_forward_call(*args):
    return pl.pallas_call(
        feed_forward_kernel,
        out_shape=(
            shape((ROWS, D), f32),
            shape((ROWS, D), f32),
            shape((ROWS, D)),
            shape((HEADS_HERE, 4, ROWS, 64)),
            shape((8, D + UNITS), f32),
            shape((3, 64, 96, 128)),
        ),
        in_specs=[VM] * 6 + [ANY],
        out_specs=(VM,) * 5 + (ANY,),
        scratch_shapes=[
            pltpu.VMEM((6, 64, 96, 128), bf16),
            pltpu.VMEM((6, 64, 96, 128), bf16),
            pltpu.VMEM((3, 64, 96, 128), bf16),
            pltpu.VMEM((3, 64, 96, 128), bf16),
            pltpu.VMEM((ROWS, D), bf16),
            pltpu.VMEM((ROWS, D), f32),
            pltpu.VMEM((ROWS, D), f32),
            DMA((BLOCKS,)), DMA((BLOCKS,)), DMA((BLOCKS,)), DMA((BLOCKS,)),
        ],
        name="feed_forward",
        compiler_params=pltpu.CompilerParams(
            collective_id=1, has_side_effects=True, vmem_limit_bytes=VMEM_LIMIT
        ),
    )(*args)


def without(axes, axis):
    return tuple(a for a in axes if a != axis)


def backward_kernel(
    cubes, params, grad_mixed, grad_branch, small_grads, reduced,
    grad_middle_in, tokens_in, normed_in, qkv_in, lse_in, mixed_in, mixed_out_in, w_qkv_in,
    tokens_grad, small_first, small_last, w_grads, w_fc1_grad, w_fc2_grad,
    grad_middle, tokens, normed, qkv, lse, mixed, mixed_out, w_qkv, own_reduced,
    mixed_back, mixed_wide, outer_back, queries, keys_t, grad_q, grad_kv, packed_back,
    branch_in, input_back, pair_out, pair_in, far_out, far_in,
    held, arrived, held_last, arrived_last,
    ff_in0, ff_sum1, ff_in1, ff_sum2, ff_in2, ff_last, ff_mate,
    w_src, w_in, w_z, w_z_in, w_y, w_y_in, w_all, column_sums,
    mix_send, mix_recv, br_send, br_recv, in_send, in_recv, sum_send, sum_recv, last_send, last_recv,
    ff_send, ff_recv, mate_sem, wx_send, wx_recv, wz_send, wz_recv, wy_send, wy_recv, wg_send, wg_recv,
    load_sem,
):
    here = Place()
    core, head, at = here.core, here.head, here.at
    mate = head + 1 - 2 * core
    far = (head + 2) % 4
    far_mate = far + 1 - 2 * core
    slots = {axis: slot_of(axis, at[axis]) for axis in RING}

    def own_share(kind):
        axis = REDUCE[kind][0]
        return reduced.at[(slice(None),) + region({axis: slots[axis]}) + (pl.ds(kind * 48, 48),)]

    pairs = (
        (qkv_in, qkv), (lse_in, lse), (mixed_in, mixed), (tokens_in, tokens), (w_qkv_in, w_qkv),
        (normed_in, normed), (mixed_out_in, mixed_out), (grad_middle_in, grad_middle),
        (own_share(0), own_reduced.at[0]), (own_share(1), own_reduced.at[1]),
    )
    loads = [pltpu.make_async_copy(src, dst, load_sem.at[k]) for k, (src, dst) in enumerate(pairs)]
    for copy in loads:
        copy.start()
    greet(here)

    def mix_copy(h, way):
        other, device = (
            (mate, here.partner()), (far, here.along("y", 2)), (far_mate, here.across()),
        )[way]
        return remote(
            grad_mixed.at[h, other], mixed_back.at[h, head], mix_send.at[h, way], mix_recv.at[h, way], device
        )

    for h in range(HEADS_HERE):
        for way in (1, 2, 0):
            mix_copy(h, way).start()

    def peer_slot(axis, step):
        return slot_of(axis, (at[axis] + step) % 4)

    def ff_left(kind, phase):
        left = ("x", "z", "y")
        for done in REDUCE[kind][:phase]:
            left = without(left, done)
        return left

    def ff_copy(kind, phase, step):
        axis = REDUCE[kind][phase]
        where = tuple(
            peer_slot(axis, step) if a == axis else slice(None) for a in ff_left(kind, phase)
        )
        where = (slice(None),) + where
        if phase == 0:
            src = reduced.at[where + (pl.ds(kind * 48, 48),)]
        else:
            src = (ff_sum1, ff_sum2)[phase - 1].at[(kind,) + where]
        dst = (ff_in0, ff_in1, ff_in2)[phase]
        return remote(
            src, dst.at[kind, step - 1],
            ff_send.at[kind, phase, step - 1], ff_recv.at[kind, phase, step - 1],
            here.along(axis, step),
        )

    def ff_start(kind, phase):
        for step in (1, 2, 3):
            ff_copy(kind, phase, step).start()

    def ff_add(kind, phase):
        axis = REDUCE[kind][phase]
        where = tuple(slots[axis] if a == axis else slice(None) for a in ff_left(kind, phase))
        arrived_in = (ff_in0, ff_in1, ff_in2)[phase]
        for step in (1, 2, 3):
            ff_copy(kind, phase, step).wait_recv()
        if phase == 0:
            loads[8 + kind].wait()

        def some(part):
            if phase == 0:
                own = own_reduced[kind, part]
            else:
                own = (ff_sum1, ff_sum2)[phase - 1][(kind, part) + where]
            return ring_total(
                own.astype(f32), *[arrived_in[kind, k, part].astype(f32) for k in range(3)]
            )

        if phase == 0:
            @pl.loop(0, 3)
            def _(part):
                ff_sum1[kind, part] = some(part).astype(bf16)
        else:
            for part in range(3):
                total = some(part)
                if phase == 1:
                    ff_sum2[kind, part] = total.astype(bf16)
                else:
                    ff_last[kind, :, part * 128 : part * 128 + 128] = total

    for kind in (0, 1):
        ff_start(kind, 0)

    held[0] = small_grads[...]
    sums = SmallSum(here, held, arrived, sum_send, sum_recv)
    sums.start(0)

    beside = dict(at)
    beside["y"] = at["y"] + 1 - 2 * (at["y"] % 2)
    beside = here.device(beside, core)

    def first_axis(n):
        return "xz"[n % 2]

    def wx_copy(n, step):
        axis = first_axis(n)
        return remote(
            w_src.at[n, (at[axis] + step) % 4], w_in.at[n, step - 1],
            wx_send.at[n, step - 1], wx_recv.at[n, step - 1], here.along(axis, step),
        )

    def wz_copy(n, step):
        return remote(
            w_z.at[n], w_z_in.at[n, step - 1], wz_send.at[n, step - 1], wz_recv.at[n, step - 1],
            here.along(first_axis(n + 1), step),
        )

    def wy_copy(n):
        return remote(w_y.at[n], w_y_in.at[n], wy_send.at[n], wy_recv.at[n], beside)

    def wg_copy(n, step):
        axis = first_axis(n)
        spot = w_all.at[n, at[axis]]
        return remote(
            spot, spot, wg_send.at[n, step - 1], wg_recv.at[n, step - 1], here.along(axis, step)
        )

    def w_begin(n, grad):
        grad = grad.astype(bf16)
        for s in range(6):
            lanes = slice(s * 128, s * 128 + 128)
            first = s * 192
            for chunk in range(4):
                low, high = max(first, chunk * 288), min(first + 192, chunk * 288 + 288)
                if low < high:
                    w_src[n, chunk, low - chunk * 288 : high - chunk * 288, :] = grad[
                        low - first : high - first, lanes
                    ]
        for step in (1, 2, 3):
            wx_copy(n, step).start()

    def w_second(n):
        for step in (1, 2, 3):
            wx_copy(n, step).wait_recv()
        w_z[n] = ring_total(
            w_src[n, at[first_axis(n)]].astype(f32), *[w_in[n, k].astype(f32) for k in range(3)]
        ).astype(bf16)
        for step in (1, 2, 3):
            wz_copy(n, step).start()

    def w_third(n):
        for step in (1, 2, 3):
            wz_copy(n, step).wait_recv()
        w_y[n] = ring_total(
            w_z[n].astype(f32), *[w_z_in[n, k].astype(f32) for k in range(3)]
        ).astype(bf16)
        wy_copy(n).start()

    def w_fourth(n):
        wy_copy(n).wait_recv()
        w_all[n, at[first_axis(n)]] = (w_y[n].astype(f32) + w_y_in[n].astype(f32)).astype(bf16)
        for step in (1, 2, 3):
            wg_copy(n, step).start()

    def w_end(n):
        for step in (1, 2, 3):
            wg_copy(n, step).wait_recv()
        w_grads[n] = w_all[n]

    br_near = remote(grad_branch, branch_in.at[head], br_send.at[0], br_recv.at[0], here.partner())
    br_far = remote(grad_branch, branch_in.at[head], br_send.at[1], br_recv.at[1], here.along("y", 2))
    br_pass = remote(branch_in.at[far], branch_in.at[far], br_send.at[2], br_recv.at[2], here.partner())
    branch_in[head] = grad_branch[...]
    for h in range(HEADS_HERE):
        mixed_back[h, head] = grad_mixed[h, head]

    zeros = jnp.zeros((TOK, 64), bf16)
    loads[0].wait()
    for h in range(HEADS_HERE):
        query = qkv[h * 3]
        queries[h] = jnp.concatenate([zeros, query], axis=1)
        keys_t[h] = qkv[h * 3 + 1].astype(f32).T.astype(bf16)

    def outer_in(h):
        for way in range(3):
            mix_copy(h, way).wait_recv()
        for j in range(4):
            mixed_wide[j * ROWS : j * ROWS + ROWS, :] = mixed_back[h, j].astype(f32)
        outer_back[h] = jnp.concatenate([mixed_wide[...].astype(bf16), zeros], axis=1)

    outer_in(0)
    br_far.start()
    br_near.start()
    for k in (1, 2, 3, 4, 5, 6, 7):
        loads[k].wait()

    def branch_on():
        br_far.wait_recv()
        br_pass.start()

    def branch_end():
        br_near.wait_recv()
        br_pass.wait_recv()
        grad = jnp.zeros((192, D), f32)
        for j in range(4):
            some = jnp.concatenate([mixed_out[h, j] for h in range(HEADS_HERE)], axis=1)
            grad = grad + dot_tn(some, branch_in[j])
        w_begin(0, grad)

    def sum_on(phase):
        total = sums.finish(phase)
        if phase < 3:
            sums.start(phase + 1)
        else:
            small_first[...] = total

    def ff_on(phase):
        for kind in (0, 1):
            ff_add(kind, phase)
            if phase < 2:
                ff_start(kind, phase + 1)

    chip = head // 2
    lane = lax.broadcasted_iota(jnp.int32, (TOK, 128), 1)

    def attend(h, carry):
        def score(k):
            chunk = slice(k * QCHUNK, k * QCHUNK + QCHUNK)
            scores = dot_nt(qkv[h * 3 + 1], qkv[h * 3, chunk, :])
            return scores, dot_nt(qkv[h * 3 + 2], outer_back[h, chunk, 0:64])

        ready = score(0)
        for k in range(CHUNKS):
            chunk = slice(k * QCHUNK, k * QCHUNK + QCHUNK)
            scores, grad_weights = ready
            if k + 1 < CHUNKS:
                ready = score(k + 1)
            given = outer_back[h, chunk, :]
            weights = jnp.exp(scores - lse[h * CHUNKS + k, 0:1, :])
            delta = jnp.sum(
                (given[:, 0:64].astype(f32) * mixed[h, chunk, :]).T, axis=0, keepdims=True
            )
            grad_scores = (weights * (grad_weights - delta)).astype(bf16)
            share = dot_nn(weights.astype(bf16), given) + dot_nn(grad_scores, queries[h, chunk, :])
            if k == 0:
                grad_kv[...] = share
            else:
                grad_kv[...] += share
            grad_q[chunk, 0:64] = dot_nn(keys_t[h], grad_scores).T * 0.125

        both = grad_kv[...]
        packed_back[:, 0:128] = jnp.where(lane < 64, grad_q[...], both).astype(bf16)
        packed_back[:, 128:192] = both[:, 0:64].astype(bf16)
        for half in (1 - chip, chip):
            share = dot_nn(
                packed_back[pl.ds(pl.multiple_of(half * 784, 16), 784), :],
                w_qkv[pl.ds(pl.multiple_of(h * 192, 16), 192), :],
            )
            for j in (0, 1):
                some = share[j * ROWS : j * ROWS + ROWS]

                @pl.when(h == 0)
                def _():
                    input_back[half, j] = some

                @pl.when(h > 0)
                def _():
                    input_back[half, j] += some

            k = 0 if half is not chip else 1
            pl.when(h == HEADS_HERE - 1)(partial(pair_start, k, half))
        column_sums[pl.ds(h, 1), :] = jnp.sum(packed_back[...].astype(f32), axis=0, keepdims=True)
        w_grad = dot_tn(packed_back[...], normed[...])
        for n in range(HEADS_HERE):
            pl.when(h == n)(partial(w_begin, n + 1, w_grad))

        @pl.when(h == 0)
        def _():
            outer_in(1)
            sum_on(0)

        @pl.when(h == 1)
        def _():
            outer_in(2)
            sum_on(1)
            branch_on()

        return carry

    pair_copies = [
        remote(pair_out.at[k], pair_in.at[k], in_send.at[k], in_recv.at[k], here.partner()) for k in (0, 1)
    ]
    far_copy = remote(far_out, far_in, in_send.at[2], in_recv.at[2], here.along("y", 2))

    def pair_start(k, half):
        pair_out[k] = input_back[half, 1 - core].astype(bf16)
        pair_copies[k].start()

    lax.fori_loop(0, HEADS_HERE, attend, 0)

    pair_copies[0].wait_recv()
    far_out[...] = (input_back[1 - chip, core] + pair_in[0].astype(f32)).astype(bf16)
    far_copy.start()
    ff_on(0)
    branch_end()
    w_second(1)
    w_second(2)
    sum_on(2)
    ff_on(1)
    w_second(3)
    w_third(1)
    w_third(2)
    sum_on(3)
    w_second(0)

    masked = row_mask(cubes, head)
    start = jnp.where(masked > 0.5, params[MASK : MASK + 1, 0:D], tokens[...].astype(f32))
    unit1, inverse1 = unit_of(start)
    pair_copies[1].wait_recv()
    near = input_back[chip, core] + pair_in[1].astype(f32)
    far_copy.wait_recv()
    back = near + far_in[...].astype(f32)
    grad_start = grad_middle[...] + unit_back(
        back * params[GAIN1 : GAIN1 + 1, 0:D], unit1, inverse1
    )
    tokens_grad[...] = jnp.where(masked > 0.5, 0.0, grad_start)
    totals = [
        jnp.sum(v, axis=0, keepdims=True)
        for v in (back * unit1, back, jnp.where(masked > 0.5, grad_start, 0.0))
    ]
    held_last[0, :, 0:384] = jnp.concatenate(
        [v[:, k * 384 : k * 384 + 384] for v in totals for k in (0, 1)] + [jnp.zeros((2, 384), f32)],
        axis=0,
    )
    line = lax.broadcasted_iota(jnp.int32, (8, 192), 0)
    of_query = jnp.concatenate([column_sums[h : h + 1, 0:64] for h in range(HEADS_HERE)], axis=1)
    of_value = jnp.concatenate([column_sums[h : h + 1, 128:192] for h in range(HEADS_HERE)], axis=1)
    held_last[0, :, 384:576] = jnp.where(
        line == 2 * head, of_query, jnp.where(line == 2 * head + 1, of_value, 0.0)
    )
    held_last[0, :, 576:640] = jnp.zeros((8, 64), f32)
    last = SmallSum(here, held_last, arrived_last, last_send, last_recv)
    last.start(0)
    w_third(3)
    last.finish(0)
    last.start(1)
    w_fourth(1)
    w_fourth(2)
    ff_on(2)
    mate_copy = remote(
        ff_last.at[:, pl.ds(pl.multiple_of((1 - core) * 24, 8), 24), :], ff_mate,
        mate_sem.at[0], mate_sem.at[1], here.partner(),
    )
    mate_copy.start()
    last.finish(1)
    last.start(2)
    w_third(0)
    w_fourth(3)
    last.finish(2)
    last.start(3)
    w_fourth(0)
    mate_copy.wait_recv()
    for kind, target in ((0, w_fc1_grad), (1, w_fc2_grad)):
        target[:, pl.ds(pl.multiple_of(core * UNITS, UNITS), UNITS)] = ff_last[
            kind, pl.ds(pl.multiple_of(core * 24, 8), 24), :
        ]
        target[:, pl.ds(pl.multiple_of((1 - core) * UNITS, UNITS), UNITS)] = ff_mate[kind]
    w_end(1)
    w_end(2)
    small_last[...] = last.finish(3)
    w_end(3)
    w_end(0)

    sums.drain()
    last.drain()
    for copy in [br_near, br_far, br_pass, far_copy, mate_copy] + pair_copies:
        copy.wait_send()
    for h in range(HEADS_HERE):
        for way in range(3):
            mix_copy(h, way).wait_send()
    for kind in (0, 1):
        for phase in range(3):
            for step in (1, 2, 3):
                ff_copy(kind, phase, step).wait_send()
    for n in range(4):
        for step in (1, 2, 3):
            wx_copy(n, step).wait_send()
            wz_copy(n, step).wait_send()
            wg_copy(n, step).wait_send()
        wy_copy(n).wait_send()


def backward_call(*args):
    loaded = (
        ((ROWS, D), f32),
        ((ROWS, D), bf16),
        ((TOK, D), bf16),
        ((9, TOK, 64), bf16),
        ((HEADS_HERE * CHUNKS, 8, QCHUNK), f32),
        ((HEADS_HERE, TOK, 64), f32),
        ((HEADS_HERE, 4, ROWS, 64), bf16),
        ((576, D), bf16),
    )
    return pl.pallas_call(
        backward_kernel,
        out_shape=(
            shape((ROWS, D), f32),
            shape((8, D + UNITS), f32),
            shape((8, 640), f32),
            shape((4, 4, 288, 128)),
            shape((24, D), f32),
            shape((24, D), f32),
        ),
        in_specs=[VM] * 5 + [ANY] * 9,
        out_specs=(VM,) * 6,
        scratch_shapes=[pltpu.VMEM(*k) for k in loaded]
        + [
            pltpu.VMEM((2, 3, 4, 4, 48, 128), bf16),
            pltpu.VMEM((HEADS_HERE, 4, ROWS, 64), bf16),
            pltpu.VMEM((TOK, 64), f32),
            pltpu.VMEM((HEADS_HERE, TOK, 128), bf16),
            pltpu.VMEM((HEADS_HERE, TOK, 128), bf16),
            pltpu.VMEM((HEADS_HERE, 64, TOK), bf16),
            pltpu.VMEM((TOK, 128), f32),
            pltpu.VMEM((TOK, 128), f32),
            pltpu.VMEM((TOK, 192), bf16),
            pltpu.VMEM((4, ROWS, D), bf16),
            pltpu.VMEM((2, 2, ROWS, D), f32),
            pltpu.VMEM((2, ROWS, D), bf16),
            pltpu.VMEM((2, ROWS, D), bf16),
            pltpu.VMEM((ROWS, D), bf16),
            pltpu.VMEM((ROWS, D), bf16),
            pltpu.VMEM((4, 8, D + UNITS), f32),
            pltpu.VMEM((10, 8, D + UNITS), f32),
            pltpu.VMEM((4, 8, 640), f32),
            pltpu.VMEM((10, 8, 640), f32),
            pltpu.VMEM((2, 3, 3, 4, 4, 48, 128), bf16),
            pltpu.VMEM((2, 3, 4, 4, 48, 128), bf16),
            pltpu.VMEM((2, 3, 3, 4, 48, 128), bf16),
            pltpu.VMEM((2, 3, 4, 48, 128), bf16),
            pltpu.VMEM((2, 3, 3, 48, 128), bf16),
            pltpu.VMEM((2, 48, UNITS), f32),
            pltpu.VMEM((2, 24, UNITS), f32),
            pltpu.VMEM((4, 4, 288, 128), bf16),
            pltpu.VMEM((4, 3, 288, 128), bf16),
            pltpu.VMEM((4, 288, 128), bf16),
            pltpu.VMEM((4, 3, 288, 128), bf16),
            pltpu.VMEM((4, 288, 128), bf16),
            pltpu.VMEM((4, 288, 128), bf16),
            pltpu.VMEM((4, 4, 288, 128), bf16),
            pltpu.VMEM((8, 192), f32),
            DMA((HEADS_HERE, 3)), DMA((HEADS_HERE, 3)), DMA((3,)), DMA((3,)), DMA((3,)), DMA((3,)),
            DMA((10,)), DMA((10,)), DMA((10,)), DMA((10,)),
            DMA((2, 3, 3)), DMA((2, 3, 3)), DMA((2,)),
            DMA((4, 3)), DMA((4, 3)), DMA((4, 3)), DMA((4, 3)), DMA((4,)), DMA((4,)), DMA((4, 3)), DMA((4, 3)),
            DMA((10,)),
        ],
        name="attention_backward",
        compiler_params=pltpu.CompilerParams(
            collective_id=2, has_side_effects=True, vmem_limit_bytes=VMEM_LIMIT
        ),
    )(*args)


def results_kernel(
    block_in, tokens_in, w_grads, w_fc1_in, w_fc2_in, first, last,
    block_out, tokens_grad, mask_grad, gain1_grad, shift1_grad, w_qkv_grad, qv_grad, w_out_grad,
    proj_grad, gain2_grad, shift2_grad, w_fc1_grad, fc1_grad, w_fc2_grad, fc2_grad,
):
    here = Place()
    pairs = (
        (block_in, block_out), (tokens_in, tokens_grad), (w_fc1_in, w_fc1_grad), (w_fc2_in, w_fc2_grad)
    )
    for src, dst in pairs:
        dst[...] = src[...]

    def pick(line, offset, count):
        column = lax.broadcasted_iota(jnp.int32, line.shape, 1) - offset
        spot = lax.broadcasted_iota(jnp.int32, (1, count), 1)
        out = jnp.zeros((1, count), f32)
        for j in range(count):
            one = jnp.sum(jnp.where(column == j, line, 0.0), axis=1, keepdims=True)
            out = jnp.where(spot == j, one, out)
        return out

    index = here.index
    for row, target in ((0, proj_grad), (1, gain2_grad), (2, shift2_grad), (3, fc2_grad)):
        target[...] = pick(first[row : row + 1, 0:D], index * 6, 6)
    fc1_grad[...] = pick(first[pl.ds(index // 16, 1), D : D + UNITS], (index % 16) * 24, 24)
    for k, target in enumerate((gain1_grad, shift1_grad, mask_grad)):
        target[...] = pick(last[pl.ds(2 * k + index // 64, 1), 0:384], (index % 64) * 6, 6)
    for k in (0, 1):
        qv_grad[k : k + 1, :] = last[pl.ds(2 * here.head + k, 1), 384:576]
    for n in range(4):
        for s in range(6):
            lanes = slice(s * 128, s * 128 + 128)
            start = s * 192
            for chunk in range(4):
                low, high = max(start, chunk * 288), min(start + 192, chunk * 288 + 288)
                if low < high:
                    got = w_grads[n, chunk, low - chunk * 288 : high - chunk * 288, :].astype(f32)
                    if n == 0:
                        w_out_grad[low - start : high - start, lanes] = got
                    else:
                        base = (n - 1) * 192 - start
                        w_qkv_grad[base + low : base + high, lanes] = got


def results_call(*args):
    six = shape((1, 6), f32)
    return pl.pallas_call(
        results_kernel,
        out_shape=(
            shape((ROWS, D), f32), shape((ROWS, D), f32), six, six, six, shape((576, D), f32),
            shape((2, 192), f32), shape((192, D), f32), six, six, six,
            shape((24, D), f32), shape((1, 24), f32), shape((24, D), f32), six,
        ),
        in_specs=[VM] * 7,
        out_specs=(VM,) * 15,
        name="results",
        compiler_params=pltpu.CompilerParams(vmem_limit_bytes=VMEM_LIMIT),
    )(*args)


def body(
    tokens, cube_mask, mask_token, norm1_gain, norm1_bias, w_qkv, qv_bias, w_out, proj_bias,
    norm2_gain, norm2_bias, w_fc1, fc1_bias, w_fc2, fc2_bias, cotangent,
):
    small = jnp.concatenate(
        [mask_token, norm1_gain, norm1_bias, proj_bias, norm2_gain, norm2_bias, fc2_bias, fc1_bias]
    ).astype(f32)
    w_qkv_t = w_qkv.T
    params, normed, qkv, lse, mixed, mixed_out, mixed_in, w_out_all, weights = forward_call(
        small, cube_mask, tokens, w_qkv_t, qv_bias, w_out, w_fc1.T, w_fc2,
    )
    block_out, grad_middle, grad_branch, grad_mixed, small_grads, reduced = feed_forward_call(
        cube_mask, params, tokens, cotangent, mixed_in, w_out_all, weights.reshape(6, 64, 96, 128),
    )
    tokens_grad, small_first, small_last, w_grads, w_fc1_grad, w_fc2_grad = backward_call(
        cube_mask, params, grad_mixed, grad_branch, small_grads, reduced.reshape(3, 4, 4, 4, 96, 128),
        grad_middle, tokens, normed.reshape(TOK, D), qkv, lse, mixed, mixed_out, w_qkv_t,
    )
    outs = list(
        results_call(block_out, tokens_grad, w_grads, w_fc1_grad, w_fc2_grad, small_first, small_last)
    )
    for k in (2, 3, 4, 8, 9, 10, 12, 14):
        outs[k] = outs[k].reshape(-1)
    outs[5] = outs[5].T
    outs[11] = outs[11].T
    return tuple(outs)


def solution(mesh):
    every = P(("clip", "head"))
    rows = P(("clip", "head"), None)
    columns = P(None, ("clip", "head"))
    in_specs = (
        rows, P("clip", None), every, every, every, P(None, "head"), P(None, "head"),
        P("head", None), every, every, every, columns, every, rows, every, rows,
    )
    out_specs = (
        rows, rows, every, every, every, P(None, "head"), P(None, "head"), P("head", None),
        every, every, every, columns, every, rows, every,
    )
    return jax.shard_map(body, mesh=mesh, in_specs=in_specs, out_specs=out_specs, check_vma=False)
```

```python
from functools import partial

import jax
import jax.numpy as jnp
import numpy as np
from jax import lax
from jax.experimental import pallas as pl
from jax.experimental.pallas import tpu as pltpu
from jax.sharding import PartitionSpec as P

HEAD_DIM = 64
GRID = 14
TOK = 1568
ROWS = 392
D = 768
HEADS_HERE = 3
QCHUNK = 224
CHUNKS = TOK // QCHUNK
UNITS = 384
BLOCKS = 4
epsilon = 1e-06
MESH = pl.DeviceIdType.MESH
VMEM_LIMIT = 60 * 2**20
f32 = jnp.float32
bf16 = jnp.bfloat16
GATHER = (("y", "x", "z"), ("y", "z", "x"))
REDUCE = (("x", "z", "y"), ("z", "x", "y"))
RING = ("x", "y", "z")


def dot_nn(left, right):
    return jnp.dot(left, right, preferred_element_type=f32)


def dot_nt(left, right):
    return lax.dot_general(left, right, (((1,), (1,)), ((), ())), preferred_element_type=f32)


def dot_tn(left, right):
    return lax.dot_general(left, right, (((0,), (0,)), ((), ())), preferred_element_type=f32)


class Place:
    def __init__(self):
        clip = lax.axis_index("clip")
        head = lax.axis_index("head")
        self.head = head
        self.index = clip * 4 + head
        self.at = {"x": clip // 8, "y": (head // 2) * 2 + clip % 2, "z": (clip // 2) % 4}
        self.core = head % 2

    def device(self, at, core):
        return {
            "clip": at["x"] * 8 + at["z"] * 2 + at["y"] % 2,
            "head": (at["y"] // 2) * 2 + core,
        }

    def along(self, axis, step):
        at = dict(self.at)
        at[axis] = (at[axis] + step) % 4
        return self.device(at, self.core)

    def partner(self):
        return self.device(self.at, 1 - self.core)

    def across(self):
        at = dict(self.at)
        at["y"] = (at["y"] + 2) % 4
        return self.device(at, 1 - self.core)


def slot_of(axis, value):
    return (value % 2) * 2 + value // 2 if axis == "y" else value


def greet(here):
    barrier = pltpu.get_barrier_semaphore()
    peers = [here.partner(), here.across()]
    peers += [here.along(axis, step) for axis in RING for step in (1, 2, 3)]
    for device in peers:
        pl.semaphore_signal(barrier, inc=1, device_id=device, device_id_type=MESH)
    pl.semaphore_wait(barrier, len(peers))


def remote(src, dst, send, recv, device):
    return pltpu.make_async_remote_copy(
        src_ref=src, dst_ref=dst, send_sem=send, recv_sem=recv, device_id=device, device_id_type=MESH
    )


def ring_total(own, first, second, third):
    return (own + second) + (first + third)


class SmallSum:
    def __init__(self, here, held, arrived, send, recv):
        self.phases = []
        count = 0
        for phase, axis in enumerate(("core", "y", "x", "z")):
            devices = [here.partner()] if axis == "core" else [here.along(axis, k) for k in (1, 2, 3)]
            copies = []
            for device in devices:
                copies.append(
                    remote(held.at[phase], arrived.at[count], send.at[count], recv.at[count], device)
                )
                count += 1
            self.phases.append((copies, list(range(count - len(devices), count))))
        self.held, self.arrived = held, arrived

    def start(self, phase):
        for copy in self.phases[phase][0]:
            copy.start()

    def finish(self, phase):
        copies, slots = self.phases[phase]
        for copy in copies:
            copy.wait_recv()
        total = self.held[phase]
        if len(slots) == 1:
            total = total + self.arrived[slots[0]]
        else:
            total = ring_total(total, *[self.arrived[slot] for slot in slots])
        if phase < 3:
            self.held[phase + 1] = total
        return total

    def drain(self):
        for copies, _ in self.phases:
            for copy in copies:
                copy.wait_send()


def region(fixed):
    return tuple(fixed.get(axis, slice(None)) for axis in ("x", "z", "y"))


def row_mask(cubes, which):
    row = lax.broadcasted_iota(jnp.int32, (ROWS, 196), 0)
    spot = jnp.where(row >= GRID * GRID, row - GRID * GRID, row)
    line = (spot * 1171) >> 14
    cube = (line >> 1) * (GRID // 2) + ((spot - line * GRID) >> 1)
    here = lax.broadcasted_iota(jnp.int32, (ROWS, 196), 1) == cube + which * 49
    return jnp.sum(jnp.where(here, cubes[...].astype(f32), 0.0), axis=1, keepdims=True)


def unit_of(values):
    average = jnp.mean(values, axis=-1, keepdims=True)
    centered = values - average
    inverse = lax.rsqrt(jnp.mean(centered * centered, axis=-1, keepdims=True) + epsilon)
    return centered * inverse, inverse


def unit_back(scaled, unit, inverse):
    return inverse * (
        scaled
        - jnp.mean(scaled, axis=-1, keepdims=True)
        - unit * jnp.mean(scaled * unit, axis=-1, keepdims=True)
    )


MASK, GAIN1, SHIFT1, PROJ, GAIN2, SHIFT2, FC2B = range(7)


def forward_kernel(
    small, fc1_bias, cubes, tokens, w_qkv, qv_bias, w_out, w_fc1, w_fc2,
    params, normed_out, qkv_out, lse_out, mixed_keep, mixed_out_keep, mixed_in_out, w_out_all_out,
    w_last_all_out, gathered,
    normed, qkv, lse, mixed, mixed_out, mixed_in, w_out_all, w_last_all,
    rows, held, arrived, own_half, their_half, chip_block, block, values_t,
    tok_send, tok_recv, sum_send, sum_recv, half_sem, ff_send, ff_recv, fwd_send, fwd_recv,
    out_send, out_recv, mix_send, mix_recv, local_sem,
):
    here = Place()
    core, head = here.core, here.head
    at = here.at
    mate = head + 1 - 2 * core
    far = (head + 2) % 4
    far_mate = far + 1 - 2 * core

    own_half[0] = w_fc1[...].astype(f32)
    own_half[1] = w_fc2[...].astype(f32)
    column = lax.broadcasted_iota(jnp.int32, (8, D), 1) - here.index * 6
    own_small = small[...].astype(f32)
    placed = jnp.zeros((8, D), f32)
    for j in range(6):
        placed = jnp.where(column == j, own_small[:, j : j + 1], placed)
    held[0, :, 0:D] = placed
    line = lax.broadcasted_iota(jnp.int32, (8, UNITS), 0)
    unit = lax.broadcasted_iota(jnp.int32, (8, UNITS), 1) - (here.index % 16) * 24
    shifted = jnp.zeros((8, UNITS), f32)
    own_bias = fc1_bias[...].astype(f32)
    for j in range(24):
        shifted = jnp.where(unit == j, own_bias[:, j : j + 1], shifted)
    held[0, :, D : D + UNITS] = jnp.where(line == here.index // 16, shifted, 0.0)
    sums = SmallSum(here, held, arrived, sum_send, sum_recv)

    greet(here)

    def tok_copy(way, k):
        lanes = pl.ds(k * 384, 384)
        src = rows.at[far, :, lanes] if way == 2 else tokens.at[:, lanes]
        dst = rows.at[far if way == 2 else head, :, lanes]
        device = here.along("y", 2) if way == 1 else here.partner()
        return remote(src, dst, tok_send.at[way, k], tok_recv.at[way, k], device)

    half_copy = remote(
        own_half.at[:, :, pl.ds(pl.multiple_of((1 - core) * UNITS, UNITS), UNITS)],
        their_half, half_sem.at[0], half_sem.at[1], here.partner(),
    )
    half_copy.start()
    sums.start(0)
    sums.finish(0)
    sums.start(1)

    half_copy.wait_recv()
    mine = pl.ds(pl.multiple_of(core * 24, 8), 24)
    theirs = pl.ds(pl.multiple_of((1 - core) * 24, 8), 24)
    for kind in (0, 1):
        chip_block[kind, mine, :] = own_half[kind, :, pl.ds(pl.multiple_of(core * UNITS, UNITS), UNITS)]
        chip_block[kind, theirs, :] = their_half[kind]
    for part in range(3):
        for kind in (0, 1):
            block[part, kind * 48 : kind * 48 + 48, :] = chip_block[
                kind, :, part * 128 : part * 128 + 128
            ].astype(bf16)

    slots = {axis: slot_of(axis, at[axis]) for axis in RING}
    ours = pl.ds(core * 3, 3)
    block_copy = pltpu.make_async_copy(block, gathered.at[(ours,) + region(slots)], local_sem.at[0])

    def ff_copy(kind, phase, step):
        order = GATHER[kind]
        of_kind = pl.ds(kind * 48, 48)
        spot = gathered.at[(ours,) + region({a: slots[a] for a in order[phase:]}) + (of_kind,)]
        return remote(
            block.at[:, of_kind] if phase == 0 else spot, spot,
            ff_send.at[kind, phase, step - 1], ff_recv.at[kind, phase, step - 1],
            here.along(order[phase], step),
        )

    def pass_copy(kind, step):
        last = GATHER[kind][2]
        of_kind = pl.ds(kind * 48, 48)
        plane = region({last: slot_of(last, (at[last] + 4 - step) % 4)})
        spot = gathered.at[(ours,) + plane + (of_kind,)]
        return remote(spot, spot, fwd_send.at[kind, step], fwd_recv.at[kind, step], here.partner())

    def ff_start(phase):
        for step in (1, 2, 3):
            for kind in (0, 1):
                ff_copy(kind, phase, step).start()

    def ff_on(phase):
        for step in (1, 2, 3):
            for kind in (0, 1):
                ff_copy(kind, phase, step).wait_recv()
        ff_start(phase + 1)

    ff_start(0)
    block_copy.start()
    for way in (1, 0):
        for k in (0, 1):
            tok_copy(way, k).start()

    last_rows = pl.ds(384, 192)

    def out_copy(way, k):
        own = (w_out, w_qkv.at[last_rows])[k]
        every = (w_out_all, w_last_all)[k]
        src = every.at[far] if way == 2 else own
        dst = every.at[far if way == 2 else head]
        device = here.along("y", 2) if way == 1 else here.partner()
        return remote(src, dst, out_send.at[way, k], out_recv.at[way, k], device)

    for k in (0, 1):
        out_copy(0, k).start()
    w_out_all[head] = w_out[...]
    w_last_all[head] = w_qkv[384:576, :]
    rows[head] = tokens[...]
    sums.finish(1)
    sums.start(2)
    block_copy.wait()
    ff_on(0)
    sums.finish(2)
    sums.start(3)
    for k in (0, 1):
        tok_copy(0, k).wait_recv()
    params[...] = sums.finish(3)

    gain = params[GAIN1 : GAIN1 + 1, 0:D]
    shift = params[SHIFT1 : SHIFT1 + 1, 0:D]
    mask_token = params[MASK : MASK + 1, 0:D]
    biases = qv_bias[...].astype(f32)
    q_bias = biases[0:1, :]
    v_bias = biases[1:2, :]

    def project(half):
        parts = []
        for j in range(2):
            which = half * 2 + j
            masked = row_mask(cubes, which)
            start = jnp.where(masked > 0.5, mask_token, rows[which].astype(f32))
            unit1, _ = unit_of(start)
            parts.append(unit1 * gain + shift)
        normed[half] = jnp.concatenate(parts, axis=0).astype(bf16)

        to = pl.ds(pl.multiple_of(half * 784, 16), 784)
        for h in range(HEADS_HERE):
            packed = dot_nt(normed[half], w_qkv[h * 192 : h * 192 + 192, :])
            lanes = slice(h * 64, h * 64 + 64)
            query = packed[:, 0:64] + q_bias[:, lanes]
            value = packed[:, 128:192] + v_bias[:, lanes]
            qkv[h * 3, to, :] = query.astype(bf16) * bf16(0.125)
            qkv[h * 3 + 1, to, :] = packed[:, 64:128].astype(bf16)
            qkv[h * 3 + 2, to, :] = value.astype(bf16)

    chip_half = head // 2
    project(chip_half)
    ff_on(1)
    for kind in (0, 1):
        pass_copy(kind, 0).start()
    for k in (0, 1):
        tok_copy(1, k).wait_recv()
        tok_copy(2, k).start()
    for k in (0, 1):
        out_copy(1, k).start()
    for k in (0, 1):
        tok_copy(2, k).wait_recv()
    project(1 - chip_half)
    early = [
        pltpu.make_async_copy(normed, normed_out, local_sem.at[1]),
        pltpu.make_async_copy(qkv, qkv_out, local_sem.at[2]),
    ]
    for copy in early:
        copy.start()

    ones_row = (lax.broadcasted_iota(jnp.int32, (16, TOK), 0) == 0).astype(f32)
    for h in range(HEADS_HERE):
        values_t[h] = jnp.concatenate([qkv[h * 3 + 2].astype(f32).T, ones_row], axis=0).astype(bf16)

    def mix_copy(h, way):
        other, device = (
            (mate, here.partner()), (far, here.along("y", 2)), (far_mate, here.across()),
        )[way]
        return remote(
            mixed_out.at[h, other], mixed_in.at[h, head], mix_send.at[h, way], mix_recv.at[h, way], device
        )

    def mix_start(h):
        for j in range(4):
            mixed_out[h, j] = mixed[h, j * ROWS : j * ROWS + ROWS, :].astype(bf16)
        for way in (1, 2, 0):
            mix_copy(h, way).start()
        mixed_in[h, head] = mixed_out[h, head]

    def ff_pass(step):
        for kind in (0, 1):
            ff_copy(kind, 2, step).wait_recv()
            pass_copy(kind, step).start()

    def out_on():
        for k in (0, 1):
            out_copy(1, k).wait_recv()
            out_copy(2, k).start()

    def attend(h, carry):
        def score(k):
            scores = dot_nt(qkv[h * 3 + 1], qkv[h * 3, k * QCHUNK : k * QCHUNK + QCHUNK, :])
            return scores, jnp.max(scores, axis=0, keepdims=True)

        ready = score(0)
        for k in range(CHUNKS):
            scores, top = ready
            if k + 1 < CHUNKS:
                ready = score(k + 1)
            weights = jnp.exp(scores - top).astype(bf16)
            outcome = dot_nn(values_t[h], weights)
            total = outcome[64:65, :]
            mixed[h, k * QCHUNK : k * QCHUNK + QCHUNK, :] = (outcome[0:64, :] / total).T
            lse[h * CHUNKS + k] = jnp.broadcast_to(top + jnp.log(total), (8, QCHUNK))
        for n in range(HEADS_HERE - 1):
            pl.when(h == n)(partial(mix_start, n))
        pl.when(h == 1)(out_on)
        return carry

    lax.fori_loop(0, HEADS_HERE, attend, 0)

    mix_start(HEADS_HERE - 1)
    for step in (1, 2, 3):
        ff_pass(step)
    for k in (0, 1):
        out_copy(0, k).wait_recv()
        out_copy(2, k).wait_recv()
    late = [
        pltpu.make_async_copy(lse, lse_out, local_sem.at[3]),
        pltpu.make_async_copy(mixed, mixed_keep, local_sem.at[4]),
        pltpu.make_async_copy(mixed_out, mixed_out_keep, local_sem.at[5]),
        pltpu.make_async_copy(w_out_all, w_out_all_out, local_sem.at[6]),
        pltpu.make_async_copy(w_last_all, w_last_all_out, local_sem.at[8]),
    ]
    for copy in late:
        copy.start()
    for kind in (0, 1):
        for step in range(4):
            pass_copy(kind, step).wait_recv()
    for h in range(HEADS_HERE):
        for way in range(3):
            mix_copy(h, way).wait_recv()
    last_copy = pltpu.make_async_copy(mixed_in, mixed_in_out, local_sem.at[7])
    last_copy.start()
    sums.drain()
    half_copy.wait_send()
    for way in range(3):
        for k in (0, 1):
            out_copy(way, k).wait_send()
            tok_copy(way, k).wait_send()
        for h in range(HEADS_HERE):
            mix_copy(h, way).wait_send()
    for kind in (0, 1):
        for phase in range(3):
            for step in (1, 2, 3):
                ff_copy(kind, phase, step).wait_send()
        for step in range(4):
            pass_copy(kind, step).wait_send()
    for copy in early + late + [last_copy]:
        copy.wait()


VM = pl.BlockSpec(memory_space=pltpu.VMEM)
ANY = pl.BlockSpec(memory_space=pl.ANY)
DMA = pltpu.SemaphoreType.DMA


def shape(dims, kind=bf16):
    return jax.ShapeDtypeStruct(dims, kind)


def forward_call(*args):
    kept = (
        ((2, 784, D), bf16),
        ((9, TOK, 64), bf16),
        ((HEADS_HERE * CHUNKS, 8, QCHUNK), f32),
        ((HEADS_HERE, TOK, 64), f32),
        ((HEADS_HERE, 4, ROWS, 64), bf16),
        ((HEADS_HERE, 4, ROWS, 64), bf16),
        ((4, 192, D), bf16),
        ((4, 192, D), bf16),
    )
    return pl.pallas_call(
        forward_kernel,
        out_shape=(shape((8, D + UNITS), f32),)
        + tuple(shape(*k) for k in kept)
        + (shape((6, 4, 4, 4, 96, 128)),),
        in_specs=[VM] * 9,
        out_specs=(VM,) + (ANY,) * 9,
        scratch_shapes=[pltpu.VMEM(*k) for k in kept]
        + [
            pltpu.VMEM((4, ROWS, D), bf16),
            pltpu.VMEM((4, 8, D + UNITS), f32),
            pltpu.VMEM((10, 8, D + UNITS), f32),
            pltpu.VMEM((2, 24, D), f32),
            pltpu.VMEM((2, 24, UNITS), f32),
            pltpu.VMEM((2, 48, UNITS), f32),
            pltpu.VMEM((3, 96, 128), bf16),
            pltpu.VMEM((HEADS_HERE, 80, TOK), bf16),
            DMA((3, 2)), DMA((3, 2)), DMA((10,)), DMA((10,)), DMA((2,)),
            DMA((2, 3, 3)), DMA((2, 3, 3)), DMA((2, 4)), DMA((2, 4)),
            DMA((3, 2)), DMA((3, 2)), DMA((HEADS_HERE, 3)), DMA((HEADS_HERE, 3)), DMA((9,)),
        ],
        name="attention_forward",
        compiler_params=pltpu.CompilerParams(
            collective_id=0, has_side_effects=True, vmem_limit_bytes=VMEM_LIMIT
        ),
    )(*args)


SQRT_HALF = 0.7071067811865476
INV_SQRT_2PI = 0.3989422804014327


def feed_forward_kernel(
    cubes, params, tokens, cotangent, mixed_in, w_out_all, weights,
    block_out, grad_middle, grad_branch, grad_mixed, small_grads, reduced_out,
    held, grads, arrived, reduced, normed2, outer, grad_normed2,
    load_sem, pair_send, pair_recv, keep_sem,
):
    here = Place()
    core, head = here.core, here.head

    def load(b):
        chips = pl.ds(b * 16, 16)
        return pltpu.make_async_copy(weights.at[:, chips], held.at[:, chips], load_sem.at[b])

    for b in range(BLOCKS):
        load(b).start()
    barrier = pltpu.get_barrier_semaphore()
    pl.semaphore_signal(barrier, inc=1, device_id=here.partner(), device_id_type=MESH)

    masked = row_mask(cubes, head)
    start = jnp.where(masked > 0.5, params[MASK : MASK + 1, 0:D], tokens[...].astype(f32))
    branch = jnp.zeros((ROWS, D), f32)
    for j in range(4):
        some = jnp.concatenate([mixed_in[h, j] for h in range(HEADS_HERE)], axis=1)
        branch = branch + dot_nn(some, w_out_all[j])
    middle = start + branch + params[PROJ : PROJ + 1, 0:D]
    gain2 = params[GAIN2 : GAIN2 + 1, 0:D]
    unit2, _ = unit_of(middle)
    normed2[...] = (unit2 * gain2 + params[SHIFT2 : SHIFT2 + 1, 0:D]).astype(bf16)
    block_out[...] = middle
    outer[...] = jnp.zeros((ROWS, D), f32)
    grad_normed2[...] = jnp.zeros((ROWS, D), f32)
    pl.semaphore_wait(barrier, 1)
    mates = pl.ds((1 - core) * 3, 3)

    def pair_copy(b):
        chips = pl.ds(b * 16, 16)
        return remote(
            grads.at[mates, chips], arrived.at[:, chips], pair_send.at[b], pair_recv.at[b], here.partner()
        )

    def keep_copy(b):
        chips = pl.ds(b * 16, 16)
        return pltpu.make_async_copy(reduced.at[:, chips], reduced_out.at[:, chips], keep_sem.at[b])

    def add_pair(b):
        chips = pl.ds(b * 16, 16)
        pair_copy(b).wait_recv()
        for part in range(3):
            reduced[part, chips] = (
                grads[core * 3 + part, chips].astype(f32) + arrived[part, chips].astype(f32)
            ).astype(bf16)
        keep_copy(b).start()

    def some_units(b, carry):
        load(b).wait()
        chips = pl.ds(b * 16, 16)

        def weight(kind):
            return jnp.concatenate(
                [
                    held[s, chips, kind * 48 : kind * 48 + 48, :].reshape(2 * UNITS, 128)
                    for s in range(6)
                ],
                axis=1,
            )

        def keep(kind, grad):
            grad = grad.astype(bf16)
            for s in range(6):
                grads[s, chips, kind * 48 : kind * 48 + 48, :] = grad[
                    :, s * 128 : s * 128 + 128
                ].reshape(16, 48, 128)

        bias = jnp.concatenate(
            [params[pl.ds(2 * b + k, 1), D : D + UNITS] for k in (0, 1)], axis=1
        )
        inner = dot_nt(normed2[...], weight(0)) + bias
        below = 0.5 + 0.5 * lax.erf(inner * SQRT_HALF)
        active = (inner * below).astype(bf16)
        slope = below + inner * (INV_SQRT_2PI * jnp.exp(-0.5 * inner * inner))
        grad_active = dot_nt(cotangent[...], weight(1))
        grad_inner = (grad_active * slope).astype(bf16)
        bias_grad = jnp.sum(grad_inner.astype(f32), axis=0, keepdims=True)
        for k in (0, 1):
            small_grads[pl.ds(2 * b + k, 1), D : D + UNITS] = bias_grad[:, k * UNITS : k * UNITS + UNITS]
        outer[...] += dot_nn(active, weight(1))
        grad_normed2[...] += dot_nn(grad_inner, weight(0))
        keep(1, dot_tn(active, cotangent[...]))
        keep(0, dot_tn(grad_inner, normed2[...]))
        pair_copy(b).start()

        @pl.when(b > 0)
        def _():
            add_pair(b - 1)

        return carry

    lax.fori_loop(0, BLOCKS, some_units, 0)

    middle = block_out[...]
    block_out[...] = middle + outer[...] + params[FC2B : FC2B + 1, 0:D]
    unit2, inverse2 = unit_of(middle)
    grad_out = cotangent[...].astype(f32)
    back = grad_normed2[...]
    grad_mid = grad_out + unit_back(back * gain2, unit2, inverse2)
    grad_middle[...] = grad_mid
    low = grad_mid.astype(bf16)
    grad_branch[...] = low
    for j in range(4):
        some = dot_nt(low, w_out_all[j]).astype(bf16)
        for h in range(HEADS_HERE):
            grad_mixed[h, j] = some[:, h * 64 : h * 64 + 64]
    sums = [
        jnp.sum(v, axis=0, keepdims=True)
        for v in (grad_mid, back * unit2, back, grad_out)
    ]
    small_grads[:, 0:D] = jnp.concatenate(sums + [jnp.zeros((4, D), f32)], axis=0)
    add_pair(BLOCKS - 1)
    for b in range(BLOCKS):
        pair_copy(b).wait_send()
        keep_copy(b).wait()


def feed_forward_call(*args):
    return pl.pallas_call(
        feed_forward_kernel,
        out_shape=(
            shape((ROWS, D), f32),
            shape((ROWS, D), f32),
            shape((ROWS, D)),
            shape((HEADS_HERE, 4, ROWS, 64)),
            shape((8, D + UNITS), f32),
            shape((3, 64, 96, 128)),
        ),
        in_specs=[VM] * 6 + [ANY],
        out_specs=(VM,) * 5 + (ANY,),
        scratch_shapes=[
            pltpu.VMEM((6, 64, 96, 128), bf16),
            pltpu.VMEM((6, 64, 96, 128), bf16),
            pltpu.VMEM((3, 64, 96, 128), bf16),
            pltpu.VMEM((3, 64, 96, 128), bf16),
            pltpu.VMEM((ROWS, D), bf16),
            pltpu.VMEM((ROWS, D), f32),
            pltpu.VMEM((ROWS, D), f32),
            DMA((BLOCKS,)), DMA((BLOCKS,)), DMA((BLOCKS,)), DMA((BLOCKS,)),
        ],
        name="feed_forward",
        compiler_params=pltpu.CompilerParams(
            collective_id=1, has_side_effects=True, vmem_limit_bytes=VMEM_LIMIT
        ),
    )(*args)


def without(axes, axis):
    return tuple(a for a in axes if a != axis)


def backward_kernel(
    cubes, params, grad_mixed, grad_branch, small_grads, reduced,
    grad_middle_in, tokens_in, normed_in, qkv_in, lse_in, mixed_in, mixed_out_in, w_qkv_in, w_last_in,
    tokens_grad, small_first, small_last, w_grads, w_fc1_grad, w_fc2_grad,
    grad_middle, tokens, normed, qkv, lse, mixed, mixed_out, w_qkv, w_last, own_reduced,
    mixed_back, mixed_wide, outer_back, queries, keys_t, grad_q, grad_kv, packed_back,
    branch_in, input_back, pair_out, pair_in, far_out, far_in,
    held, arrived, held_last, arrived_last,
    ff_in0, ff_sum1, ff_in1, ff_sum2, ff_in2, ff_last, ff_mate,
    w_src, w_in, w_z, w_z_in, w_y, w_y_in, w_all, column_sums,
    mix_send, mix_recv, br_send, br_recv, in_send, in_recv, sum_send, sum_recv, last_send, last_recv,
    ff_send, ff_recv, mate_sem, wx_send, wx_recv, wz_send, wz_recv, wy_send, wy_recv, wg_send, wg_recv,
    load_sem, last_out, last_in, head_send, head_recv,
):
    here = Place()
    core, head, at = here.core, here.head, here.at
    mate = head + 1 - 2 * core
    far = (head + 2) % 4
    far_mate = far + 1 - 2 * core
    slots = {axis: slot_of(axis, at[axis]) for axis in RING}

    def own_share(kind):
        axis = REDUCE[kind][0]
        return reduced.at[(slice(None),) + region({axis: slots[axis]}) + (pl.ds(kind * 48, 48),)]

    pairs = (
        (qkv_in, qkv), (lse_in, lse), (mixed_in, mixed), (tokens_in, tokens), (w_qkv_in, w_qkv),
        (normed_in, normed), (mixed_out_in, mixed_out), (grad_middle_in, grad_middle),
        (own_share(0), own_reduced.at[0]), (own_share(1), own_reduced.at[1]), (w_last_in, w_last),
    )
    loads = [pltpu.make_async_copy(src, dst, load_sem.at[k]) for k, (src, dst) in enumerate(pairs)]
    for copy in loads:
        copy.start()
    greet(here)

    def mix_copy(h, way):
        other, device = (
            (mate, here.partner()), (far, here.along("y", 2)), (far_mate, here.across()),
        )[way]
        return remote(
            grad_mixed.at[h, other], mixed_back.at[h, head], mix_send.at[h, way], mix_recv.at[h, way], device
        )

    for h in range(HEADS_HERE):
        for way in (1, 2, 0):
            mix_copy(h, way).start()

    def peer_slot(axis, step):
        return slot_of(axis, (at[axis] + step) % 4)

    def ff_left(kind, phase):
        left = ("x", "z", "y")
        for done in REDUCE[kind][:phase]:
            left = without(left, done)
        return left

    def ff_copy(kind, phase, step):
        axis = REDUCE[kind][phase]
        where = tuple(
            peer_slot(axis, step) if a == axis else slice(None) for a in ff_left(kind, phase)
        )
        where = (slice(None),) + where
        if phase == 0:
            src = reduced.at[where + (pl.ds(kind * 48, 48),)]
        else:
            src = (ff_sum1, ff_sum2)[phase - 1].at[(kind,) + where]
        dst = (ff_in0, ff_in1, ff_in2)[phase]
        return remote(
            src, dst.at[kind, step - 1],
            ff_send.at[kind, phase, step - 1], ff_recv.at[kind, phase, step - 1],
            here.along(axis, step),
        )

    def ff_start(kind, phase):
        for step in (1, 2, 3):
            ff_copy(kind, phase, step).start()

    def ff_add(kind, phase):
        axis = REDUCE[kind][phase]
        where = tuple(slots[axis] if a == axis else slice(None) for a in ff_left(kind, phase))
        arrived_in = (ff_in0, ff_in1, ff_in2)[phase]
        for step in (1, 2, 3):
            ff_copy(kind, phase, step).wait_recv()
        if phase == 0:
            loads[8 + kind].wait()

        def some(part):
            if phase == 0:
                own = own_reduced[kind, part]
            else:
                own = (ff_sum1, ff_sum2)[phase - 1][(kind, part) + where]
            return ring_total(
                own.astype(f32), *[arrived_in[kind, k, part].astype(f32) for k in range(3)]
            )

        if phase == 0:
            @pl.loop(0, 3)
            def _(part):
                ff_sum1[kind, part] = some(part).astype(bf16)
        else:
            for part in range(3):
                total = some(part)
                if phase == 1:
                    ff_sum2[kind, part] = total.astype(bf16)
                else:
                    ff_last[kind, :, part * 128 : part * 128 + 128] = total

    for kind in (0, 1):
        ff_start(kind, 0)

    held[0] = small_grads[...]
    sums = SmallSum(here, held, arrived, sum_send, sum_recv)
    sums.start(0)

    beside = dict(at)
    beside["y"] = at["y"] + 1 - 2 * (at["y"] % 2)
    beside = here.device(beside, core)

    def first_axis(n):
        return "xz"[n % 2]

    def wx_copy(n, step):
        axis = first_axis(n)
        return remote(
            w_src.at[n, (at[axis] + step) % 4], w_in.at[n, step - 1],
            wx_send.at[n, step - 1], wx_recv.at[n, step - 1], here.along(axis, step),
        )

    def wz_copy(n, step):
        return remote(
            w_z.at[n], w_z_in.at[n, step - 1], wz_send.at[n, step - 1], wz_recv.at[n, step - 1],
            here.along(first_axis(n + 1), step),
        )

    def wy_copy(n):
        return remote(w_y.at[n], w_y_in.at[n], wy_send.at[n], wy_recv.at[n], beside)

    def wg_copy(n, step):
        axis = first_axis(n)
        spot = w_all.at[n, at[axis]]
        return remote(
            spot, spot, wg_send.at[n, step - 1], wg_recv.at[n, step - 1], here.along(axis, step)
        )

    def w_begin(n, grad):
        grad = grad.astype(bf16)
        for s in range(6):
            lanes = slice(s * 128, s * 128 + 128)
            first = s * 192
            for chunk in range(4):
                low, high = max(first, chunk * 288), min(first + 192, chunk * 288 + 288)
                if low < high:
                    w_src[n, chunk, low - chunk * 288 : high - chunk * 288, :] = grad[
                        low - first : high - first, lanes
                    ]
        for step in (1, 2, 3):
            wx_copy(n, step).start()

    def w_second(n):
        for step in (1, 2, 3):
            wx_copy(n, step).wait_recv()
        w_z[n] = ring_total(
            w_src[n, at[first_axis(n)]].astype(f32), *[w_in[n, k].astype(f32) for k in range(3)]
        ).astype(bf16)
        for step in (1, 2, 3):
            wz_copy(n, step).start()

    def w_third(n):
        for step in (1, 2, 3):
            wz_copy(n, step).wait_recv()
        w_y[n] = ring_total(
            w_z[n].astype(f32), *[w_z_in[n, k].astype(f32) for k in range(3)]
        ).astype(bf16)
        wy_copy(n).start()

    def w_fourth(n):
        wy_copy(n).wait_recv()
        w_all[n, at[first_axis(n)]] = (w_y[n].astype(f32) + w_y_in[n].astype(f32)).astype(bf16)
        for step in (1, 2, 3):
            wg_copy(n, step).start()

    def w_end(n):
        for step in (1, 2, 3):
            wg_copy(n, step).wait_recv()
        w_grads[n] = w_all[n]

    br_near = remote(grad_branch, branch_in.at[head], br_send.at[0], br_recv.at[0], here.partner())
    br_far = remote(grad_branch, branch_in.at[head], br_send.at[1], br_recv.at[1], here.along("y", 2))
    br_pass = remote(branch_in.at[far], branch_in.at[far], br_send.at[2], br_recv.at[2], here.partner())
    branch_in[head] = grad_branch[...]
    for h in range(HEADS_HERE):
        mixed_back[h, head] = grad_mixed[h, head]

    zeros = jnp.zeros((TOK, 64), bf16)
    loads[0].wait()
    for h in range(HEADS_HERE):
        query = qkv[h * 3]
        queries[h] = jnp.concatenate([zeros, query], axis=1)
        keys_t[h] = qkv[h * 3 + 1].astype(f32).T.astype(bf16)

    def outer_in(h):
        for way in range(3):
            mix_copy(h, way).wait_recv()
        for j in range(4):
            mixed_wide[j * ROWS : j * ROWS + ROWS, :] = mixed_back[h, j].astype(f32)
        outer_back[h] = jnp.concatenate([mixed_wide[...].astype(bf16), zeros], axis=1)

    outer_in(0)
    br_far.start()
    br_near.start()
    for k in (1, 2, 3, 4, 5, 6, 7):
        loads[k].wait()

    def branch_on():
        br_far.wait_recv()
        br_pass.start()

    def branch_end():
        br_near.wait_recv()
        br_pass.wait_recv()
        grad = jnp.zeros((192, D), f32)
        for j in range(4):
            some = jnp.concatenate([mixed_out[h, j] for h in range(HEADS_HERE)], axis=1)
            grad = grad + dot_tn(some, branch_in[j])
        w_begin(0, grad)

    def sum_on(phase):
        total = sums.finish(phase)
        if phase < 3:
            sums.start(phase + 1)
        else:
            small_first[...] = total

    def ff_on(phase):
        for kind in (0, 1):
            ff_add(kind, phase)
            if phase < 2:
                ff_start(kind, phase + 1)

    chip = head // 2
    lane = lax.broadcasted_iota(jnp.int32, (TOK, 128), 1)

    def attend(h, carry):
        def score(k):
            chunk = slice(k * QCHUNK, k * QCHUNK + QCHUNK)
            scores = dot_nt(qkv[h * 3 + 1], qkv[h * 3, chunk, :])
            return scores, dot_nt(qkv[h * 3 + 2], outer_back[h, chunk, 0:64])

        ready = score(0)
        for k in range(CHUNKS):
            chunk = slice(k * QCHUNK, k * QCHUNK + QCHUNK)
            scores, grad_weights = ready
            if k + 1 < CHUNKS:
                ready = score(k + 1)
            given = outer_back[h, chunk, :]
            weights = jnp.exp(scores - lse[h * CHUNKS + k, 0:1, :])
            delta = jnp.sum(
                (given[:, 0:64].astype(f32) * mixed[h, chunk, :]).T, axis=0, keepdims=True
            )
            grad_scores = (weights * (grad_weights - delta)).astype(bf16)
            share = dot_nn(weights.astype(bf16), given) + dot_nn(grad_scores, queries[h, chunk, :])
            if k == 0:
                grad_kv[...] = share
            else:
                grad_kv[...] += share
            grad_q[chunk, 0:64] = dot_nn(keys_t[h], grad_scores).T * 0.125

        both = grad_kv[...]
        first = jnp.where(lane < 64, grad_q[...], both)
        packed_back[:, 0:128] = first.astype(bf16)
        packed_back[:, 128:192] = both[:, 0:64].astype(bf16)
        @pl.when(h < HEADS_HERE - 1)
        def _():
            for k, half in enumerate((1 - chip, chip)):
                share = dot_nn(
                    packed_back[pl.ds(pl.multiple_of(half * 784, 16), 784), :],
                    w_qkv[pl.ds(pl.multiple_of(h * 192, 16), 192), :],
                )
                for j in (0, 1):
                    some = share[j * ROWS : j * ROWS + ROWS]

                    @pl.when(h == 0)
                    def _():
                        input_back[half, j] = some

                    @pl.when(h > 0)
                    def _():
                        input_back[half, j] += some

                pl.when(h == HEADS_HERE - 2)(partial(pair_start, k, half))

        @pl.when(h == HEADS_HERE - 1)
        def _():
            for j in range(4):
                own = slice(j * ROWS, j * ROWS + ROWS)
                last_out[j] = jnp.concatenate([first[own], both[own, 0:64]], axis=1).astype(bf16)
            for way in (1, 2, 0):
                head_copy(way).start()

        column_sums[pl.ds(h, 1), :] = jnp.sum(packed_back[...].astype(f32), axis=0, keepdims=True)
        w_grad = dot_tn(packed_back[...], normed[...])
        for n in range(HEADS_HERE):
            pl.when(h == n)(partial(w_begin, n + 1, w_grad))

        @pl.when(h == 0)
        def _():
            outer_in(1)
            sum_on(0)

        @pl.when(h == 1)
        def _():
            outer_in(2)
            sum_on(1)
            branch_on()
            pair_copies[0].wait_recv()
            far_out[...] = (input_back[1 - chip, core] + pair_in[0].astype(f32)).astype(bf16)
            far_copy.start()

        return carry

    pair_copies = [
        remote(pair_out.at[k], pair_in.at[k], in_send.at[k], in_recv.at[k], here.partner()) for k in (0, 1)
    ]
    far_copy = remote(far_out, far_in, in_send.at[2], in_recv.at[2], here.along("y", 2))

    def head_copy(way):
        other, device = (
            (mate, here.partner()), (far, here.along("y", 2)), (far_mate, here.across()),
        )[way]
        return remote(last_out.at[other], last_in.at[head], head_send.at[way], head_recv.at[way], device)

    def pair_start(k, half):
        pair_out[k] = input_back[half, 1 - core].astype(bf16)
        pair_copies[k].start()

    lax.fori_loop(0, HEADS_HERE, attend, 0)

    ff_on(0)
    branch_end()
    w_second(1)
    w_second(2)
    sum_on(2)
    ff_on(1)
    w_second(3)
    w_third(1)
    w_third(2)
    sum_on(3)
    w_second(0)

    masked = row_mask(cubes, head)
    start = jnp.where(masked > 0.5, params[MASK : MASK + 1, 0:D], tokens[...].astype(f32))
    unit1, inverse1 = unit_of(start)
    pair_copies[1].wait_recv()
    far_copy.wait_recv()
    last_in[head] = last_out[head]
    loads[10].wait()
    back = input_back[chip, core] + pair_in[1].astype(f32) + far_in[...].astype(f32)
    for way in range(3):
        head_copy(way).wait_recv()
    for j in range(4):
        back = back + dot_nn(last_in[j], w_last[j])
    grad_start = grad_middle[...] + unit_back(
        back * params[GAIN1 : GAIN1 + 1, 0:D], unit1, inverse1
    )
    tokens_grad[...] = jnp.where(masked > 0.5, 0.0, grad_start)
    totals = [
        jnp.sum(v, axis=0, keepdims=True)
        for v in (back * unit1, back, jnp.where(masked > 0.5, grad_start, 0.0))
    ]
    held_last[0, :, 0:384] = jnp.concatenate(
        [v[:, k * 384 : k * 384 + 384] for v in totals for k in (0, 1)] + [jnp.zeros((2, 384), f32)],
        axis=0,
    )
    line = lax.broadcasted_iota(jnp.int32, (8, 192), 0)
    of_query = jnp.concatenate([column_sums[h : h + 1, 0:64] for h in range(HEADS_HERE)], axis=1)
    of_value = jnp.concatenate([column_sums[h : h + 1, 128:192] for h in range(HEADS_HERE)], axis=1)
    held_last[0, :, 384:576] = jnp.where(
        line == 2 * head, of_query, jnp.where(line == 2 * head + 1, of_value, 0.0)
    )
    held_last[0, :, 576:640] = jnp.zeros((8, 64), f32)
    last = SmallSum(here, held_last, arrived_last, last_send, last_recv)
    last.start(0)
    w_third(3)
    last.finish(0)
    last.start(1)
    w_fourth(1)
    w_fourth(2)
    ff_on(2)
    mate_copy = remote(
        ff_last.at[:, pl.ds(pl.multiple_of((1 - core) * 24, 8), 24), :], ff_mate,
        mate_sem.at[0], mate_sem.at[1], here.partner(),
    )
    mate_copy.start()
    last.finish(1)
    last.start(2)
    w_third(0)
    w_fourth(3)
    last.finish(2)
    last.start(3)
    w_fourth(0)
    mate_copy.wait_recv()
    for kind, target in ((0, w_fc1_grad), (1, w_fc2_grad)):
        target[:, pl.ds(pl.multiple_of(core * UNITS, UNITS), UNITS)] = ff_last[
            kind, pl.ds(pl.multiple_of(core * 24, 8), 24), :
        ]
        target[:, pl.ds(pl.multiple_of((1 - core) * UNITS, UNITS), UNITS)] = ff_mate[kind]
    w_end(1)
    w_end(2)
    small_last[...] = last.finish(3)
    w_end(3)
    w_end(0)

    sums.drain()
    last.drain()
    for copy in [br_near, br_far, br_pass, far_copy, mate_copy] + pair_copies:
        copy.wait_send()
    for way in range(3):
        head_copy(way).wait_send()
    for h in range(HEADS_HERE):
        for way in range(3):
            mix_copy(h, way).wait_send()
    for kind in (0, 1):
        for phase in range(3):
            for step in (1, 2, 3):
                ff_copy(kind, phase, step).wait_send()
    for n in range(4):
        for step in (1, 2, 3):
            wx_copy(n, step).wait_send()
            wz_copy(n, step).wait_send()
            wg_copy(n, step).wait_send()
        wy_copy(n).wait_send()


def backward_call(*args):
    loaded = (
        ((ROWS, D), f32),
        ((ROWS, D), bf16),
        ((TOK, D), bf16),
        ((9, TOK, 64), bf16),
        ((HEADS_HERE * CHUNKS, 8, QCHUNK), f32),
        ((HEADS_HERE, TOK, 64), f32),
        ((HEADS_HERE, 4, ROWS, 64), bf16),
        ((576, D), bf16),
        ((4, 192, D), bf16),
    )
    return pl.pallas_call(
        backward_kernel,
        out_shape=(
            shape((ROWS, D), f32),
            shape((8, D + UNITS), f32),
            shape((8, 640), f32),
            shape((4, 4, 288, 128)),
            shape((24, D), f32),
            shape((24, D), f32),
        ),
        in_specs=[VM] * 5 + [ANY] * 10,
        out_specs=(VM,) * 6,
        scratch_shapes=[pltpu.VMEM(*k) for k in loaded]
        + [
            pltpu.VMEM((2, 3, 4, 4, 48, 128), bf16),
            pltpu.VMEM((HEADS_HERE, 4, ROWS, 64), bf16),
            pltpu.VMEM((TOK, 64), f32),
            pltpu.VMEM((HEADS_HERE, TOK, 128), bf16),
            pltpu.VMEM((HEADS_HERE, TOK, 128), bf16),
            pltpu.VMEM((HEADS_HERE, 64, TOK), bf16),
            pltpu.VMEM((TOK, 128), f32),
            pltpu.VMEM((TOK, 128), f32),
            pltpu.VMEM((TOK, 192), bf16),
            pltpu.VMEM((4, ROWS, D), bf16),
            pltpu.VMEM((2, 2, ROWS, D), f32),
            pltpu.VMEM((2, ROWS, D), bf16),
            pltpu.VMEM((2, ROWS, D), bf16),
            pltpu.VMEM((ROWS, D), bf16),
            pltpu.VMEM((ROWS, D), bf16),
            pltpu.VMEM((4, 8, D + UNITS), f32),
            pltpu.VMEM((10, 8, D + UNITS), f32),
            pltpu.VMEM((4, 8, 640), f32),
            pltpu.VMEM((10, 8, 640), f32),
            pltpu.VMEM((2, 3, 3, 4, 4, 48, 128), bf16),
            pltpu.VMEM((2, 3, 4, 4, 48, 128), bf16),
            pltpu.VMEM((2, 3, 3, 4, 48, 128), bf16),
            pltpu.VMEM((2, 3, 4, 48, 128), bf16),
            pltpu.VMEM((2, 3, 3, 48, 128), bf16),
            pltpu.VMEM((2, 48, UNITS), f32),
            pltpu.VMEM((2, 24, UNITS), f32),
            pltpu.VMEM((4, 4, 288, 128), bf16),
            pltpu.VMEM((4, 3, 288, 128), bf16),
            pltpu.VMEM((4, 288, 128), bf16),
            pltpu.VMEM((4, 3, 288, 128), bf16),
            pltpu.VMEM((4, 288, 128), bf16),
            pltpu.VMEM((4, 288, 128), bf16),
            pltpu.VMEM((4, 4, 288, 128), bf16),
            pltpu.VMEM((8, 192), f32),
            DMA((HEADS_HERE, 3)), DMA((HEADS_HERE, 3)), DMA((3,)), DMA((3,)), DMA((3,)), DMA((3,)),
            DMA((10,)), DMA((10,)), DMA((10,)), DMA((10,)),
            DMA((2, 3, 3)), DMA((2, 3, 3)), DMA((2,)),
            DMA((4, 3)), DMA((4, 3)), DMA((4, 3)), DMA((4, 3)), DMA((4,)), DMA((4,)), DMA((4, 3)), DMA((4, 3)),
            DMA((11,)),
            pltpu.VMEM((4, ROWS, 192), bf16),
            pltpu.VMEM((4, ROWS, 192), bf16),
            DMA((3,)), DMA((3,)),
        ],
        name="attention_backward",
        compiler_params=pltpu.CompilerParams(
            collective_id=2, has_side_effects=True, vmem_limit_bytes=VMEM_LIMIT
        ),
    )(*args)


def results_kernel(
    block_in, tokens_in, w_grads, w_fc1_in, w_fc2_in, first, last,
    block_out, tokens_grad, mask_grad, gain1_grad, shift1_grad, w_qkv_grad, qv_grad, w_out_grad,
    proj_grad, gain2_grad, shift2_grad, w_fc1_grad, fc1_grad, w_fc2_grad, fc2_grad,
):
    here = Place()
    pairs = (
        (block_in, block_out), (tokens_in, tokens_grad), (w_fc1_in, w_fc1_grad), (w_fc2_in, w_fc2_grad)
    )
    for src, dst in pairs:
        dst[...] = src[...]

    def pick(line, offset, count):
        column = lax.broadcasted_iota(jnp.int32, line.shape, 1) - offset
        spot = lax.broadcasted_iota(jnp.int32, (1, count), 1)
        out = jnp.zeros((1, count), f32)
        for j in range(count):
            one = jnp.sum(jnp.where(column == j, line, 0.0), axis=1, keepdims=True)
            out = jnp.where(spot == j, one, out)
        return out

    index = here.index
    for row, target in ((0, proj_grad), (1, gain2_grad), (2, shift2_grad), (3, fc2_grad)):
        target[...] = pick(first[row : row + 1, 0:D], index * 6, 6)
    fc1_grad[...] = pick(first[pl.ds(index // 16, 1), D : D + UNITS], (index % 16) * 24, 24)
    for k, target in enumerate((gain1_grad, shift1_grad, mask_grad)):
        target[...] = pick(last[pl.ds(2 * k + index // 64, 1), 0:384], (index % 64) * 6, 6)
    for k in (0, 1):
        qv_grad[k : k + 1, :] = last[pl.ds(2 * here.head + k, 1), 384:576]
    for n in range(4):
        for s in range(6):
            lanes = slice(s * 128, s * 128 + 128)
            start = s * 192
            for chunk in range(4):
                low, high = max(start, chunk * 288), min(start + 192, chunk * 288 + 288)
                if low < high:
                    got = w_grads[n, chunk, low - chunk * 288 : high - chunk * 288, :].astype(f32)
                    if n == 0:
                        w_out_grad[low - start : high - start, lanes] = got
                    else:
                        base = (n - 1) * 192 - start
                        w_qkv_grad[base + low : base + high, lanes] = got


def results_call(*args):
    six = shape((1, 6), f32)
    return pl.pallas_call(
        results_kernel,
        out_shape=(
            shape((ROWS, D), f32), shape((ROWS, D), f32), six, six, six, shape((576, D), f32),
            shape((2, 192), f32), shape((192, D), f32), six, six, six,
            shape((24, D), f32), shape((1, 24), f32), shape((24, D), f32), six,
        ),
        in_specs=[VM] * 7,
        out_specs=(VM,) * 15,
        name="results",
        compiler_params=pltpu.CompilerParams(vmem_limit_bytes=VMEM_LIMIT),
    )(*args)


def body(
    tokens, cube_mask, mask_token, norm1_gain, norm1_bias, w_qkv, qv_bias, w_out, proj_bias,
    norm2_gain, norm2_bias, w_fc1, fc1_bias, w_fc2, fc2_bias, cotangent,
):
    small = jnp.stack(
        [mask_token, norm1_gain, norm1_bias, proj_bias, norm2_gain, norm2_bias, fc2_bias, fc2_bias]
    )
    w_qkv_t = w_qkv.T
    params, normed, qkv, lse, mixed, mixed_out, mixed_in, w_out_all, w_last_all, weights = forward_call(
        small, fc1_bias[None], cube_mask, tokens, w_qkv_t, qv_bias, w_out, w_fc1.T, w_fc2,
    )
    block_out, grad_middle, grad_branch, grad_mixed, small_grads, reduced = feed_forward_call(
        cube_mask, params, tokens, cotangent, mixed_in, w_out_all, weights.reshape(6, 64, 96, 128),
    )
    tokens_grad, small_first, small_last, w_grads, w_fc1_grad, w_fc2_grad = backward_call(
        cube_mask, params, grad_mixed, grad_branch, small_grads, reduced.reshape(3, 4, 4, 4, 96, 128),
        grad_middle, tokens, normed.reshape(TOK, D), qkv, lse, mixed, mixed_out, w_qkv_t, w_last_all,
    )
    outs = list(
        results_call(block_out, tokens_grad, w_grads, w_fc1_grad, w_fc2_grad, small_first, small_last)
    )
    for k in (2, 3, 4, 8, 9, 10, 12, 14):
        outs[k] = outs[k].reshape(-1)
    outs[5] = outs[5].T
    outs[11] = outs[11].T
    return tuple(outs)


def solution(mesh):
    every = P(("clip", "head"))
    rows = P(("clip", "head"), None)
    columns = P(None, ("clip", "head"))
    in_specs = (
        rows, P("clip", None), every, every, every, P(None, "head"), P(None, "head"),
        P("head", None), every, every, every, columns, every, rows, every, rows,
    )
    out_specs = (
        rows, rows, every, every, every, P(None, "head"), P(None, "head"), P("head", None),
        every, every, every, columns, every, rows, every,
    )
    return jax.shard_map(body, mesh=mesh, in_specs=in_specs, out_specs=out_specs, check_vma=False)
```

```python
from functools import partial

import jax
import jax.numpy as jnp
import numpy as np
from jax import lax
from jax.experimental import pallas as pl
from jax.experimental.pallas import tpu as pltpu
from jax.sharding import PartitionSpec as P

HEAD_DIM = 64
GRID = 14
TOK = 1568
ROWS = 392
D = 768
HEADS_HERE = 3
QCHUNK = 224
CHUNKS = TOK // QCHUNK
UNITS = 384
BLOCKS = 4
epsilon = 1e-06
MESH = pl.DeviceIdType.MESH
VMEM_LIMIT = 60 * 2**20
f32 = jnp.float32
bf16 = jnp.bfloat16
GATHER = (("y", "x", "z"), ("y", "z", "x"))
REDUCE = (("x", "z", "y"), ("z", "x", "y"))
RING = ("x", "y", "z")


def dot_nn(left, right):
    return jnp.dot(left, right, preferred_element_type=f32)


def dot_nt(left, right):
    return lax.dot_general(left, right, (((1,), (1,)), ((), ())), preferred_element_type=f32)


def dot_tn(left, right):
    return lax.dot_general(left, right, (((0,), (0,)), ((), ())), preferred_element_type=f32)


class Place:
    def __init__(self):
        clip = lax.axis_index("clip")
        head = lax.axis_index("head")
        self.head = head
        self.index = clip * 4 + head
        self.at = {"x": clip // 8, "y": (head // 2) * 2 + clip % 2, "z": (clip // 2) % 4}
        self.core = head % 2

    def device(self, at, core):
        return {
            "clip": at["x"] * 8 + at["z"] * 2 + at["y"] % 2,
            "head": (at["y"] // 2) * 2 + core,
        }

    def along(self, axis, step):
        at = dict(self.at)
        at[axis] = (at[axis] + step) % 4
        return self.device(at, self.core)

    def partner(self):
        return self.device(self.at, 1 - self.core)

    def across(self):
        at = dict(self.at)
        at["y"] = (at["y"] + 2) % 4
        return self.device(at, 1 - self.core)


def slot_of(axis, value):
    return (value % 2) * 2 + value // 2 if axis == "y" else value


def greet(here):
    barrier = pltpu.get_barrier_semaphore()
    peers = [here.partner(), here.across()]
    peers += [here.along(axis, step) for axis in RING for step in (1, 2, 3)]
    for device in peers:
        pl.semaphore_signal(barrier, inc=1, device_id=device, device_id_type=MESH)
    pl.semaphore_wait(barrier, len(peers))


def remote(src, dst, send, recv, device):
    return pltpu.make_async_remote_copy(
        src_ref=src, dst_ref=dst, send_sem=send, recv_sem=recv, device_id=device, device_id_type=MESH
    )


def ring_total(own, first, second, third):
    return (own + second) + (first + third)


class SmallSum:
    def __init__(self, here, held, arrived, send, recv):
        self.phases = []
        count = 0
        for phase, axis in enumerate(("core", "y", "x", "z")):
            devices = [here.partner()] if axis == "core" else [here.along(axis, k) for k in (1, 2, 3)]
            copies = []
            for device in devices:
                copies.append(
                    remote(held.at[phase], arrived.at[count], send.at[count], recv.at[count], device)
                )
                count += 1
            self.phases.append((copies, list(range(count - len(devices), count))))
        self.held, self.arrived = held, arrived

    def start(self, phase):
        for copy in self.phases[phase][0]:
            copy.start()

    def finish(self, phase):
        copies, slots = self.phases[phase]
        for copy in copies:
            copy.wait_recv()
        total = self.held[phase]
        if len(slots) == 1:
            total = total + self.arrived[slots[0]]
        else:
            total = ring_total(total, *[self.arrived[slot] for slot in slots])
        if phase < 3:
            self.held[phase + 1] = total
        return total

    def drain(self):
        for copies, _ in self.phases:
            for copy in copies:
                copy.wait_send()


def region(fixed):
    return tuple(fixed.get(axis, slice(None)) for axis in ("x", "z", "y"))


def row_mask(cubes, which):
    row = lax.broadcasted_iota(jnp.int32, (ROWS, 196), 0)
    spot = jnp.where(row >= GRID * GRID, row - GRID * GRID, row)
    line = (spot * 1171) >> 14
    cube = (line >> 1) * (GRID // 2) + ((spot - line * GRID) >> 1)
    here = lax.broadcasted_iota(jnp.int32, (ROWS, 196), 1) == cube + which * 49
    return jnp.sum(jnp.where(here, cubes[...].astype(f32), 0.0), axis=1, keepdims=True)


def unit_of(values):
    average = jnp.mean(values, axis=-1, keepdims=True)
    centered = values - average
    inverse = lax.rsqrt(jnp.mean(centered * centered, axis=-1, keepdims=True) + epsilon)
    return centered * inverse, inverse


def unit_back(scaled, unit, inverse):
    return inverse * (
        scaled
        - jnp.mean(scaled, axis=-1, keepdims=True)
        - unit * jnp.mean(scaled * unit, axis=-1, keepdims=True)
    )


MASK, GAIN1, SHIFT1, PROJ, GAIN2, SHIFT2, FC2B = range(7)


def forward_kernel(
    small, fc1_bias, cubes, tokens, w_qkv, qv_bias, w_out, w_fc1, w_fc2,
    params, normed_out, qkv_out, lse_out, mixed_keep, pair_keep, last_keep, pair_in_out, last_in_out, w_out_all_out,
    w_last_all_out, gathered,
    normed, qkv, lse, mixed, pair_out, last_out, pair_in, last_in, w_out_all, w_last_all,
    rows, held, arrived, own_half, their_half, chip_block, block, values_t,
    tok_send, tok_recv, sum_send, sum_recv, half_sem, ff_send, ff_recv, fwd_send, fwd_recv,
    out_send, out_recv, mix_send, mix_recv, local_sem, on_send, on_recv,
):
    here = Place()
    core, head = here.core, here.head
    at = here.at
    mate = head + 1 - 2 * core
    far = (head + 2) % 4
    far_mate = far + 1 - 2 * core

    own_half[0] = w_fc1[...].astype(f32)
    own_half[1] = w_fc2[...].astype(f32)
    column = lax.broadcasted_iota(jnp.int32, (8, D), 1) - here.index * 6
    own_small = small[...].astype(f32)
    placed = jnp.zeros((8, D), f32)
    for j in range(6):
        placed = jnp.where(column == j, own_small[:, j : j + 1], placed)
    held[0, :, 0:D] = placed
    line = lax.broadcasted_iota(jnp.int32, (8, UNITS), 0)
    unit = lax.broadcasted_iota(jnp.int32, (8, UNITS), 1) - (here.index % 16) * 24
    shifted = jnp.zeros((8, UNITS), f32)
    own_bias = fc1_bias[...].astype(f32)
    for j in range(24):
        shifted = jnp.where(unit == j, own_bias[:, j : j + 1], shifted)
    held[0, :, D : D + UNITS] = jnp.where(line == here.index // 16, shifted, 0.0)
    sums = SmallSum(here, held, arrived, sum_send, sum_recv)

    greet(here)

    def tok_copy(way, k):
        lanes = pl.ds(k * 384, 384)
        src = rows.at[far, :, lanes] if way == 2 else tokens.at[:, lanes]
        dst = rows.at[far if way == 2 else head, :, lanes]
        device = here.along("y", 2) if way == 1 else here.partner()
        return remote(src, dst, tok_send.at[way, k], tok_recv.at[way, k], device)

    half_copy = remote(
        own_half.at[:, :, pl.ds(pl.multiple_of((1 - core) * UNITS, UNITS), UNITS)],
        their_half, half_sem.at[0], half_sem.at[1], here.partner(),
    )
    half_copy.start()
    sums.start(0)
    sums.finish(0)
    sums.start(1)

    half_copy.wait_recv()
    mine = pl.ds(pl.multiple_of(core * 24, 8), 24)
    theirs = pl.ds(pl.multiple_of((1 - core) * 24, 8), 24)
    for kind in (0, 1):
        chip_block[kind, mine, :] = own_half[kind, :, pl.ds(pl.multiple_of(core * UNITS, UNITS), UNITS)]
        chip_block[kind, theirs, :] = their_half[kind]
    for part in range(3):
        for kind in (0, 1):
            block[part, kind * 48 : kind * 48 + 48, :] = chip_block[
                kind, :, part * 128 : part * 128 + 128
            ].astype(bf16)

    slots = {axis: slot_of(axis, at[axis]) for axis in RING}
    ours = pl.ds(core * 3, 3)
    block_copy = pltpu.make_async_copy(block, gathered.at[(ours,) + region(slots)], local_sem.at[0])

    def ff_copy(kind, phase, step):
        order = GATHER[kind]
        of_kind = pl.ds(kind * 48, 48)
        spot = gathered.at[(ours,) + region({a: slots[a] for a in order[phase:]}) + (of_kind,)]
        return remote(
            block.at[:, of_kind] if phase == 0 else spot, spot,
            ff_send.at[kind, phase, step - 1], ff_recv.at[kind, phase, step - 1],
            here.along(order[phase], step),
        )

    def pass_copy(kind, step):
        last = GATHER[kind][2]
        of_kind = pl.ds(kind * 48, 48)
        plane = region({last: slot_of(last, (at[last] + 4 - step) % 4)})
        spot = gathered.at[(ours,) + plane + (of_kind,)]
        return remote(spot, spot, fwd_send.at[kind, step], fwd_recv.at[kind, step], here.partner())

    def onward_copy(kind, way):
        last = GATHER[kind][2]
        from_slot = slot_of(last, (at[last] + (3 if way == 0 else 1)) % 4)
        plane = region({last: from_slot, "y": pl.ds(2 * way, 2)})
        spot = gathered.at[(ours,) + plane + (pl.ds(kind * 48, 48),)]
        return remote(
            spot, spot, on_send.at[kind, way], on_recv.at[kind, way],
            here.along(last, 1 if way == 0 else 3),
        )

    def ff_start(phase):
        for step in (1, 3) if phase == 2 else (1, 3, 2):
            for kind in (0, 1):
                ff_copy(kind, phase, step).start()

    def ff_on(phase):
        for step in (1, 2, 3):
            for kind in (0, 1):
                ff_copy(kind, phase, step).wait_recv()
        ff_start(phase + 1)

    ff_start(0)
    block_copy.start()
    for way in (1, 0):
        for k in (0, 1):
            tok_copy(way, k).start()

    last_rows = pl.ds(384, 192)

    def out_copy(way, k):
        own = (w_out, w_qkv.at[last_rows])[k]
        every = (w_out_all, w_last_all)[k]
        src = every.at[far] if way == 2 else own
        dst = every.at[far if way == 2 else head]
        device = here.along("y", 2) if way == 1 else here.partner()
        return remote(src, dst, out_send.at[way, k], out_recv.at[way, k], device)

    for k in (0, 1):
        out_copy(0, k).start()
    w_out_all[head] = w_out[...]
    w_last_all[head] = w_qkv[384:576, :]
    rows[head] = tokens[...]
    sums.finish(1)
    sums.start(2)
    block_copy.wait()
    ff_on(0)
    sums.finish(2)
    sums.start(3)
    for k in (0, 1):
        tok_copy(0, k).wait_recv()
    params[...] = sums.finish(3)

    gain = params[GAIN1 : GAIN1 + 1, 0:D]
    shift = params[SHIFT1 : SHIFT1 + 1, 0:D]
    mask_token = params[MASK : MASK + 1, 0:D]
    biases = qv_bias[...].astype(f32)
    q_bias = biases[0:1, :]
    v_bias = biases[1:2, :]

    def project(half):
        parts = []
        for j in range(2):
            which = half * 2 + j
            masked = row_mask(cubes, which)
            start = jnp.where(masked > 0.5, mask_token, rows[which].astype(f32))
            unit1, _ = unit_of(start)
            parts.append(unit1 * gain + shift)
        normed[half] = jnp.concatenate(parts, axis=0).astype(bf16)

        to = pl.ds(pl.multiple_of(half * 784, 16), 784)
        for h in range(HEADS_HERE):
            packed = dot_nt(normed[half], w_qkv[h * 192 : h * 192 + 192, :])
            lanes = slice(h * 64, h * 64 + 64)
            query = packed[:, 0:64] + q_bias[:, lanes]
            value = packed[:, 128:192] + v_bias[:, lanes]
            qkv[h * 3, to, :] = query.astype(bf16) * bf16(0.125)
            qkv[h * 3 + 1, to, :] = packed[:, 64:128].astype(bf16)
            qkv[h * 3 + 2, to, :] = value.astype(bf16)

    chip_half = head // 2
    project(chip_half)
    ff_on(1)
    for kind in (0, 1):
        pass_copy(kind, 0).start()
    for k in (0, 1):
        tok_copy(1, k).wait_recv()
        tok_copy(2, k).start()
    for k in (0, 1):
        out_copy(1, k).start()
    for k in (0, 1):
        tok_copy(2, k).wait_recv()
    project(1 - chip_half)
    early = [
        pltpu.make_async_copy(normed, normed_out, local_sem.at[1]),
        pltpu.make_async_copy(qkv, qkv_out, local_sem.at[2]),
    ]
    for copy in early:
        copy.start()

    ones_row = (lax.broadcasted_iota(jnp.int32, (16, TOK), 0) == 0).astype(f32)
    for h in range(HEADS_HERE):
        values_t[h] = jnp.concatenate([qkv[h * 3 + 2].astype(f32).T, ones_row], axis=0).astype(bf16)

    def mix_copy(k, way):
        other, device = (
            (mate, here.partner()), (far, here.along("y", 2)), (far_mate, here.across()),
        )[way]
        src, dst = ((pair_out, pair_in), (last_out, last_in))[k]
        return remote(src.at[other], dst.at[head], mix_send.at[k, way], mix_recv.at[k, way], device)

    def mix_start(k):
        for j in range(4):
            own = slice(j * ROWS, j * ROWS + ROWS)
            if k == 0:
                pair_out[j] = jnp.concatenate([mixed[0, own, :], mixed[1, own, :]], axis=1).astype(bf16)
            else:
                last_out[j] = mixed[2, own, :].astype(bf16)
        for way in (1, 2, 0):
            mix_copy(k, way).start()
        if k == 0:
            pair_in[head] = pair_out[head]
        else:
            last_in[head] = last_out[head]

    def ff_onward():
        for way, step in enumerate((1, 3)):
            for kind in (0, 1):
                ff_copy(kind, 2, step).wait_recv()
                onward_copy(kind, way).start()
        for step in (1, 3):
            for kind in (0, 1):
                pass_copy(kind, step).start()

    def out_on():
        for k in (0, 1):
            out_copy(1, k).wait_recv()
            out_copy(2, k).start()

    def attend(h, carry):
        def score(k):
            scores = dot_nt(qkv[h * 3 + 1], qkv[h * 3, k * QCHUNK : k * QCHUNK + QCHUNK, :])
            return scores, jnp.max(scores, axis=0, keepdims=True)

        ready = score(0)
        for k in range(CHUNKS):
            scores, top = ready
            if k + 1 < CHUNKS:
                ready = score(k + 1)
            weights = jnp.exp(scores - top).astype(bf16)
            outcome = dot_nn(values_t[h], weights)
            total = outcome[64:65, :]
            mixed[h, k * QCHUNK : k * QCHUNK + QCHUNK, :] = (outcome[0:64, :] / total).T
            lse[h * CHUNKS + k] = jnp.broadcast_to(top + jnp.log(total), (8, QCHUNK))
        pl.when(h == 0)(ff_onward)

        @pl.when(h == 1)
        def _():
            mix_start(0)
            out_on()

        return carry

    lax.fori_loop(0, HEADS_HERE, attend, 0)

    mix_start(1)
    for kind in (0, 1):
        for way in (0, 1):
            onward_copy(kind, way).wait_recv()
        pass_copy(kind, 2).start()
    for k in (0, 1):
        out_copy(0, k).wait_recv()
        out_copy(2, k).wait_recv()
    late = [
        pltpu.make_async_copy(lse, lse_out, local_sem.at[3]),
        pltpu.make_async_copy(mixed, mixed_keep, local_sem.at[4]),
        pltpu.make_async_copy(pair_out, pair_keep, local_sem.at[5]),
        pltpu.make_async_copy(last_out, last_keep, local_sem.at[9]),
        pltpu.make_async_copy(w_out_all, w_out_all_out, local_sem.at[6]),
        pltpu.make_async_copy(w_last_all, w_last_all_out, local_sem.at[8]),
    ]
    for copy in late:
        copy.start()
    for kind in (0, 1):
        for step in range(4):
            pass_copy(kind, step).wait_recv()
    for k in (0, 1):
        for way in range(3):
            mix_copy(k, way).wait_recv()
    last_copies = [
        pltpu.make_async_copy(pair_in, pair_in_out, local_sem.at[7]),
        pltpu.make_async_copy(last_in, last_in_out, local_sem.at[10]),
    ]
    for copy in last_copies:
        copy.start()
    sums.drain()
    half_copy.wait_send()
    for way in range(3):
        for k in (0, 1):
            out_copy(way, k).wait_send()
            tok_copy(way, k).wait_send()
        for k in (0, 1):
            mix_copy(k, way).wait_send()
    for kind in (0, 1):
        for phase in range(3):
            for step in (1, 3) if phase == 2 else (1, 2, 3):
                ff_copy(kind, phase, step).wait_send()
        for way in (0, 1):
            onward_copy(kind, way).wait_send()
        for step in range(4):
            pass_copy(kind, step).wait_send()
    for copy in early + late + last_copies:
        copy.wait()


VM = pl.BlockSpec(memory_space=pltpu.VMEM)
ANY = pl.BlockSpec(memory_space=pl.ANY)
DMA = pltpu.SemaphoreType.DMA


def shape(dims, kind=bf16):
    return jax.ShapeDtypeStruct(dims, kind)


def forward_call(*args):
    kept = (
        ((2, 784, D), bf16),
        ((9, TOK, 64), bf16),
        ((HEADS_HERE * CHUNKS, 8, QCHUNK), f32),
        ((HEADS_HERE, TOK, 64), f32),
        ((4, ROWS, 128), bf16),
        ((4, ROWS, 64), bf16),
        ((4, ROWS, 128), bf16),
        ((4, ROWS, 64), bf16),
        ((4, 192, D), bf16),
        ((4, 192, D), bf16),
    )
    return pl.pallas_call(
        forward_kernel,
        out_shape=(shape((8, D + UNITS), f32),)
        + tuple(shape(*k) for k in kept)
        + (shape((6, 4, 4, 4, 96, 128)),),
        in_specs=[VM] * 9,
        out_specs=(VM,) + (ANY,) * 11,
        scratch_shapes=[pltpu.VMEM(*k) for k in kept]
        + [
            pltpu.VMEM((4, ROWS, D), bf16),
            pltpu.VMEM((4, 8, D + UNITS), f32),
            pltpu.VMEM((10, 8, D + UNITS), f32),
            pltpu.VMEM((2, 24, D), f32),
            pltpu.VMEM((2, 24, UNITS), f32),
            pltpu.VMEM((2, 48, UNITS), f32),
            pltpu.VMEM((3, 96, 128), bf16),
            pltpu.VMEM((HEADS_HERE, 80, TOK), bf16),
            DMA((3, 2)), DMA((3, 2)), DMA((10,)), DMA((10,)), DMA((2,)),
            DMA((2, 3, 3)), DMA((2, 3, 3)), DMA((2, 4)), DMA((2, 4)),
            DMA((3, 2)), DMA((3, 2)), DMA((2, 3)), DMA((2, 3)), DMA((11,)), DMA((2, 2)), DMA((2, 2)),
        ],
        name="attention_forward",
        compiler_params=pltpu.CompilerParams(
            collective_id=0, has_side_effects=True, vmem_limit_bytes=VMEM_LIMIT
        ),
    )(*args)


SQRT_HALF = 0.7071067811865476
INV_SQRT_2PI = 0.3989422804014327


def feed_forward_kernel(
    cubes, params, tokens, cotangent, pair_in, last_in, w_out_all, weights,
    block_out, grad_middle, grad_branch, grad_pair, grad_last, small_grads, reduced_out,
    held, grads, arrived, reduced, normed2, outer, grad_normed2,
    load_sem, pair_send, pair_recv, keep_sem,
):
    here = Place()
    core, head = here.core, here.head

    def load(b):
        chips = pl.ds(b * 16, 16)
        return pltpu.make_async_copy(weights.at[:, chips], held.at[:, chips], load_sem.at[b])

    for b in range(BLOCKS):
        load(b).start()
    barrier = pltpu.get_barrier_semaphore()
    pl.semaphore_signal(barrier, inc=1, device_id=here.partner(), device_id_type=MESH)

    masked = row_mask(cubes, head)
    start = jnp.where(masked > 0.5, params[MASK : MASK + 1, 0:D], tokens[...].astype(f32))
    branch = jnp.zeros((ROWS, D), f32)
    for j in range(4):
        some = jnp.concatenate([pair_in[j], last_in[j]], axis=1)
        branch = branch + dot_nn(some, w_out_all[j])
    middle = start + branch + params[PROJ : PROJ + 1, 0:D]
    gain2 = params[GAIN2 : GAIN2 + 1, 0:D]
    unit2, _ = unit_of(middle)
    normed2[...] = (unit2 * gain2 + params[SHIFT2 : SHIFT2 + 1, 0:D]).astype(bf16)
    block_out[...] = middle
    outer[...] = jnp.zeros((ROWS, D), f32)
    grad_normed2[...] = jnp.zeros((ROWS, D), f32)
    pl.semaphore_wait(barrier, 1)
    mates = pl.ds((1 - core) * 3, 3)

    def pair_copy(b):
        chips = pl.ds(b * 16, 16)
        return remote(
            grads.at[mates, chips], arrived.at[:, chips], pair_send.at[b], pair_recv.at[b], here.partner()
        )

    def keep_copy(b):
        chips = pl.ds(b * 16, 16)
        return pltpu.make_async_copy(reduced.at[:, chips], reduced_out.at[:, chips], keep_sem.at[b])

    def add_pair(b):
        chips = pl.ds(b * 16, 16)
        pair_copy(b).wait_recv()
        for part in range(3):
            reduced[part, chips] = (
                grads[core * 3 + part, chips].astype(f32) + arrived[part, chips].astype(f32)
            ).astype(bf16)
        keep_copy(b).start()

    def some_units(b, carry):
        load(b).wait()
        chips = pl.ds(b * 16, 16)

        def weight(kind):
            return jnp.concatenate(
                [
                    held[s, chips, kind * 48 : kind * 48 + 48, :].reshape(2 * UNITS, 128)
                    for s in range(6)
                ],
                axis=1,
            )

        def keep(kind, grad):
            grad = grad.astype(bf16)
            for s in range(6):
                grads[s, chips, kind * 48 : kind * 48 + 48, :] = grad[
                    :, s * 128 : s * 128 + 128
                ].reshape(16, 48, 128)

        bias = jnp.concatenate(
            [params[pl.ds(2 * b + k, 1), D : D + UNITS] for k in (0, 1)], axis=1
        )
        inner = dot_nt(normed2[...], weight(0)) + bias
        below = 0.5 + 0.5 * lax.erf(inner * SQRT_HALF)
        active = (inner * below).astype(bf16)
        slope = below + inner * (INV_SQRT_2PI * jnp.exp(-0.5 * inner * inner))
        grad_active = dot_nt(cotangent[...], weight(1))
        grad_inner = (grad_active * slope).astype(bf16)
        bias_grad = jnp.sum(grad_inner.astype(f32), axis=0, keepdims=True)
        for k in (0, 1):
            small_grads[pl.ds(2 * b + k, 1), D : D + UNITS] = bias_grad[:, k * UNITS : k * UNITS + UNITS]
        outer[...] += dot_nn(active, weight(1))
        grad_normed2[...] += dot_nn(grad_inner, weight(0))
        keep(1, dot_tn(active, cotangent[...]))
        keep(0, dot_tn(grad_inner, normed2[...]))
        pair_copy(b).start()

        @pl.when(b > 0)
        def _():
            add_pair(b - 1)

        return carry

    lax.fori_loop(0, BLOCKS, some_units, 0)

    middle = block_out[...]
    block_out[...] = middle + outer[...] + params[FC2B : FC2B + 1, 0:D]
    unit2, inverse2 = unit_of(middle)
    grad_out = cotangent[...].astype(f32)
    back = grad_normed2[...]
    grad_mid = grad_out + unit_back(back * gain2, unit2, inverse2)
    grad_middle[...] = grad_mid
    low = grad_mid.astype(bf16)
    grad_branch[...] = low
    for j in range(4):
        some = dot_nt(low, w_out_all[j]).astype(bf16)
        grad_pair[j] = some[:, 0:128]
        grad_last[j] = some[:, 128:192]
    sums = [
        jnp.sum(v, axis=0, keepdims=True)
        for v in (grad_mid, back * unit2, back, grad_out)
    ]
    small_grads[:, 0:D] = jnp.concatenate(sums + [jnp.zeros((4, D), f32)], axis=0)
    add_pair(BLOCKS - 1)
    for b in range(BLOCKS):
        pair_copy(b).wait_send()
        keep_copy(b).wait()


def feed_forward_call(*args):
    return pl.pallas_call(
        feed_forward_kernel,
        out_shape=(
            shape((ROWS, D), f32),
            shape((ROWS, D), f32),
            shape((ROWS, D)),
            shape((4, ROWS, 128)),
            shape((4, ROWS, 64)),
            shape((8, D + UNITS), f32),
            shape((3, 64, 96, 128)),
        ),
        in_specs=[VM] * 7 + [ANY],
        out_specs=(VM,) * 6 + (ANY,),
        scratch_shapes=[
            pltpu.VMEM((6, 64, 96, 128), bf16),
            pltpu.VMEM((6, 64, 96, 128), bf16),
            pltpu.VMEM((3, 64, 96, 128), bf16),
            pltpu.VMEM((3, 64, 96, 128), bf16),
            pltpu.VMEM((ROWS, D), bf16),
            pltpu.VMEM((ROWS, D), f32),
            pltpu.VMEM((ROWS, D), f32),
            DMA((BLOCKS,)), DMA((BLOCKS,)), DMA((BLOCKS,)), DMA((BLOCKS,)),
        ],
        name="feed_forward",
        compiler_params=pltpu.CompilerParams(
            collective_id=1, has_side_effects=True, vmem_limit_bytes=VMEM_LIMIT
        ),
    )(*args)


def without(axes, axis):
    return tuple(a for a in axes if a != axis)


def backward_kernel(
    cubes, params, grad_pair, grad_last, grad_branch, small_grads, reduced,
    grad_middle_in, tokens_in, normed_in, qkv_in, lse_in, mixed_in, pair_in_, last_in_, w_qkv_in, w_last_in,
    tokens_grad, small_first, small_last, w_grads, w_fc1_grad, w_fc2_grad,
    grad_middle, tokens, normed, qkv, lse, mixed, mixed_pair, mixed_last, w_qkv, w_last, own_reduced,
    pair_back, last_back, mixed_wide, outer_back, queries, keys_t, grad_q, grad_kv, packed_back,
    branch_in, input_back, pair_out, pair_in, far_out, far_in,
    held, arrived, held_last, arrived_last,
    ff_in0, ff_sum1, ff_in1, ff_sum2, ff_in2, ff_last, ff_mate,
    w_src, w_in, w_z, w_z_in, w_y, w_y_in, w_all, column_sums,
    mix_send, mix_recv, br_send, br_recv, in_send, in_recv, sum_send, sum_recv, last_send, last_recv,
    ff_send, ff_recv, mate_sem, wx_send, wx_recv, wz_send, wz_recv, wy_send, wy_recv, wg_send, wg_recv,
    load_sem, last_out, last_in, head_send, head_recv,
):
    here = Place()
    core, head, at = here.core, here.head, here.at
    mate = head + 1 - 2 * core
    far = (head + 2) % 4
    far_mate = far + 1 - 2 * core
    slots = {axis: slot_of(axis, at[axis]) for axis in RING}

    def own_share(kind):
        axis = REDUCE[kind][0]
        return reduced.at[(slice(None),) + region({axis: slots[axis]}) + (pl.ds(kind * 48, 48),)]

    pairs = (
        (qkv_in, qkv), (lse_in, lse), (mixed_in, mixed), (tokens_in, tokens), (w_qkv_in, w_qkv),
        (normed_in, normed), (pair_in_, mixed_pair), (grad_middle_in, grad_middle),
        (own_share(0), own_reduced.at[0]), (own_share(1), own_reduced.at[1]), (w_last_in, w_last),
        (last_in_, mixed_last),
    )
    loads = [pltpu.make_async_copy(src, dst, load_sem.at[k]) for k, (src, dst) in enumerate(pairs)]
    for copy in loads:
        copy.start()
    greet(here)

    def mix_copy(k, way):
        other, device = (
            (mate, here.partner()), (far, here.along("y", 2)), (far_mate, here.across()),
        )[way]
        src, dst = ((grad_pair, pair_back), (grad_last, last_back))[k]
        return remote(src.at[other], dst.at[head], mix_send.at[k, way], mix_recv.at[k, way], device)

    for k in (0, 1):
        for way in (1, 2, 0):
            mix_copy(k, way).start()

    def peer_slot(axis, step):
        return slot_of(axis, (at[axis] + step) % 4)

    def ff_left(kind, phase):
        left = ("x", "z", "y")
        for done in REDUCE[kind][:phase]:
            left = without(left, done)
        return left

    def ff_copy(kind, phase, step):
        axis = REDUCE[kind][phase]
        where = tuple(
            peer_slot(axis, step) if a == axis else slice(None) for a in ff_left(kind, phase)
        )
        where = (slice(None),) + where
        if phase == 0:
            src = reduced.at[where + (pl.ds(kind * 48, 48),)]
        else:
            src = (ff_sum1, ff_sum2)[phase - 1].at[(kind,) + where]
        dst = (ff_in0, ff_in1, ff_in2)[phase]
        return remote(
            src, dst.at[kind, step - 1],
            ff_send.at[kind, phase, step - 1], ff_recv.at[kind, phase, step - 1],
            here.along(axis, step),
        )

    def ff_start(kind, phase):
        for step in (1, 2, 3):
            ff_copy(kind, phase, step).start()

    def ff_add(kind, phase):
        axis = REDUCE[kind][phase]
        where = tuple(slots[axis] if a == axis else slice(None) for a in ff_left(kind, phase))
        arrived_in = (ff_in0, ff_in1, ff_in2)[phase]
        for step in (1, 2, 3):
            ff_copy(kind, phase, step).wait_recv()
        if phase == 0:
            loads[8 + kind].wait()

        def some(part):
            if phase == 0:
                own = own_reduced[kind, part]
            else:
                own = (ff_sum1, ff_sum2)[phase - 1][(kind, part) + where]
            return ring_total(
                own.astype(f32), *[arrived_in[kind, k, part].astype(f32) for k in range(3)]
            )

        if phase == 0:
            @pl.loop(0, 3)
            def _(part):
                ff_sum1[kind, part] = some(part).astype(bf16)
        else:
            for part in range(3):
                total = some(part)
                if phase == 1:
                    ff_sum2[kind, part] = total.astype(bf16)
                else:
                    ff_last[kind, :, part * 128 : part * 128 + 128] = total

    for kind in (0, 1):
        ff_start(kind, 0)

    held[0] = small_grads[...]
    sums = SmallSum(here, held, arrived, sum_send, sum_recv)
    sums.start(0)

    beside = dict(at)
    beside["y"] = at["y"] + 1 - 2 * (at["y"] % 2)
    beside = here.device(beside, core)

    def first_axis(n):
        return "xz"[n % 2]

    def wx_copy(n, step):
        axis = first_axis(n)
        return remote(
            w_src.at[n, (at[axis] + step) % 4], w_in.at[n, step - 1],
            wx_send.at[n, step - 1], wx_recv.at[n, step - 1], here.along(axis, step),
        )

    def wz_copy(n, step):
        return remote(
            w_z.at[n], w_z_in.at[n, step - 1], wz_send.at[n, step - 1], wz_recv.at[n, step - 1],
            here.along(first_axis(n + 1), step),
        )

    def wy_copy(n):
        return remote(w_y.at[n], w_y_in.at[n], wy_send.at[n], wy_recv.at[n], beside)

    def wg_copy(n, step):
        axis = first_axis(n)
        spot = w_all.at[n, at[axis]]
        return remote(
            spot, spot, wg_send.at[n, step - 1], wg_recv.at[n, step - 1], here.along(axis, step)
        )

    def w_begin(n, grad):
        grad = grad.astype(bf16)
        for s in range(6):
            lanes = slice(s * 128, s * 128 + 128)
            first = s * 192
            for chunk in range(4):
                low, high = max(first, chunk * 288), min(first + 192, chunk * 288 + 288)
                if low < high:
                    w_src[n, chunk, low - chunk * 288 : high - chunk * 288, :] = grad[
                        low - first : high - first, lanes
                    ]
        for step in (1, 2, 3):
            wx_copy(n, step).start()

    def w_second(n):
        for step in (1, 2, 3):
            wx_copy(n, step).wait_recv()
        w_z[n] = ring_total(
            w_src[n, at[first_axis(n)]].astype(f32), *[w_in[n, k].astype(f32) for k in range(3)]
        ).astype(bf16)
        for step in (1, 2, 3):
            wz_copy(n, step).start()

    def w_third(n):
        for step in (1, 2, 3):
            wz_copy(n, step).wait_recv()
        w_y[n] = ring_total(
            w_z[n].astype(f32), *[w_z_in[n, k].astype(f32) for k in range(3)]
        ).astype(bf16)
        wy_copy(n).start()

    def w_fourth(n):
        wy_copy(n).wait_recv()
        w_all[n, at[first_axis(n)]] = (w_y[n].astype(f32) + w_y_in[n].astype(f32)).astype(bf16)
        for step in (1, 2, 3):
            wg_copy(n, step).start()

    def w_end(n):
        for step in (1, 2, 3):
            wg_copy(n, step).wait_recv()
        w_grads[n] = w_all[n]

    br_near = remote(grad_branch, branch_in.at[head], br_send.at[0], br_recv.at[0], here.partner())
    br_far = remote(grad_branch, branch_in.at[head], br_send.at[1], br_recv.at[1], here.along("y", 2))
    br_pass = remote(branch_in.at[far], branch_in.at[far], br_send.at[2], br_recv.at[2], here.partner())
    branch_in[head] = grad_branch[...]
    pair_back[head] = grad_pair[head]
    last_back[head] = grad_last[head]

    zeros = jnp.zeros((TOK, 64), bf16)
    loads[0].wait()
    for h in range(HEADS_HERE):
        query = qkv[h * 3]
        queries[h] = jnp.concatenate([zeros, query], axis=1)
        keys_t[h] = qkv[h * 3 + 1].astype(f32).T.astype(bf16)

    def outer_in(h):
        if h != 1:
            for way in range(3):
                mix_copy(h // 2, way).wait_recv()
        for j in range(4):
            block = last_back[j] if h == 2 else pair_back[j]
            lanes = slice(64, 128) if h == 1 else slice(0, 64)
            mixed_wide[j * ROWS : j * ROWS + ROWS, :] = block.astype(f32)[:, lanes]
        outer_back[h] = jnp.concatenate([mixed_wide[...].astype(bf16), zeros], axis=1)

    outer_in(0)
    br_far.start()
    br_near.start()
    for k in (1, 2, 3, 4, 5, 6, 7, 11):
        loads[k].wait()

    def branch_on():
        br_far.wait_recv()
        br_pass.start()

    def branch_end():
        br_near.wait_recv()
        br_pass.wait_recv()
        grad = jnp.zeros((192, D), f32)
        for j in range(4):
            some = jnp.concatenate([mixed_pair[j], mixed_last[j]], axis=1)
            grad = grad + dot_tn(some, branch_in[j])
        w_begin(0, grad)

    def sum_on(phase):
        total = sums.finish(phase)
        if phase < 3:
            sums.start(phase + 1)
        else:
            small_first[...] = total

    def ff_on(phase):
        for kind in (0, 1):
            ff_add(kind, phase)
            if phase < 2:
                ff_start(kind, phase + 1)

    chip = head // 2
    lane = lax.broadcasted_iota(jnp.int32, (TOK, 128), 1)

    def attend(h, carry):
        def score(k):
            chunk = slice(k * QCHUNK, k * QCHUNK + QCHUNK)
            scores = dot_nt(qkv[h * 3 + 1], qkv[h * 3, chunk, :])
            return scores, dot_nt(qkv[h * 3 + 2], outer_back[h, chunk, 0:64])

        ready = score(0)
        for k in range(CHUNKS):
            chunk = slice(k * QCHUNK, k * QCHUNK + QCHUNK)
            scores, grad_weights = ready
            if k + 1 < CHUNKS:
                ready = score(k + 1)
            given = outer_back[h, chunk, :]
            weights = jnp.exp(scores - lse[h * CHUNKS + k, 0:1, :])
            delta = jnp.sum(
                (given[:, 0:64].astype(f32) * mixed[h, chunk, :]).T, axis=0, keepdims=True
            )
            grad_scores = (weights * (grad_weights - delta)).astype(bf16)
            share = dot_nn(weights.astype(bf16), given) + dot_nn(grad_scores, queries[h, chunk, :])
            if k == 0:
                grad_kv[...] = share
            else:
                grad_kv[...] += share
            grad_q[chunk, 0:64] = dot_nn(keys_t[h], grad_scores).T * 0.125

        both = grad_kv[...]
        first = jnp.where(lane < 64, grad_q[...], both)
        packed_back[:, 0:128] = first.astype(bf16)
        packed_back[:, 128:192] = both[:, 0:64].astype(bf16)
        @pl.when(h < HEADS_HERE - 1)
        def _():
            for k, half in enumerate((1 - chip, chip)):
                share = dot_nn(
                    packed_back[pl.ds(pl.multiple_of(half * 784, 16), 784), :],
                    w_qkv[pl.ds(pl.multiple_of(h * 192, 16), 192), :],
                )
                for j in (0, 1):
                    some = share[j * ROWS : j * ROWS + ROWS]

                    @pl.when(h == 0)
                    def _():
                        input_back[half, j] = some

                    @pl.when(h > 0)
                    def _():
                        input_back[half, j] += some

                pl.when(h == HEADS_HERE - 2)(partial(pair_start, k, half))

        @pl.when(h == HEADS_HERE - 1)
        def _():
            for j in range(4):
                own = slice(j * ROWS, j * ROWS + ROWS)
                last_out[j] = jnp.concatenate([first[own], both[own, 0:64]], axis=1).astype(bf16)
            for way in (1, 2, 0):
                head_copy(way).start()

        column_sums[pl.ds(h, 1), :] = jnp.sum(packed_back[...].astype(f32), axis=0, keepdims=True)
        w_grad = dot_tn(packed_back[...], normed[...])
        for n in range(HEADS_HERE):
            pl.when(h == n)(partial(w_begin, n + 1, w_grad))

        @pl.when(h == 0)
        def _():
            outer_in(1)
            sum_on(0)

        @pl.when(h == 1)
        def _():
            outer_in(2)
            sum_on(1)
            branch_on()
            pair_copies[0].wait_recv()
            far_out[...] = (input_back[1 - chip, core] + pair_in[0].astype(f32)).astype(bf16)
            far_copy.start()

        return carry

    pair_copies = [
        remote(pair_out.at[k], pair_in.at[k], in_send.at[k], in_recv.at[k], here.partner()) for k in (0, 1)
    ]
    far_copy = remote(far_out, far_in, in_send.at[2], in_recv.at[2], here.along("y", 2))

    def head_copy(way):
        other, device = (
            (mate, here.partner()), (far, here.along("y", 2)), (far_mate, here.across()),
        )[way]
        return remote(last_out.at[other], last_in.at[head], head_send.at[way], head_recv.at[way], device)

    def pair_start(k, half):
        pair_out[k] = input_back[half, 1 - core].astype(bf16)
        pair_copies[k].start()

    lax.fori_loop(0, HEADS_HERE, attend, 0)

    branch_end()
    w_second(1)
    w_second(2)
    ff_on(0)
    sum_on(2)
    w_second(3)
    w_third(1)
    w_third(2)
    w_second(0)
    sum_on(3)

    masked = row_mask(cubes, head)
    start = jnp.where(masked > 0.5, params[MASK : MASK + 1, 0:D], tokens[...].astype(f32))
    unit1, inverse1 = unit_of(start)
    pair_copies[1].wait_recv()
    far_copy.wait_recv()
    last_in[head] = last_out[head]
    loads[10].wait()
    back = input_back[chip, core] + pair_in[1].astype(f32) + far_in[...].astype(f32)
    for way in range(3):
        head_copy(way).wait_recv()
    for j in range(4):
        back = back + dot_nn(last_in[j], w_last[j])
    grad_start = grad_middle[...] + unit_back(
        back * params[GAIN1 : GAIN1 + 1, 0:D], unit1, inverse1
    )
    tokens_grad[...] = jnp.where(masked > 0.5, 0.0, grad_start)
    totals = [
        jnp.sum(v, axis=0, keepdims=True)
        for v in (back * unit1, back, jnp.where(masked > 0.5, grad_start, 0.0))
    ]
    held_last[0, :, 0:384] = jnp.concatenate(
        [v[:, k * 384 : k * 384 + 384] for v in totals for k in (0, 1)] + [jnp.zeros((2, 384), f32)],
        axis=0,
    )
    line = lax.broadcasted_iota(jnp.int32, (8, 192), 0)
    of_query = jnp.concatenate([column_sums[h : h + 1, 0:64] for h in range(HEADS_HERE)], axis=1)
    of_value = jnp.concatenate([column_sums[h : h + 1, 128:192] for h in range(HEADS_HERE)], axis=1)
    held_last[0, :, 384:576] = jnp.where(
        line == 2 * head, of_query, jnp.where(line == 2 * head + 1, of_value, 0.0)
    )
    held_last[0, :, 576:640] = jnp.zeros((8, 64), f32)
    last = SmallSum(here, held_last, arrived_last, last_send, last_recv)
    last.start(0)
    w_third(3)
    last.finish(0)
    last.start(1)
    w_third(0)
    w_fourth(1)
    w_fourth(2)
    ff_on(1)
    last.finish(1)
    last.start(2)
    w_fourth(3)
    w_fourth(0)
    ff_on(2)
    mate_copy = remote(
        ff_last.at[:, pl.ds(pl.multiple_of((1 - core) * 24, 8), 24), :], ff_mate,
        mate_sem.at[0], mate_sem.at[1], here.partner(),
    )
    mate_copy.start()
    last.finish(2)
    last.start(3)
    w_end(1)
    w_end(2)
    w_end(3)
    mate_copy.wait_recv()
    for kind, target in ((0, w_fc1_grad), (1, w_fc2_grad)):
        target[:, pl.ds(pl.multiple_of(core * UNITS, UNITS), UNITS)] = ff_last[
            kind, pl.ds(pl.multiple_of(core * 24, 8), 24), :
        ]
        target[:, pl.ds(pl.multiple_of((1 - core) * UNITS, UNITS), UNITS)] = ff_mate[kind]
    w_end(0)
    small_last[...] = last.finish(3)

    sums.drain()
    last.drain()
    for copy in [br_near, br_far, br_pass, far_copy, mate_copy] + pair_copies:
        copy.wait_send()
    for way in range(3):
        head_copy(way).wait_send()
    for k in (0, 1):
        for way in range(3):
            mix_copy(k, way).wait_send()
    for kind in (0, 1):
        for phase in range(3):
            for step in (1, 2, 3):
                ff_copy(kind, phase, step).wait_send()
    for n in range(4):
        for step in (1, 2, 3):
            wx_copy(n, step).wait_send()
            wz_copy(n, step).wait_send()
            wg_copy(n, step).wait_send()
        wy_copy(n).wait_send()


def backward_call(*args):
    loaded = (
        ((ROWS, D), f32),
        ((ROWS, D), bf16),
        ((TOK, D), bf16),
        ((9, TOK, 64), bf16),
        ((HEADS_HERE * CHUNKS, 8, QCHUNK), f32),
        ((HEADS_HERE, TOK, 64), f32),
        ((4, ROWS, 128), bf16),
        ((4, ROWS, 64), bf16),
        ((576, D), bf16),
        ((4, 192, D), bf16),
    )
    return pl.pallas_call(
        backward_kernel,
        out_shape=(
            shape((ROWS, D), f32),
            shape((8, D + UNITS), f32),
            shape((8, 640), f32),
            shape((4, 4, 288, 128)),
            shape((24, D), f32),
            shape((24, D), f32),
        ),
        in_specs=[VM] * 6 + [ANY] * 11,
        out_specs=(VM,) * 6,
        scratch_shapes=[pltpu.VMEM(*k) for k in loaded]
        + [
            pltpu.VMEM((2, 3, 4, 4, 48, 128), bf16),
            pltpu.VMEM((4, ROWS, 128), bf16),
            pltpu.VMEM((4, ROWS, 64), bf16),
            pltpu.VMEM((TOK, 64), f32),
            pltpu.VMEM((HEADS_HERE, TOK, 128), bf16),
            pltpu.VMEM((HEADS_HERE, TOK, 128), bf16),
            pltpu.VMEM((HEADS_HERE, 64, TOK), bf16),
            pltpu.VMEM((TOK, 128), f32),
            pltpu.VMEM((TOK, 128), f32),
            pltpu.VMEM((TOK, 192), bf16),
            pltpu.VMEM((4, ROWS, D), bf16),
            pltpu.VMEM((2, 2, ROWS, D), f32),
            pltpu.VMEM((2, ROWS, D), bf16),
            pltpu.VMEM((2, ROWS, D), bf16),
            pltpu.VMEM((ROWS, D), bf16),
            pltpu.VMEM((ROWS, D), bf16),
            pltpu.VMEM((4, 8, D + UNITS), f32),
            pltpu.VMEM((10, 8, D + UNITS), f32),
            pltpu.VMEM((4, 8, 640), f32),
            pltpu.VMEM((10, 8, 640), f32),
            pltpu.VMEM((2, 3, 3, 4, 4, 48, 128), bf16),
            pltpu.VMEM((2, 3, 4, 4, 48, 128), bf16),
            pltpu.VMEM((2, 3, 3, 4, 48, 128), bf16),
            pltpu.VMEM((2, 3, 4, 48, 128), bf16),
            pltpu.VMEM((2, 3, 3, 48, 128), bf16),
            pltpu.VMEM((2, 48, UNITS), f32),
            pltpu.VMEM((2, 24, UNITS), f32),
            pltpu.VMEM((4, 4, 288, 128), bf16),
            pltpu.VMEM((4, 3, 288, 128), bf16),
            pltpu.VMEM((4, 288, 128), bf16),
            pltpu.VMEM((4, 3, 288, 128), bf16),
            pltpu.VMEM((4, 288, 128), bf16),
            pltpu.VMEM((4, 288, 128), bf16),
            pltpu.VMEM((4, 4, 288, 128), bf16),
            pltpu.VMEM((8, 192), f32),
            DMA((2, 3)), DMA((2, 3)), DMA((3,)), DMA((3,)), DMA((3,)), DMA((3,)),
            DMA((10,)), DMA((10,)), DMA((10,)), DMA((10,)),
            DMA((2, 3, 3)), DMA((2, 3, 3)), DMA((2,)),
            DMA((4, 3)), DMA((4, 3)), DMA((4, 3)), DMA((4, 3)), DMA((4,)), DMA((4,)), DMA((4, 3)), DMA((4, 3)),
            DMA((12,)),
            pltpu.VMEM((4, ROWS, 192), bf16),
            pltpu.VMEM((4, ROWS, 192), bf16),
            DMA((3,)), DMA((3,)),
        ],
        name="attention_backward",
        compiler_params=pltpu.CompilerParams(
            collective_id=2, has_side_effects=True, vmem_limit_bytes=VMEM_LIMIT
        ),
    )(*args)


def results_kernel(
    block_in, tokens_in, w_grads, w_fc1_in, w_fc2_in, first, last,
    block_out, tokens_grad, mask_grad, gain1_grad, shift1_grad, w_qkv_grad, qv_grad, w_out_grad,
    proj_grad, gain2_grad, shift2_grad, w_fc1_grad, fc1_grad, w_fc2_grad, fc2_grad,
):
    here = Place()
    pairs = (
        (block_in, block_out), (tokens_in, tokens_grad), (w_fc1_in, w_fc1_grad), (w_fc2_in, w_fc2_grad)
    )
    for src, dst in pairs:
        dst[...] = src[...]

    def pick(line, offset, count):
        column = lax.broadcasted_iota(jnp.int32, line.shape, 1) - offset
        spot = lax.broadcasted_iota(jnp.int32, (1, count), 1)
        out = jnp.zeros((1, count), f32)
        for j in range(count):
            one = jnp.sum(jnp.where(column == j, line, 0.0), axis=1, keepdims=True)
            out = jnp.where(spot == j, one, out)
        return out

    index = here.index
    for row, target in ((0, proj_grad), (1, gain2_grad), (2, shift2_grad), (3, fc2_grad)):
        target[...] = pick(first[row : row + 1, 0:D], index * 6, 6)
    fc1_grad[...] = pick(first[pl.ds(index // 16, 1), D : D + UNITS], (index % 16) * 24, 24)
    for k, target in enumerate((gain1_grad, shift1_grad, mask_grad)):
        target[...] = pick(last[pl.ds(2 * k + index // 64, 1), 0:384], (index % 64) * 6, 6)
    for k in (0, 1):
        qv_grad[k : k + 1, :] = last[pl.ds(2 * here.head + k, 1), 384:576]
    for n in range(4):
        for s in range(6):
            lanes = slice(s * 128, s * 128 + 128)
            start = s * 192
            for chunk in range(4):
                low, high = max(start, chunk * 288), min(start + 192, chunk * 288 + 288)
                if low < high:
                    got = w_grads[n, chunk, low - chunk * 288 : high - chunk * 288, :].astype(f32)
                    if n == 0:
                        w_out_grad[low - start : high - start, lanes] = got
                    else:
                        base = (n - 1) * 192 - start
                        w_qkv_grad[base + low : base + high, lanes] = got


def results_call(*args):
    six = shape((1, 6), f32)
    return pl.pallas_call(
        results_kernel,
        out_shape=(
            shape((ROWS, D), f32), shape((ROWS, D), f32), six, six, six, shape((576, D), f32),
            shape((2, 192), f32), shape((192, D), f32), six, six, six,
            shape((24, D), f32), shape((1, 24), f32), shape((24, D), f32), six,
        ),
        in_specs=[VM] * 7,
        out_specs=(VM,) * 15,
        name="results",
        compiler_params=pltpu.CompilerParams(vmem_limit_bytes=VMEM_LIMIT),
    )(*args)


def body(
    tokens, cube_mask, mask_token, norm1_gain, norm1_bias, w_qkv, qv_bias, w_out, proj_bias,
    norm2_gain, norm2_bias, w_fc1, fc1_bias, w_fc2, fc2_bias, cotangent,
):
    small = jnp.stack(
        [mask_token, norm1_gain, norm1_bias, proj_bias, norm2_gain, norm2_bias, fc2_bias, fc2_bias]
    )
    w_qkv_t = w_qkv.T
    (
        params, normed, qkv, lse, mixed, pair_out, last_out, pair_in, last_in, w_out_all, w_last_all, weights,
    ) = forward_call(
        small, fc1_bias[None], cube_mask, tokens, w_qkv_t, qv_bias, w_out, w_fc1.T, w_fc2,
    )
    block_out, grad_middle, grad_branch, grad_pair, grad_last, small_grads, reduced = feed_forward_call(
        cube_mask, params, tokens, cotangent, pair_in, last_in, w_out_all, weights.reshape(6, 64, 96, 128),
    )
    tokens_grad, small_first, small_last, w_grads, w_fc1_grad, w_fc2_grad = backward_call(
        cube_mask, params, grad_pair, grad_last, grad_branch, small_grads, reduced.reshape(3, 4, 4, 4, 96, 128),
        grad_middle, tokens, normed.reshape(TOK, D), qkv, lse, mixed, pair_out, last_out,
        w_qkv_t, w_last_all,
    )
    outs = list(
        results_call(block_out, tokens_grad, w_grads, w_fc1_grad, w_fc2_grad, small_first, small_last)
    )
    for k in (2, 3, 4, 8, 9, 10, 12, 14):
        outs[k] = outs[k].reshape(-1)
    outs[5] = outs[5].T
    outs[11] = outs[11].T
    return tuple(outs)


def solution(mesh):
    every = P(("clip", "head"))
    rows = P(("clip", "head"), None)
    columns = P(None, ("clip", "head"))
    in_specs = (
        rows, P("clip", None), every, every, every, P(None, "head"), P(None, "head"),
        P("head", None), every, every, every, columns, every, rows, every, rows,
    )
    out_specs = (
        rows, rows, every, every, every, P(None, "head"), P(None, "head"), P("head", None),
        every, every, every, columns, every, rows, every,
    )
    return jax.shard_map(body, mesh=mesh, in_specs=in_specs, out_specs=out_specs, check_vma=False)
```

```python
from functools import partial

import jax
import jax.numpy as jnp
import numpy as np
from jax import lax
from jax.experimental import pallas as pl
from jax.experimental.pallas import tpu as pltpu
from jax.sharding import PartitionSpec as P

HEAD_DIM = 64
GRID = 14
TOK = 1568
ROWS = 392
D = 768
HEADS_HERE = 3
QCHUNK = 224
CHUNKS = TOK // QCHUNK
UNITS = 384
BLOCKS = 4
epsilon = 1e-06
MESH = pl.DeviceIdType.MESH
VMEM_LIMIT = 60 * 2**20
f32 = jnp.float32
bf16 = jnp.bfloat16
GATHER = (("y", "x", "z"), ("y", "z", "x"))
REDUCE = (("x", "z", "y"), ("z", "x", "y"))
RING = ("x", "y", "z")


def dot_nn(left, right):
    return jnp.dot(left, right, preferred_element_type=f32)


def dot_nt(left, right):
    return lax.dot_general(left, right, (((1,), (1,)), ((), ())), preferred_element_type=f32)


def dot_tn(left, right):
    return lax.dot_general(left, right, (((0,), (0,)), ((), ())), preferred_element_type=f32)


def fold(values, start):
    return jnp.concatenate(
        [values[start : start + 200, 0:64], values[start + 192 : start + ROWS, 0:64]], axis=1
    ).astype(bf16)


def unfold(folded):
    wide = folded.astype(f32)
    return jnp.concatenate([wide[:, 0:64], wide[8:200, 64:128]], axis=0).astype(bf16)


class Place:
    def __init__(self):
        clip = lax.axis_index("clip")
        head = lax.axis_index("head")
        self.head = head
        self.index = clip * 4 + head
        self.at = {"x": clip // 8, "y": (head // 2) * 2 + clip % 2, "z": (clip // 2) % 4}
        self.core = head % 2

    def device(self, at, core):
        return {
            "clip": at["x"] * 8 + at["z"] * 2 + at["y"] % 2,
            "head": (at["y"] // 2) * 2 + core,
        }

    def along(self, axis, step):
        at = dict(self.at)
        at[axis] = (at[axis] + step) % 4
        return self.device(at, self.core)

    def partner(self):
        return self.device(self.at, 1 - self.core)

    def across(self):
        at = dict(self.at)
        at["y"] = (at["y"] + 2) % 4
        return self.device(at, 1 - self.core)


def slot_of(axis, value):
    return (value % 2) * 2 + value // 2 if axis == "y" else value


def greet(here):
    barrier = pltpu.get_barrier_semaphore()
    peers = [here.partner(), here.across()]
    peers += [here.along(axis, step) for axis in RING for step in (1, 2, 3)]
    for device in peers:
        pl.semaphore_signal(barrier, inc=1, device_id=device, device_id_type=MESH)
    pl.semaphore_wait(barrier, len(peers))


def remote(src, dst, send, recv, device):
    return pltpu.make_async_remote_copy(
        src_ref=src, dst_ref=dst, send_sem=send, recv_sem=recv, device_id=device, device_id_type=MESH
    )


def ring_total(own, first, second, third):
    return (own + second) + (first + third)


class SmallSum:
    def __init__(self, here, held, arrived, send, recv):
        self.phases = []
        count = 0
        for phase, axis in enumerate(("core", "y", "x", "z")):
            devices = [here.partner()] if axis == "core" else [here.along(axis, k) for k in (1, 2, 3)]
            copies = []
            for device in devices:
                copies.append(
                    remote(held.at[phase], arrived.at[count], send.at[count], recv.at[count], device)
                )
                count += 1
            self.phases.append((copies, list(range(count - len(devices), count))))
        self.held, self.arrived = held, arrived

    def start(self, phase):
        for copy in self.phases[phase][0]:
            copy.start()

    def finish(self, phase):
        copies, slots = self.phases[phase]
        for copy in copies:
            copy.wait_recv()
        total = self.held[phase]
        if len(slots) == 1:
            total = total + self.arrived[slots[0]]
        else:
            total = ring_total(total, *[self.arrived[slot] for slot in slots])
        if phase < 3:
            self.held[phase + 1] = total
        return total

    def drain(self):
        for copies, _ in self.phases:
            for copy in copies:
                copy.wait_send()


def region(fixed):
    return tuple(fixed.get(axis, slice(None)) for axis in ("x", "z", "y"))


def row_mask(cubes, which):
    row = lax.broadcasted_iota(jnp.int32, (ROWS, 196), 0)
    spot = jnp.where(row >= GRID * GRID, row - GRID * GRID, row)
    line = (spot * 1171) >> 14
    cube = (line >> 1) * (GRID // 2) + ((spot - line * GRID) >> 1)
    here = lax.broadcasted_iota(jnp.int32, (ROWS, 196), 1) == cube + which * 49
    return jnp.sum(jnp.where(here, cubes[...].astype(f32), 0.0), axis=1, keepdims=True)


def unit_of(values):
    average = jnp.mean(values, axis=-1, keepdims=True)
    centered = values - average
    inverse = lax.rsqrt(jnp.mean(centered * centered, axis=-1, keepdims=True) + epsilon)
    return centered * inverse, inverse


def unit_back(scaled, unit, inverse):
    return inverse * (
        scaled
        - jnp.mean(scaled, axis=-1, keepdims=True)
        - unit * jnp.mean(scaled * unit, axis=-1, keepdims=True)
    )


MASK, GAIN1, SHIFT1, PROJ, GAIN2, SHIFT2, FC2B = range(7)


def forward_kernel(
    small, fc1_bias, cubes, tokens, w_qkv, qv_bias, w_out, w_fc1, w_fc2,
    params, normed_out, qkv_out, lse_out, mixed_keep, pair_keep, last_keep, pair_in_out, last_in_out, w_out_all_out,
    w_last_all_out, gathered,
    normed, qkv, lse, mixed, pair_out, last_out, pair_in, last_in, w_out_all, w_last_all,
    rows, held, arrived, own_half, their_half, chip_block, block, values_t,
    tok_send, tok_recv, sum_send, sum_recv, half_sem, ff_send, ff_recv, fwd_send, fwd_recv,
    out_send, out_recv, mix_send, mix_recv, local_sem, on_send, on_recv,
):
    here = Place()
    core, head = here.core, here.head
    at = here.at
    mate = head + 1 - 2 * core
    far = (head + 2) % 4
    far_mate = far + 1 - 2 * core

    own_half[0] = w_fc1[...].astype(f32)
    own_half[1] = w_fc2[...].astype(f32)
    column = lax.broadcasted_iota(jnp.int32, (8, D), 1) - here.index * 6
    own_small = small[...].astype(f32)
    placed = jnp.zeros((8, D), f32)
    for j in range(6):
        placed = jnp.where(column == j, own_small[:, j : j + 1], placed)
    held[0, :, 0:D] = placed
    line = lax.broadcasted_iota(jnp.int32, (8, UNITS), 0)
    unit = lax.broadcasted_iota(jnp.int32, (8, UNITS), 1) - (here.index % 16) * 24
    shifted = jnp.zeros((8, UNITS), f32)
    own_bias = fc1_bias[...].astype(f32)
    for j in range(24):
        shifted = jnp.where(unit == j, own_bias[:, j : j + 1], shifted)
    held[0, :, D : D + UNITS] = jnp.where(line == here.index // 16, shifted, 0.0)
    sums = SmallSum(here, held, arrived, sum_send, sum_recv)

    greet(here)

    def tok_copy(way, k):
        lanes = pl.ds(k * 384, 384)
        src = rows.at[far, :, lanes] if way == 2 else tokens.at[:, lanes]
        dst = rows.at[far if way == 2 else head, :, lanes]
        device = here.along("y", 2) if way == 1 else here.partner()
        return remote(src, dst, tok_send.at[way, k], tok_recv.at[way, k], device)

    half_copy = remote(
        own_half.at[:, :, pl.ds(pl.multiple_of((1 - core) * UNITS, UNITS), UNITS)],
        their_half, half_sem.at[0], half_sem.at[1], here.partner(),
    )
    half_copy.start()
    sums.start(0)
    sums.finish(0)
    sums.start(1)

    half_copy.wait_recv()
    mine = pl.ds(pl.multiple_of(core * 24, 8), 24)
    theirs = pl.ds(pl.multiple_of((1 - core) * 24, 8), 24)
    for kind in (0, 1):
        chip_block[kind, mine, :] = own_half[kind, :, pl.ds(pl.multiple_of(core * UNITS, UNITS), UNITS)]
        chip_block[kind, theirs, :] = their_half[kind]
    for part in range(3):
        for kind in (0, 1):
            block[part, kind * 48 : kind * 48 + 48, :] = chip_block[
                kind, :, part * 128 : part * 128 + 128
            ].astype(bf16)

    slots = {axis: slot_of(axis, at[axis]) for axis in RING}
    ours = pl.ds(core * 3, 3)
    block_copy = pltpu.make_async_copy(block, gathered.at[(ours,) + region(slots)], local_sem.at[0])

    def ff_copy(kind, phase, step):
        order = GATHER[kind]
        of_kind = pl.ds(kind * 48, 48)
        spot = gathered.at[(ours,) + region({a: slots[a] for a in order[phase:]}) + (of_kind,)]
        return remote(
            block.at[:, of_kind] if phase == 0 else spot, spot,
            ff_send.at[kind, phase, step - 1], ff_recv.at[kind, phase, step - 1],
            here.along(order[phase], step),
        )

    def pass_copy(kind, step):
        last = GATHER[kind][2]
        of_kind = pl.ds(kind * 48, 48)
        plane = region({last: slot_of(last, (at[last] + 4 - step) % 4)})
        spot = gathered.at[(ours,) + plane + (of_kind,)]
        return remote(spot, spot, fwd_send.at[kind, step], fwd_recv.at[kind, step], here.partner())

    def onward_copy(kind, way):
        last = GATHER[kind][2]
        from_slot = slot_of(last, (at[last] + (3 if way == 0 else 1)) % 4)
        plane = region({last: from_slot, "y": pl.ds(2 * way, 2)})
        spot = gathered.at[(ours,) + plane + (pl.ds(kind * 48, 48),)]
        return remote(
            spot, spot, on_send.at[kind, way], on_recv.at[kind, way],
            here.along(last, 1 if way == 0 else 3),
        )

    def ff_start(phase):
        for step in (1, 3) if phase == 2 else (1, 3, 2):
            for kind in (0, 1):
                ff_copy(kind, phase, step).start()

    def ff_on(phase):
        for step in (1, 2, 3):
            for kind in (0, 1):
                ff_copy(kind, phase, step).wait_recv()
        ff_start(phase + 1)

    ff_start(0)
    block_copy.start()
    for way in (1, 0):
        for k in (0, 1):
            tok_copy(way, k).start()

    last_rows = pl.ds(384, 192)

    def out_copy(way, k):
        own = (w_out, w_qkv.at[last_rows])[k]
        every = (w_out_all, w_last_all)[k]
        src = every.at[far] if way == 2 else own
        dst = every.at[far if way == 2 else head]
        device = here.along("y", 2) if way == 1 else here.partner()
        return remote(src, dst, out_send.at[way, k], out_recv.at[way, k], device)

    for k in (0, 1):
        out_copy(0, k).start()
    w_out_all[head] = w_out[...]
    w_last_all[head] = w_qkv[384:576, :]
    rows[head] = tokens[...]
    sums.finish(1)
    sums.start(2)
    block_copy.wait()
    ff_on(0)
    sums.finish(2)
    sums.start(3)
    for k in (0, 1):
        tok_copy(0, k).wait_recv()
    params[...] = sums.finish(3)

    gain = params[GAIN1 : GAIN1 + 1, 0:D]
    shift = params[SHIFT1 : SHIFT1 + 1, 0:D]
    mask_token = params[MASK : MASK + 1, 0:D]
    biases = qv_bias[...].astype(f32)
    q_bias = biases[0:1, :]
    v_bias = biases[1:2, :]

    def project(half):
        parts = []
        for j in range(2):
            which = half * 2 + j
            masked = row_mask(cubes, which)
            start = jnp.where(masked > 0.5, mask_token, rows[which].astype(f32))
            unit1, _ = unit_of(start)
            parts.append(unit1 * gain + shift)
        normed[half] = jnp.concatenate(parts, axis=0).astype(bf16)

        to = pl.ds(pl.multiple_of(half * 784, 16), 784)
        for h in range(HEADS_HERE):
            packed = dot_nt(normed[half], w_qkv[h * 192 : h * 192 + 192, :])
            lanes = slice(h * 64, h * 64 + 64)
            query = packed[:, 0:64] + q_bias[:, lanes]
            value = packed[:, 128:192] + v_bias[:, lanes]
            qkv[h * 3, to, :] = query.astype(bf16) * bf16(0.125)
            qkv[h * 3 + 1, to, :] = packed[:, 64:128].astype(bf16)
            qkv[h * 3 + 2, to, :] = value.astype(bf16)

    chip_half = head // 2
    project(chip_half)
    ff_on(1)
    for kind in (0, 1):
        pass_copy(kind, 0).start()
    for k in (0, 1):
        tok_copy(1, k).wait_recv()
        tok_copy(2, k).start()
    for k in (0, 1):
        out_copy(1, k).start()
    for k in (0, 1):
        tok_copy(2, k).wait_recv()
    project(1 - chip_half)
    early = [
        pltpu.make_async_copy(normed, normed_out, local_sem.at[1]),
        pltpu.make_async_copy(qkv, qkv_out, local_sem.at[2]),
    ]
    for copy in early:
        copy.start()

    ones_row = (lax.broadcasted_iota(jnp.int32, (16, TOK), 0) == 0).astype(f32)
    for h in range(HEADS_HERE):
        values_t[h] = jnp.concatenate([qkv[h * 3 + 2].astype(f32).T, ones_row], axis=0).astype(bf16)

    def mix_copy(k, way):
        other, device = (
            (mate, here.partner()), (far, here.along("y", 2)), (far_mate, here.across()),
        )[way]
        src, dst = ((pair_out, pair_in), (last_out, last_in))[k]
        return remote(src.at[other], dst.at[head], mix_send.at[k, way], mix_recv.at[k, way], device)

    def mix_start(k):
        for j in range(4):
            own = slice(j * ROWS, j * ROWS + ROWS)
            if k == 0:
                pair_out[j] = jnp.concatenate([mixed[0, own, :], mixed[1, own, :]], axis=1).astype(bf16)
            else:
                last_out[j] = fold(mixed.at[2], j * ROWS)
        for way in (1, 2, 0):
            mix_copy(k, way).start()
        if k == 0:
            pair_in[head] = pair_out[head]
        else:
            last_in[head] = last_out[head]

    def ff_onward():
        for way, step in enumerate((1, 3)):
            for kind in (0, 1):
                ff_copy(kind, 2, step).wait_recv()
                onward_copy(kind, way).start()
        for step in (1, 3):
            for kind in (0, 1):
                pass_copy(kind, step).start()

    def out_on():
        for k in (0, 1):
            out_copy(1, k).wait_recv()
            out_copy(2, k).start()

    def attend(h, carry):
        def score(k):
            scores = dot_nt(qkv[h * 3 + 1], qkv[h * 3, k * QCHUNK : k * QCHUNK + QCHUNK, :])
            return scores, jnp.max(scores, axis=0, keepdims=True)

        ready = score(0)
        for k in range(CHUNKS):
            scores, top = ready
            if k + 1 < CHUNKS:
                ready = score(k + 1)
            weights = jnp.exp(scores - top).astype(bf16)
            outcome = dot_nn(values_t[h], weights)
            total = outcome[64:65, :]
            mixed[h, k * QCHUNK : k * QCHUNK + QCHUNK, :] = (outcome[0:64, :] / total).T
            lse[h * CHUNKS + k] = jnp.broadcast_to(top + jnp.log(total), (8, QCHUNK))
        pl.when(h == 0)(ff_onward)

        @pl.when(h == 1)
        def _():
            mix_start(0)
            out_on()

        return carry

    lax.fori_loop(0, HEADS_HERE, attend, 0)

    mix_start(1)
    for kind in (0, 1):
        for way in (0, 1):
            onward_copy(kind, way).wait_recv()
        pass_copy(kind, 2).start()
    for k in (0, 1):
        out_copy(0, k).wait_recv()
        out_copy(2, k).wait_recv()
    late = [
        pltpu.make_async_copy(lse, lse_out, local_sem.at[3]),
        pltpu.make_async_copy(mixed, mixed_keep, local_sem.at[4]),
        pltpu.make_async_copy(pair_out, pair_keep, local_sem.at[5]),
        pltpu.make_async_copy(last_out, last_keep, local_sem.at[9]),
        pltpu.make_async_copy(w_out_all, w_out_all_out, local_sem.at[6]),
        pltpu.make_async_copy(w_last_all, w_last_all_out, local_sem.at[8]),
    ]
    for copy in late:
        copy.start()
    for kind in (0, 1):
        for step in range(4):
            pass_copy(kind, step).wait_recv()
    for k in (0, 1):
        for way in range(3):
            mix_copy(k, way).wait_recv()
    last_copies = [
        pltpu.make_async_copy(pair_in, pair_in_out, local_sem.at[7]),
        pltpu.make_async_copy(last_in, last_in_out, local_sem.at[10]),
    ]
    for copy in last_copies:
        copy.start()
    sums.drain()
    half_copy.wait_send()
    for way in range(3):
        for k in (0, 1):
            out_copy(way, k).wait_send()
            tok_copy(way, k).wait_send()
        for k in (0, 1):
            mix_copy(k, way).wait_send()
    for kind in (0, 1):
        for phase in range(3):
            for step in (1, 3) if phase == 2 else (1, 2, 3):
                ff_copy(kind, phase, step).wait_send()
        for way in (0, 1):
            onward_copy(kind, way).wait_send()
        for step in range(4):
            pass_copy(kind, step).wait_send()
    for copy in early + late + last_copies:
        copy.wait()


VM = pl.BlockSpec(memory_space=pltpu.VMEM)
ANY = pl.BlockSpec(memory_space=pl.ANY)
DMA = pltpu.SemaphoreType.DMA


def shape(dims, kind=bf16):
    return jax.ShapeDtypeStruct(dims, kind)


def forward_call(*args):
    kept = (
        ((2, 784, D), bf16),
        ((9, TOK, 64), bf16),
        ((HEADS_HERE * CHUNKS, 8, QCHUNK), f32),
        ((HEADS_HERE, TOK, 64), f32),
        ((4, ROWS, 128), bf16),
        ((4, 200, 128), bf16),
        ((4, ROWS, 128), bf16),
        ((4, 200, 128), bf16),
        ((4, 192, D), bf16),
        ((4, 192, D), bf16),
    )
    return pl.pallas_call(
        forward_kernel,
        out_shape=(shape((8, D + UNITS), f32),)
        + tuple(shape(*k) for k in kept)
        + (shape((6, 4, 4, 4, 96, 128)),),
        in_specs=[VM] * 9,
        out_specs=(VM,) + (ANY,) * 11,
        scratch_shapes=[pltpu.VMEM(*k) for k in kept]
        + [
            pltpu.VMEM((4, ROWS, D), bf16),
            pltpu.VMEM((4, 8, D + UNITS), f32),
            pltpu.VMEM((10, 8, D + UNITS), f32),
            pltpu.VMEM((2, 24, D), f32),
            pltpu.VMEM((2, 24, UNITS), f32),
            pltpu.VMEM((2, 48, UNITS), f32),
            pltpu.VMEM((3, 96, 128), bf16),
            pltpu.VMEM((HEADS_HERE, 80, TOK), bf16),
            DMA((3, 2)), DMA((3, 2)), DMA((10,)), DMA((10,)), DMA((2,)),
            DMA((2, 3, 3)), DMA((2, 3, 3)), DMA((2, 4)), DMA((2, 4)),
            DMA((3, 2)), DMA((3, 2)), DMA((2, 3)), DMA((2, 3)), DMA((11,)), DMA((2, 2)), DMA((2, 2)),
        ],
        name="attention_forward",
        compiler_params=pltpu.CompilerParams(
            collective_id=0, has_side_effects=True, vmem_limit_bytes=VMEM_LIMIT
        ),
    )(*args)


SQRT_HALF = 0.7071067811865476
INV_SQRT_2PI = 0.3989422804014327


def feed_forward_kernel(
    cubes, params, tokens, cotangent, pair_in, last_in, w_out_all, weights,
    block_out, grad_middle, grad_branch, grad_pair, grad_last, small_grads, reduced_out,
    held, grads, arrived, reduced, normed2, outer, grad_normed2,
    load_sem, pair_send, pair_recv, keep_sem,
):
    here = Place()
    core, head = here.core, here.head

    def load(b):
        chips = pl.ds(b * 16, 16)
        return pltpu.make_async_copy(weights.at[:, chips], held.at[:, chips], load_sem.at[b])

    for b in range(BLOCKS):
        load(b).start()
    barrier = pltpu.get_barrier_semaphore()
    pl.semaphore_signal(barrier, inc=1, device_id=here.partner(), device_id_type=MESH)

    masked = row_mask(cubes, head)
    start = jnp.where(masked > 0.5, params[MASK : MASK + 1, 0:D], tokens[...].astype(f32))
    branch = jnp.zeros((ROWS, D), f32)
    for j in range(4):
        some = jnp.concatenate([pair_in[j], unfold(last_in[j])], axis=1)
        branch = branch + dot_nn(some, w_out_all[j])
    middle = start + branch + params[PROJ : PROJ + 1, 0:D]
    gain2 = params[GAIN2 : GAIN2 + 1, 0:D]
    unit2, _ = unit_of(middle)
    normed2[...] = (unit2 * gain2 + params[SHIFT2 : SHIFT2 + 1, 0:D]).astype(bf16)
    block_out[...] = middle
    outer[...] = jnp.zeros((ROWS, D), f32)
    grad_normed2[...] = jnp.zeros((ROWS, D), f32)
    pl.semaphore_wait(barrier, 1)
    mates = pl.ds((1 - core) * 3, 3)

    def pair_copy(b):
        chips = pl.ds(b * 16, 16)
        return remote(
            grads.at[mates, chips], arrived.at[:, chips], pair_send.at[b], pair_recv.at[b], here.partner()
        )

    def keep_copy(b):
        chips = pl.ds(b * 16, 16)
        return pltpu.make_async_copy(reduced.at[:, chips], reduced_out.at[:, chips], keep_sem.at[b])

    def add_pair(b):
        chips = pl.ds(b * 16, 16)
        pair_copy(b).wait_recv()
        for part in range(3):
            reduced[part, chips] = (
                grads[core * 3 + part, chips].astype(f32) + arrived[part, chips].astype(f32)
            ).astype(bf16)
        keep_copy(b).start()

    def some_units(b, carry):
        load(b).wait()
        chips = pl.ds(b * 16, 16)

        def weight(kind):
            return jnp.concatenate(
                [
                    held[s, chips, kind * 48 : kind * 48 + 48, :].reshape(2 * UNITS, 128)
                    for s in range(6)
                ],
                axis=1,
            )

        def keep(kind, grad):
            grad = grad.astype(bf16)
            for s in range(6):
                grads[s, chips, kind * 48 : kind * 48 + 48, :] = grad[
                    :, s * 128 : s * 128 + 128
                ].reshape(16, 48, 128)

        bias = jnp.concatenate(
            [params[pl.ds(2 * b + k, 1), D : D + UNITS] for k in (0, 1)], axis=1
        )
        inner = dot_nt(normed2[...], weight(0)) + bias
        below = 0.5 + 0.5 * lax.erf(inner * SQRT_HALF)
        active = (inner * below).astype(bf16)
        slope = below + inner * (INV_SQRT_2PI * jnp.exp(-0.5 * inner * inner))
        grad_active = dot_nt(cotangent[...], weight(1))
        grad_inner = (grad_active * slope).astype(bf16)
        bias_grad = jnp.sum(grad_inner.astype(f32), axis=0, keepdims=True)
        for k in (0, 1):
            small_grads[pl.ds(2 * b + k, 1), D : D + UNITS] = bias_grad[:, k * UNITS : k * UNITS + UNITS]
        outer[...] += dot_nn(active, weight(1))
        grad_normed2[...] += dot_nn(grad_inner, weight(0))
        keep(1, dot_tn(active, cotangent[...]))
        keep(0, dot_tn(grad_inner, normed2[...]))
        pair_copy(b).start()

        @pl.when(b > 0)
        def _():
            add_pair(b - 1)

        return carry

    lax.fori_loop(0, BLOCKS, some_units, 0)

    middle = block_out[...]
    block_out[...] = middle + outer[...] + params[FC2B : FC2B + 1, 0:D]
    unit2, inverse2 = unit_of(middle)
    grad_out = cotangent[...].astype(f32)
    back = grad_normed2[...]
    grad_mid = grad_out + unit_back(back * gain2, unit2, inverse2)
    grad_middle[...] = grad_mid
    low = grad_mid.astype(bf16)
    grad_branch[...] = low
    for j in range(4):
        some = dot_nt(low, w_out_all[j]).astype(bf16)
        grad_pair[j] = some[:, 0:128]
        grad_last[j] = some[:, 128:192]
    sums = [
        jnp.sum(v, axis=0, keepdims=True)
        for v in (grad_mid, back * unit2, back, grad_out)
    ]
    small_grads[:, 0:D] = jnp.concatenate(sums + [jnp.zeros((4, D), f32)], axis=0)
    add_pair(BLOCKS - 1)
    for b in range(BLOCKS):
        pair_copy(b).wait_send()
        keep_copy(b).wait()


def feed_forward_call(*args):
    return pl.pallas_call(
        feed_forward_kernel,
        out_shape=(
            shape((ROWS, D), f32),
            shape((ROWS, D), f32),
            shape((ROWS, D)),
            shape((4, ROWS, 128)),
            shape((4, ROWS, 64)),
            shape((8, D + UNITS), f32),
            shape((3, 64, 96, 128)),
        ),
        in_specs=[VM] * 7 + [ANY],
        out_specs=(VM,) * 6 + (ANY,),
        scratch_shapes=[
            pltpu.VMEM((6, 64, 96, 128), bf16),
            pltpu.VMEM((6, 64, 96, 128), bf16),
            pltpu.VMEM((3, 64, 96, 128), bf16),
            pltpu.VMEM((3, 64, 96, 128), bf16),
            pltpu.VMEM((ROWS, D), bf16),
            pltpu.VMEM((ROWS, D), f32),
            pltpu.VMEM((ROWS, D), f32),
            DMA((BLOCKS,)), DMA((BLOCKS,)), DMA((BLOCKS,)), DMA((BLOCKS,)),
        ],
        name="feed_forward",
        compiler_params=pltpu.CompilerParams(
            collective_id=1, has_side_effects=True, vmem_limit_bytes=VMEM_LIMIT
        ),
    )(*args)


def without(axes, axis):
    return tuple(a for a in axes if a != axis)


def backward_kernel(
    cubes, params, grad_pair, grad_last, grad_branch, small_grads, reduced,
    grad_middle_in, tokens_in, normed_in, qkv_in, lse_in, mixed_in, pair_in_, last_in_, w_qkv_in, w_last_in,
    tokens_grad, small_first, small_last, w_grads, w_fc1_grad, w_fc2_grad,
    grad_middle, tokens, normed, qkv, lse, mixed, mixed_pair, mixed_last, w_qkv, w_last, own_reduced,
    pair_back, last_back, mixed_wide, outer_back, queries, keys_t, grad_q, grad_kv, packed_back,
    branch_in, input_back, pair_out, pair_in, far_out, far_in,
    held, arrived, held_last, arrived_last,
    ff_in0, ff_sum1, ff_in1, ff_sum2, ff_in2, ff_last, ff_mate,
    w_src, w_in, w_z, w_z_in, w_y, w_y_in, w_all, column_sums,
    mix_send, mix_recv, br_send, br_recv, in_send, in_recv, sum_send, sum_recv, last_send, last_recv,
    ff_send, ff_recv, mate_sem, wx_send, wx_recv, wz_send, wz_recv, wy_send, wy_recv, wg_send, wg_recv,
    load_sem, last_out, last_in, value_out, value_in, head_send, head_recv,
):
    here = Place()
    core, head, at = here.core, here.head, here.at
    mate = head + 1 - 2 * core
    far = (head + 2) % 4
    far_mate = far + 1 - 2 * core
    slots = {axis: slot_of(axis, at[axis]) for axis in RING}

    def own_share(kind):
        axis = REDUCE[kind][0]
        return reduced.at[(slice(None),) + region({axis: slots[axis]}) + (pl.ds(kind * 48, 48),)]

    pairs = (
        (qkv_in, qkv), (lse_in, lse), (mixed_in, mixed), (tokens_in, tokens), (w_qkv_in, w_qkv),
        (normed_in, normed), (pair_in_, mixed_pair), (grad_middle_in, grad_middle),
        (own_share(0), own_reduced.at[0]), (own_share(1), own_reduced.at[1]), (w_last_in, w_last),
        (last_in_, mixed_last),
    )
    loads = [pltpu.make_async_copy(src, dst, load_sem.at[k]) for k, (src, dst) in enumerate(pairs)]
    for copy in loads:
        copy.start()
    greet(here)

    def mix_copy(k, way):
        other, device = (
            (mate, here.partner()), (far, here.along("y", 2)), (far_mate, here.across()),
        )[way]
        src, dst = ((grad_pair, pair_back), (grad_last, last_back))[k]
        return remote(src.at[other], dst.at[head], mix_send.at[k, way], mix_recv.at[k, way], device)

    for k in (0, 1):
        for way in (1, 2, 0):
            mix_copy(k, way).start()

    def peer_slot(axis, step):
        return slot_of(axis, (at[axis] + step) % 4)

    def ff_left(kind, phase):
        left = ("x", "z", "y")
        for done in REDUCE[kind][:phase]:
            left = without(left, done)
        return left

    def ff_copy(kind, phase, step):
        axis = REDUCE[kind][phase]
        where = tuple(
            peer_slot(axis, step) if a == axis else slice(None) for a in ff_left(kind, phase)
        )
        where = (slice(None),) + where
        if phase == 0:
            src = reduced.at[where + (pl.ds(kind * 48, 48),)]
        else:
            src = (ff_sum1, ff_sum2)[phase - 1].at[(kind,) + where]
        dst = (ff_in0, ff_in1, ff_in2)[phase]
        return remote(
            src, dst.at[kind, step - 1],
            ff_send.at[kind, phase, step - 1], ff_recv.at[kind, phase, step - 1],
            here.along(axis, step),
        )

    def ff_start(kind, phase):
        for step in (1, 2, 3):
            ff_copy(kind, phase, step).start()

    def ff_add(kind, phase):
        axis = REDUCE[kind][phase]
        where = tuple(slots[axis] if a == axis else slice(None) for a in ff_left(kind, phase))
        arrived_in = (ff_in0, ff_in1, ff_in2)[phase]
        for step in (1, 2, 3):
            ff_copy(kind, phase, step).wait_recv()
        if phase == 0:
            loads[8 + kind].wait()

        def some(part):
            if phase == 0:
                own = own_reduced[kind, part]
            else:
                own = (ff_sum1, ff_sum2)[phase - 1][(kind, part) + where]
            return ring_total(
                own.astype(f32), *[arrived_in[kind, k, part].astype(f32) for k in range(3)]
            )

        if phase == 0:
            @pl.loop(0, 3)
            def _(part):
                ff_sum1[kind, part] = some(part).astype(bf16)
        else:
            for part in range(3):
                total = some(part)
                if phase == 1:
                    ff_sum2[kind, part] = total.astype(bf16)
                else:
                    ff_last[kind, :, part * 128 : part * 128 + 128] = total

    for kind in (0, 1):
        ff_start(kind, 0)

    held[0] = small_grads[...]
    sums = SmallSum(here, held, arrived, sum_send, sum_recv)
    sums.start(0)

    beside = dict(at)
    beside["y"] = at["y"] + 1 - 2 * (at["y"] % 2)
    beside = here.device(beside, core)

    def first_axis(n):
        return "xz"[n % 2]

    def wx_copy(n, step):
        axis = first_axis(n)
        return remote(
            w_src.at[n, (at[axis] + step) % 4], w_in.at[n, step - 1],
            wx_send.at[n, step - 1], wx_recv.at[n, step - 1], here.along(axis, step),
        )

    def wz_copy(n, step):
        return remote(
            w_z.at[n], w_z_in.at[n, step - 1], wz_send.at[n, step - 1], wz_recv.at[n, step - 1],
            here.along(first_axis(n + 1), step),
        )

    def wy_copy(n):
        return remote(w_y.at[n], w_y_in.at[n], wy_send.at[n], wy_recv.at[n], beside)

    def wg_copy(n, step):
        axis = first_axis(n)
        spot = w_all.at[n, at[axis]]
        return remote(
            spot, spot, wg_send.at[n, step - 1], wg_recv.at[n, step - 1], here.along(axis, step)
        )

    def w_begin(n, grad):
        grad = grad.astype(bf16)
        for s in range(6):
            lanes = slice(s * 128, s * 128 + 128)
            first = s * 192
            for chunk in range(4):
                low, high = max(first, chunk * 288), min(first + 192, chunk * 288 + 288)
                if low < high:
                    w_src[n, chunk, low - chunk * 288 : high - chunk * 288, :] = grad[
                        low - first : high - first, lanes
                    ]
        for step in (1, 2, 3):
            wx_copy(n, step).start()

    def w_second(n):
        for step in (1, 2, 3):
            wx_copy(n, step).wait_recv()
        w_z[n] = ring_total(
            w_src[n, at[first_axis(n)]].astype(f32), *[w_in[n, k].astype(f32) for k in range(3)]
        ).astype(bf16)
        for step in (1, 2, 3):
            wz_copy(n, step).start()

    def w_third(n):
        for step in (1, 2, 3):
            wz_copy(n, step).wait_recv()
        w_y[n] = ring_total(
            w_z[n].astype(f32), *[w_z_in[n, k].astype(f32) for k in range(3)]
        ).astype(bf16)
        wy_copy(n).start()

    def w_fourth(n):
        wy_copy(n).wait_recv()
        w_all[n, at[first_axis(n)]] = (w_y[n].astype(f32) + w_y_in[n].astype(f32)).astype(bf16)
        for step in (1, 2, 3):
            wg_copy(n, step).start()

    def w_end(n):
        for step in (1, 2, 3):
            wg_copy(n, step).wait_recv()
        w_grads[n] = w_all[n]

    br_near = remote(grad_branch, branch_in.at[head], br_send.at[0], br_recv.at[0], here.partner())
    br_far = remote(grad_branch, branch_in.at[head], br_send.at[1], br_recv.at[1], here.along("y", 2))
    br_pass = remote(branch_in.at[far], branch_in.at[far], br_send.at[2], br_recv.at[2], here.partner())
    branch_in[head] = grad_branch[...]
    pair_back[head] = grad_pair[head]
    last_back[head] = grad_last[head]

    zeros = jnp.zeros((TOK, 64), bf16)
    loads[0].wait()
    for h in range(HEADS_HERE):
        query = qkv[h * 3]
        queries[h] = jnp.concatenate([zeros, query], axis=1)
        keys_t[h] = qkv[h * 3 + 1].astype(f32).T.astype(bf16)

    def outer_in(h):
        if h != 1:
            for way in range(3):
                mix_copy(h // 2, way).wait_recv()
        for j in range(4):
            block = last_back[j] if h == 2 else pair_back[j]
            lanes = slice(64, 128) if h == 1 else slice(0, 64)
            mixed_wide[j * ROWS : j * ROWS + ROWS, :] = block.astype(f32)[:, lanes]
        outer_back[h] = jnp.concatenate([mixed_wide[...].astype(bf16), zeros], axis=1)

    outer_in(0)
    br_far.start()
    br_near.start()
    for k in (1, 2, 3, 4, 5, 6, 7, 11):
        loads[k].wait()

    def branch_on():
        br_far.wait_recv()
        br_pass.start()

    def branch_end():
        br_near.wait_recv()
        br_pass.wait_recv()
        grad = jnp.zeros((192, D), f32)
        for j in range(4):
            some = jnp.concatenate([mixed_pair[j], unfold(mixed_last[j])], axis=1)
            grad = grad + dot_tn(some, branch_in[j])
        w_begin(0, grad)

    def sum_on(phase):
        total = sums.finish(phase)
        if phase < 3:
            sums.start(phase + 1)
        else:
            small_first[...] = total

    def ff_on(phase):
        for kind in (0, 1):
            ff_add(kind, phase)
            if phase < 2:
                ff_start(kind, phase + 1)

    chip = head // 2
    lane = lax.broadcasted_iota(jnp.int32, (TOK, 128), 1)

    def attend(h, carry):
        def score(k):
            chunk = slice(k * QCHUNK, k * QCHUNK + QCHUNK)
            scores = dot_nt(qkv[h * 3 + 1], qkv[h * 3, chunk, :])
            return scores, dot_nt(qkv[h * 3 + 2], outer_back[h, chunk, 0:64])

        ready = score(0)
        for k in range(CHUNKS):
            chunk = slice(k * QCHUNK, k * QCHUNK + QCHUNK)
            scores, grad_weights = ready
            if k + 1 < CHUNKS:
                ready = score(k + 1)
            given = outer_back[h, chunk, :]
            weights = jnp.exp(scores - lse[h * CHUNKS + k, 0:1, :])
            delta = jnp.sum(
                (given[:, 0:64].astype(f32) * mixed[h, chunk, :]).T, axis=0, keepdims=True
            )
            grad_scores = (weights * (grad_weights - delta)).astype(bf16)
            share = dot_nn(weights.astype(bf16), given) + dot_nn(grad_scores, queries[h, chunk, :])
            if k == 0:
                grad_kv[...] = share
            else:
                grad_kv[...] += share
            grad_q[chunk, 0:64] = dot_nn(keys_t[h], grad_scores).T * 0.125

        both = grad_kv[...]
        first = jnp.where(lane < 64, grad_q[...], both)
        packed_back[:, 0:128] = first.astype(bf16)
        packed_back[:, 128:192] = both[:, 0:64].astype(bf16)
        @pl.when(h < HEADS_HERE - 1)
        def _():
            for k, half in enumerate((1 - chip, chip)):
                share = dot_nn(
                    packed_back[pl.ds(pl.multiple_of(half * 784, 16), 784), :],
                    w_qkv[pl.ds(pl.multiple_of(h * 192, 16), 192), :],
                )
                for j in (0, 1):
                    some = share[j * ROWS : j * ROWS + ROWS]

                    @pl.when(h == 0)
                    def _():
                        input_back[half, j] = some

                    @pl.when(h > 0)
                    def _():
                        input_back[half, j] += some

                pl.when(h == HEADS_HERE - 2)(partial(pair_start, k, half))

        @pl.when(h == HEADS_HERE - 1)
        def _():
            for j in range(4):
                own = slice(j * ROWS, j * ROWS + ROWS)
                last_out[j] = first[own].astype(bf16)
                value_out[j] = fold(both, j * ROWS)
            for way in (1, 2, 0):
                for k in (0, 1):
                    head_copy(k, way).start()

        column_sums[pl.ds(h, 1), :] = jnp.sum(packed_back[...].astype(f32), axis=0, keepdims=True)

        @pl.when(h == HEADS_HERE - 2)
        def _():
            pair_copies[0].wait_recv()
            far_out[...] = (input_back[1 - chip, core] + pair_in[0].astype(f32)).astype(bf16)
            far_copy.start()

        w_grad = dot_tn(packed_back[...], normed[...])
        for n in range(HEADS_HERE):
            pl.when(h == n)(partial(w_begin, n + 1, w_grad))

        @pl.when(h == 0)
        def _():
            outer_in(1)
            sum_on(0)

        @pl.when(h == 1)
        def _():
            outer_in(2)
            sum_on(1)
            branch_on()

        return carry

    pair_copies = [
        remote(pair_out.at[k], pair_in.at[k], in_send.at[k], in_recv.at[k], here.partner()) for k in (0, 1)
    ]
    far_copy = remote(far_out, far_in, in_send.at[2], in_recv.at[2], here.along("y", 2))

    def head_copy(k, way):
        other, device = (
            (mate, here.partner()), (far, here.along("y", 2)), (far_mate, here.across()),
        )[way]
        src, dst = ((last_out, last_in), (value_out, value_in))[k]
        return remote(src.at[other], dst.at[head], head_send.at[k, way], head_recv.at[k, way], device)

    def pair_start(k, half):
        pair_out[k] = input_back[half, 1 - core].astype(bf16)
        pair_copies[k].start()

    lax.fori_loop(0, HEADS_HERE, attend, 0)

    branch_end()
    w_second(1)
    w_second(2)
    ff_on(0)
    sum_on(2)
    w_second(3)
    w_third(1)
    w_third(2)
    w_second(0)
    sum_on(3)

    masked = row_mask(cubes, head)
    start = jnp.where(masked > 0.5, params[MASK : MASK + 1, 0:D], tokens[...].astype(f32))
    unit1, inverse1 = unit_of(start)
    pair_copies[1].wait_recv()
    far_copy.wait_recv()
    last_in[head] = last_out[head]
    value_in[head] = value_out[head]
    loads[10].wait()
    back = input_back[chip, core] + pair_in[1].astype(f32) + far_in[...].astype(f32)
    for way in range(3):
        for k in (0, 1):
            head_copy(k, way).wait_recv()
    for j in range(4):
        some = jnp.concatenate([last_in[j], unfold(value_in[j])], axis=1)
        back = back + dot_nn(some, w_last[j])
    grad_start = grad_middle[...] + unit_back(
        back * params[GAIN1 : GAIN1 + 1, 0:D], unit1, inverse1
    )
    tokens_grad[...] = jnp.where(masked > 0.5, 0.0, grad_start)
    totals = [
        jnp.sum(v, axis=0, keepdims=True)
        for v in (back * unit1, back, jnp.where(masked > 0.5, grad_start, 0.0))
    ]
    held_last[0, :, 0:384] = jnp.concatenate(
        [v[:, k * 384 : k * 384 + 384] for v in totals for k in (0, 1)] + [jnp.zeros((2, 384), f32)],
        axis=0,
    )
    line = lax.broadcasted_iota(jnp.int32, (8, 192), 0)
    of_query = jnp.concatenate([column_sums[h : h + 1, 0:64] for h in range(HEADS_HERE)], axis=1)
    of_value = jnp.concatenate([column_sums[h : h + 1, 128:192] for h in range(HEADS_HERE)], axis=1)
    held_last[0, :, 384:576] = jnp.where(
        line == 2 * head, of_query, jnp.where(line == 2 * head + 1, of_value, 0.0)
    )
    held_last[0, :, 576:640] = jnp.zeros((8, 64), f32)
    last = SmallSum(here, held_last, arrived_last, last_send, last_recv)
    last.start(0)
    w_third(3)
    last.finish(0)
    last.start(1)
    w_third(0)
    w_fourth(1)
    w_fourth(2)
    ff_on(1)
    last.finish(1)
    last.start(2)
    w_fourth(3)
    w_fourth(0)
    ff_on(2)
    mate_copy = remote(
        ff_last.at[:, pl.ds(pl.multiple_of((1 - core) * 24, 8), 24), :], ff_mate,
        mate_sem.at[0], mate_sem.at[1], here.partner(),
    )
    mate_copy.start()
    last.finish(2)
    last.start(3)
    w_end(1)
    w_end(2)
    w_end(3)
    mate_copy.wait_recv()
    for kind, target in ((0, w_fc1_grad), (1, w_fc2_grad)):
        target[:, pl.ds(pl.multiple_of(core * UNITS, UNITS), UNITS)] = ff_last[
            kind, pl.ds(pl.multiple_of(core * 24, 8), 24), :
        ]
        target[:, pl.ds(pl.multiple_of((1 - core) * UNITS, UNITS), UNITS)] = ff_mate[kind]
    w_end(0)
    small_last[...] = last.finish(3)

    sums.drain()
    last.drain()
    for copy in [br_near, br_far, br_pass, far_copy, mate_copy] + pair_copies:
        copy.wait_send()
    for way in range(3):
        for k in (0, 1):
            head_copy(k, way).wait_send()
    for k in (0, 1):
        for way in range(3):
            mix_copy(k, way).wait_send()
    for kind in (0, 1):
        for phase in range(3):
            for step in (1, 2, 3):
                ff_copy(kind, phase, step).wait_send()
    for n in range(4):
        for step in (1, 2, 3):
            wx_copy(n, step).wait_send()
            wz_copy(n, step).wait_send()
            wg_copy(n, step).wait_send()
        wy_copy(n).wait_send()


def backward_call(*args):
    loaded = (
        ((ROWS, D), f32),
        ((ROWS, D), bf16),
        ((TOK, D), bf16),
        ((9, TOK, 64), bf16),
        ((HEADS_HERE * CHUNKS, 8, QCHUNK), f32),
        ((HEADS_HERE, TOK, 64), f32),
        ((4, ROWS, 128), bf16),
        ((4, 200, 128), bf16),
        ((576, D), bf16),
        ((4, 192, D), bf16),
    )
    return pl.pallas_call(
        backward_kernel,
        out_shape=(
            shape((ROWS, D), f32),
            shape((8, D + UNITS), f32),
            shape((8, 640), f32),
            shape((4, 4, 288, 128)),
            shape((24, D), f32),
            shape((24, D), f32),
        ),
        in_specs=[VM] * 6 + [ANY] * 11,
        out_specs=(VM,) * 6,
        scratch_shapes=[pltpu.VMEM(*k) for k in loaded]
        + [
            pltpu.VMEM((2, 3, 4, 4, 48, 128), bf16),
            pltpu.VMEM((4, ROWS, 128), bf16),
            pltpu.VMEM((4, ROWS, 64), bf16),
            pltpu.VMEM((TOK, 64), f32),
            pltpu.VMEM((HEADS_HERE, TOK, 128), bf16),
            pltpu.VMEM((HEADS_HERE, TOK, 128), bf16),
            pltpu.VMEM((HEADS_HERE, 64, TOK), bf16),
            pltpu.VMEM((TOK, 128), f32),
            pltpu.VMEM((TOK, 128), f32),
            pltpu.VMEM((TOK, 192), bf16),
            pltpu.VMEM((4, ROWS, D), bf16),
            pltpu.VMEM((2, 2, ROWS, D), f32),
            pltpu.VMEM((2, ROWS, D), bf16),
            pltpu.VMEM((2, ROWS, D), bf16),
            pltpu.VMEM((ROWS, D), bf16),
            pltpu.VMEM((ROWS, D), bf16),
            pltpu.VMEM((4, 8, D + UNITS), f32),
            pltpu.VMEM((10, 8, D + UNITS), f32),
            pltpu.VMEM((4, 8, 640), f32),
            pltpu.VMEM((10, 8, 640), f32),
            pltpu.VMEM((2, 3, 3, 4, 4, 48, 128), bf16),
            pltpu.VMEM((2, 3, 4, 4, 48, 128), bf16),
            pltpu.VMEM((2, 3, 3, 4, 48, 128), bf16),
            pltpu.VMEM((2, 3, 4, 48, 128), bf16),
            pltpu.VMEM((2, 3, 3, 48, 128), bf16),
            pltpu.VMEM((2, 48, UNITS), f32),
            pltpu.VMEM((2, 24, UNITS), f32),
            pltpu.VMEM((4, 4, 288, 128), bf16),
            pltpu.VMEM((4, 3, 288, 128), bf16),
            pltpu.VMEM((4, 288, 128), bf16),
            pltpu.VMEM((4, 3, 288, 128), bf16),
            pltpu.VMEM((4, 288, 128), bf16),
            pltpu.VMEM((4, 288, 128), bf16),
            pltpu.VMEM((4, 4, 288, 128), bf16),
            pltpu.VMEM((8, 192), f32),
            DMA((2, 3)), DMA((2, 3)), DMA((3,)), DMA((3,)), DMA((3,)), DMA((3,)),
            DMA((10,)), DMA((10,)), DMA((10,)), DMA((10,)),
            DMA((2, 3, 3)), DMA((2, 3, 3)), DMA((2,)),
            DMA((4, 3)), DMA((4, 3)), DMA((4, 3)), DMA((4, 3)), DMA((4,)), DMA((4,)), DMA((4, 3)), DMA((4, 3)),
            DMA((12,)),
            pltpu.VMEM((4, ROWS, 128), bf16),
            pltpu.VMEM((4, ROWS, 128), bf16),
            pltpu.VMEM((4, 200, 128), bf16),
            pltpu.VMEM((4, 200, 128), bf16),
            DMA((2, 3)), DMA((2, 3)),
        ],
        name="attention_backward",
        compiler_params=pltpu.CompilerParams(
            collective_id=2, has_side_effects=True, vmem_limit_bytes=VMEM_LIMIT
        ),
    )(*args)


def results_kernel(
    block_in, tokens_in, w_grads, w_fc1_in, w_fc2_in, first, last,
    block_out, tokens_grad, mask_grad, gain1_grad, shift1_grad, w_qkv_grad, qv_grad, w_out_grad,
    proj_grad, gain2_grad, shift2_grad, w_fc1_grad, fc1_grad, w_fc2_grad, fc2_grad,
):
    here = Place()
    pairs = (
        (block_in, block_out), (tokens_in, tokens_grad), (w_fc1_in, w_fc1_grad), (w_fc2_in, w_fc2_grad)
    )
    for src, dst in pairs:
        dst[...] = src[...]

    def pick(line, offset, count):
        column = lax.broadcasted_iota(jnp.int32, line.shape, 1) - offset
        spot = lax.broadcasted_iota(jnp.int32, (1, count), 1)
        out = jnp.zeros((1, count), f32)
        for j in range(count):
            one = jnp.sum(jnp.where(column == j, line, 0.0), axis=1, keepdims=True)
            out = jnp.where(spot == j, one, out)
        return out

    index = here.index
    for row, target in ((0, proj_grad), (1, gain2_grad), (2, shift2_grad), (3, fc2_grad)):
        target[...] = pick(first[row : row + 1, 0:D], index * 6, 6)
    fc1_grad[...] = pick(first[pl.ds(index // 16, 1), D : D + UNITS], (index % 16) * 24, 24)
    for k, target in enumerate((gain1_grad, shift1_grad, mask_grad)):
        target[...] = pick(last[pl.ds(2 * k + index // 64, 1), 0:384], (index % 64) * 6, 6)
    for k in (0, 1):
        qv_grad[k : k + 1, :] = last[pl.ds(2 * here.head + k, 1), 384:576]
    for n in range(4):
        for s in range(6):
            lanes = slice(s * 128, s * 128 + 128)
            start = s * 192
            for chunk in range(4):
                low, high = max(start, chunk * 288), min(start + 192, chunk * 288 + 288)
                if low < high:
                    got = w_grads[n, chunk, low - chunk * 288 : high - chunk * 288, :].astype(f32)
                    if n == 0:
                        w_out_grad[low - start : high - start, lanes] = got
                    else:
                        base = (n - 1) * 192 - start
                        w_qkv_grad[base + low : base + high, lanes] = got


def results_call(*args):
    six = shape((1, 6), f32)
    return pl.pallas_call(
        results_kernel,
        out_shape=(
            shape((ROWS, D), f32), shape((ROWS, D), f32), six, six, six, shape((576, D), f32),
            shape((2, 192), f32), shape((192, D), f32), six, six, six,
            shape((24, D), f32), shape((1, 24), f32), shape((24, D), f32), six,
        ),
        in_specs=[VM] * 7,
        out_specs=(VM,) * 15,
        name="results",
        compiler_params=pltpu.CompilerParams(vmem_limit_bytes=VMEM_LIMIT),
    )(*args)


def body(
    tokens, cube_mask, mask_token, norm1_gain, norm1_bias, w_qkv, qv_bias, w_out, proj_bias,
    norm2_gain, norm2_bias, w_fc1, fc1_bias, w_fc2, fc2_bias, cotangent,
):
    small = jnp.stack(
        [mask_token, norm1_gain, norm1_bias, proj_bias, norm2_gain, norm2_bias, fc2_bias, fc2_bias]
    )
    w_qkv_t = w_qkv.T
    (
        params, normed, qkv, lse, mixed, pair_out, last_out, pair_in, last_in, w_out_all, w_last_all, weights,
    ) = forward_call(
        small, fc1_bias[None], cube_mask, tokens, w_qkv_t, qv_bias, w_out, w_fc1.T, w_fc2,
    )
    block_out, grad_middle, grad_branch, grad_pair, grad_last, small_grads, reduced = feed_forward_call(
        cube_mask, params, tokens, cotangent, pair_in, last_in, w_out_all, weights.reshape(6, 64, 96, 128),
    )
    tokens_grad, small_first, small_last, w_grads, w_fc1_grad, w_fc2_grad = backward_call(
        cube_mask, params, grad_pair, grad_last, grad_branch, small_grads, reduced.reshape(3, 4, 4, 4, 96, 128),
        grad_middle, tokens, normed.reshape(TOK, D), qkv, lse, mixed, pair_out, last_out,
        w_qkv_t, w_last_all,
    )
    outs = list(
        results_call(block_out, tokens_grad, w_grads, w_fc1_grad, w_fc2_grad, small_first, small_last)
    )
    for k in (2, 3, 4, 8, 9, 10, 12, 14):
        outs[k] = outs[k].reshape(-1)
    outs[5] = outs[5].T
    outs[11] = outs[11].T
    return tuple(outs)


def solution(mesh):
    every = P(("clip", "head"))
    rows = P(("clip", "head"), None)
    columns = P(None, ("clip", "head"))
    in_specs = (
        rows, P("clip", None), every, every, every, P(None, "head"), P(None, "head"),
        P("head", None), every, every, every, columns, every, rows, every, rows,
    )
    out_specs = (
        rows, rows, every, every, every, P(None, "head"), P(None, "head"), P("head", None),
        every, every, every, columns, every, rows, every,
    )
    return jax.shard_map(body, mesh=mesh, in_specs=in_specs, out_specs=out_specs, check_vma=False)
```

```python
from functools import partial

import jax
import jax.numpy as jnp
import numpy as np
from jax import lax
from jax.experimental import pallas as pl
from jax.experimental.pallas import tpu as pltpu
from jax.sharding import PartitionSpec as P

HEAD_DIM = 64
GRID = 14
TOK = 1568
ROWS = 392
D = 768
HEADS_HERE = 3
QCHUNK = 224
CHUNKS = TOK // QCHUNK
UNITS = 384
BLOCKS = 4
epsilon = 1e-06
MESH = pl.DeviceIdType.MESH
VMEM_LIMIT = 60 * 2**20
f32 = jnp.float32
bf16 = jnp.bfloat16
GATHER = (("y", "x", "z"), ("y", "z", "x"))
REDUCE = (("x", "z", "y"), ("z", "x", "y"))
RING = ("x", "y", "z")


def dot_nn(left, right):
    return jnp.dot(left, right, preferred_element_type=f32)


def dot_nt(left, right):
    return lax.dot_general(left, right, (((1,), (1,)), ((), ())), preferred_element_type=f32)


def dot_tn(left, right):
    return lax.dot_general(left, right, (((0,), (0,)), ((), ())), preferred_element_type=f32)


def fold(values, start):
    return jnp.concatenate(
        [values[start : start + 200, 0:64], values[start + 192 : start + ROWS, 0:64]], axis=1
    ).astype(bf16)


def unfold(folded):
    wide = folded.astype(f32)
    return jnp.concatenate([wide[:, 0:64], wide[8:200, 64:128]], axis=0).astype(bf16)


class Place:
    def __init__(self):
        clip = lax.axis_index("clip")
        head = lax.axis_index("head")
        self.head = head
        self.index = clip * 4 + head
        self.at = {"x": clip // 8, "y": (head // 2) * 2 + clip % 2, "z": (clip // 2) % 4}
        self.core = head % 2

    def device(self, at, core):
        return {
            "clip": at["x"] * 8 + at["z"] * 2 + at["y"] % 2,
            "head": (at["y"] // 2) * 2 + core,
        }

    def along(self, axis, step):
        at = dict(self.at)
        at[axis] = (at[axis] + step) % 4
        return self.device(at, self.core)

    def partner(self):
        return self.device(self.at, 1 - self.core)

    def across(self):
        at = dict(self.at)
        at["y"] = (at["y"] + 2) % 4
        return self.device(at, 1 - self.core)


def slot_of(axis, value):
    return (value % 2) * 2 + value // 2 if axis == "y" else value


def greet(here):
    barrier = pltpu.get_barrier_semaphore()
    peers = [here.partner(), here.across()]
    peers += [here.along(axis, step) for axis in RING for step in (1, 2, 3)]
    for device in peers:
        pl.semaphore_signal(barrier, inc=1, device_id=device, device_id_type=MESH)
    pl.semaphore_wait(barrier, len(peers))


def remote(src, dst, send, recv, device):
    return pltpu.make_async_remote_copy(
        src_ref=src, dst_ref=dst, send_sem=send, recv_sem=recv, device_id=device, device_id_type=MESH
    )


def ring_total(own, first, second, third):
    return (own + second) + (first + third)


class SmallSum:
    def __init__(self, here, held, arrived, send, recv):
        self.phases = []
        count = 0
        for phase, axis in enumerate(("core", "y", "x", "z")):
            devices = [here.partner()] if axis == "core" else [here.along(axis, k) for k in (1, 2, 3)]
            copies = []
            for device in devices:
                copies.append(
                    remote(held.at[phase], arrived.at[count], send.at[count], recv.at[count], device)
                )
                count += 1
            self.phases.append((copies, list(range(count - len(devices), count))))
        self.held, self.arrived = held, arrived

    def start(self, phase):
        for copy in self.phases[phase][0]:
            copy.start()

    def finish(self, phase):
        copies, slots = self.phases[phase]
        for copy in copies:
            copy.wait_recv()
        total = self.held[phase]
        if len(slots) == 1:
            total = total + self.arrived[slots[0]]
        else:
            total = ring_total(total, *[self.arrived[slot] for slot in slots])
        if phase < 3:
            self.held[phase + 1] = total
        return total

    def drain(self):
        for copies, _ in self.phases:
            for copy in copies:
                copy.wait_send()


def region(fixed):
    return tuple(fixed.get(axis, slice(None)) for axis in ("x", "z", "y"))


def row_mask(cubes, which):
    row = lax.broadcasted_iota(jnp.int32, (ROWS, 196), 0)
    spot = jnp.where(row >= GRID * GRID, row - GRID * GRID, row)
    line = (spot * 1171) >> 14
    cube = (line >> 1) * (GRID // 2) + ((spot - line * GRID) >> 1)
    here = lax.broadcasted_iota(jnp.int32, (ROWS, 196), 1) == cube + which * 49
    return jnp.sum(jnp.where(here, cubes[...].astype(f32), 0.0), axis=1, keepdims=True)


def unit_of(values):
    average = jnp.mean(values, axis=-1, keepdims=True)
    centered = values - average
    inverse = lax.rsqrt(jnp.mean(centered * centered, axis=-1, keepdims=True) + epsilon)
    return centered * inverse, inverse


def unit_back(scaled, unit, inverse):
    return inverse * (
        scaled
        - jnp.mean(scaled, axis=-1, keepdims=True)
        - unit * jnp.mean(scaled * unit, axis=-1, keepdims=True)
    )


MASK, GAIN1, SHIFT1, PROJ, GAIN2, SHIFT2, FC2B = range(7)


def forward_kernel(
    small, fc1_bias, cubes, tokens, w_qkv, qv_bias, w_out, w_fc1, w_fc2,
    params, normed_out, qkv_out, lse_out, mixed_keep, pair_keep, last_keep, pair_in_out, last_in_out, w_out_all_out,
    w_last_all_out, gathered,
    normed, qkv, lse, mixed, pair_out, last_out, pair_in, last_in, w_out_all, w_last_all,
    rows, held, arrived, own_half, their_half, chip_block, block, values_t,
    tok_send, tok_recv, sum_send, sum_recv, half_sem, ff_send, ff_recv, fwd_send, fwd_recv,
    out_send, out_recv, mix_send, mix_recv, local_sem, on_send, on_recv,
):
    here = Place()
    core, head = here.core, here.head
    at = here.at
    mate = head + 1 - 2 * core
    far = (head + 2) % 4
    far_mate = far + 1 - 2 * core

    own_half[0] = w_fc1[...].astype(f32)
    own_half[1] = w_fc2[...].astype(f32)
    column = lax.broadcasted_iota(jnp.int32, (8, D), 1) - here.index * 6
    own_small = small[...].astype(f32)
    placed = jnp.zeros((8, D), f32)
    for j in range(6):
        placed = jnp.where(column == j, own_small[:, j : j + 1], placed)
    held[0, :, 0:D] = placed
    line = lax.broadcasted_iota(jnp.int32, (8, UNITS), 0)
    unit = lax.broadcasted_iota(jnp.int32, (8, UNITS), 1) - (here.index % 16) * 24
    shifted = jnp.zeros((8, UNITS), f32)
    own_bias = fc1_bias[...].astype(f32)
    for j in range(24):
        shifted = jnp.where(unit == j, own_bias[:, j : j + 1], shifted)
    held[0, :, D : D + UNITS] = jnp.where(line == here.index // 16, shifted, 0.0)
    sums = SmallSum(here, held, arrived, sum_send, sum_recv)

    greet(here)

    def tok_copy(way, k):
        lanes = pl.ds(k * 384, 384)
        src = rows.at[far, :, lanes] if way == 2 else tokens.at[:, lanes]
        dst = rows.at[far if way == 2 else head, :, lanes]
        device = here.along("y", 2) if way == 1 else here.partner()
        return remote(src, dst, tok_send.at[way, k], tok_recv.at[way, k], device)

    half_copy = remote(
        own_half.at[:, :, pl.ds(pl.multiple_of((1 - core) * UNITS, UNITS), UNITS)],
        their_half, half_sem.at[0], half_sem.at[1], here.partner(),
    )
    half_copy.start()
    sums.start(0)
    sums.finish(0)
    sums.start(1)

    half_copy.wait_recv()
    mine = pl.ds(pl.multiple_of(core * 24, 8), 24)
    theirs = pl.ds(pl.multiple_of((1 - core) * 24, 8), 24)
    for kind in (0, 1):
        chip_block[kind, mine, :] = own_half[kind, :, pl.ds(pl.multiple_of(core * UNITS, UNITS), UNITS)]
        chip_block[kind, theirs, :] = their_half[kind]
    for part in range(3):
        for kind in (0, 1):
            block[part, kind * 48 : kind * 48 + 48, :] = chip_block[
                kind, :, part * 128 : part * 128 + 128
            ].astype(bf16)

    slots = {axis: slot_of(axis, at[axis]) for axis in RING}
    ours = pl.ds(core * 3, 3)
    block_copy = pltpu.make_async_copy(block, gathered.at[(ours,) + region(slots)], local_sem.at[0])

    def ff_copy(kind, phase, step):
        order = GATHER[kind]
        of_kind = pl.ds(kind * 48, 48)
        spot = gathered.at[(ours,) + region({a: slots[a] for a in order[phase:]}) + (of_kind,)]
        return remote(
            block.at[:, of_kind] if phase == 0 else spot, spot,
            ff_send.at[kind, phase, step - 1], ff_recv.at[kind, phase, step - 1],
            here.along(order[phase], step),
        )

    def pass_copy(kind, step):
        last = GATHER[kind][2]
        of_kind = pl.ds(kind * 48, 48)
        plane = region({last: slot_of(last, (at[last] + 4 - step) % 4)})
        spot = gathered.at[(ours,) + plane + (of_kind,)]
        return remote(spot, spot, fwd_send.at[kind, step], fwd_recv.at[kind, step], here.partner())

    def onward_copy(kind, way):
        last = GATHER[kind][2]
        from_slot = slot_of(last, (at[last] + (3 if way == 0 else 1)) % 4)
        plane = region({last: from_slot, "y": pl.ds(2 * way, 2)})
        spot = gathered.at[(ours,) + plane + (pl.ds(kind * 48, 48),)]
        return remote(
            spot, spot, on_send.at[kind, way], on_recv.at[kind, way],
            here.along(last, 1 if way == 0 else 3),
        )

    def ff_start(phase):
        for step in (1, 3) if phase == 2 else (1, 3, 2):
            for kind in (0, 1):
                ff_copy(kind, phase, step).start()

    def ff_on(phase):
        for step in (1, 2, 3):
            for kind in (0, 1):
                ff_copy(kind, phase, step).wait_recv()
        ff_start(phase + 1)

    ff_start(0)
    block_copy.start()
    for way in (1, 0):
        for k in (0, 1):
            tok_copy(way, k).start()

    last_rows = pl.ds(384, 192)

    def out_copy(way, k):
        own = (w_out, w_qkv.at[last_rows])[k]
        every = (w_out_all, w_last_all)[k]
        src = every.at[far] if way == 2 else own
        dst = every.at[far if way == 2 else head]
        device = here.along("y", 2) if way == 1 else here.partner()
        return remote(src, dst, out_send.at[way, k], out_recv.at[way, k], device)

    for k in (0, 1):
        out_copy(0, k).start()
    w_out_all[head] = w_out[...]
    w_last_all[head] = w_qkv[384:576, :]
    rows[head] = tokens[...]
    sums.finish(1)
    sums.start(2)
    block_copy.wait()
    ff_on(0)
    sums.finish(2)
    sums.start(3)
    for k in (0, 1):
        tok_copy(0, k).wait_recv()
    params[...] = sums.finish(3)

    gain = params[GAIN1 : GAIN1 + 1, 0:D]
    shift = params[SHIFT1 : SHIFT1 + 1, 0:D]
    mask_token = params[MASK : MASK + 1, 0:D]
    biases = qv_bias[...].astype(f32)
    q_bias = biases[0:1, :]
    v_bias = biases[1:2, :]

    def project(half):
        parts = []
        for j in range(2):
            which = half * 2 + j
            masked = row_mask(cubes, which)
            start = jnp.where(masked > 0.5, mask_token, rows[which].astype(f32))
            unit1, _ = unit_of(start)
            parts.append(unit1 * gain + shift)
        normed[half] = jnp.concatenate(parts, axis=0).astype(bf16)

        to = pl.ds(pl.multiple_of(half * 784, 16), 784)
        for h in range(HEADS_HERE):
            packed = dot_nt(normed[half], w_qkv[h * 192 : h * 192 + 192, :])
            lanes = slice(h * 64, h * 64 + 64)
            query = packed[:, 0:64] + q_bias[:, lanes]
            value = packed[:, 128:192] + v_bias[:, lanes]
            qkv[h * 3, to, :] = query.astype(bf16) * bf16(0.125)
            qkv[h * 3 + 1, to, :] = packed[:, 64:128].astype(bf16)
            qkv[h * 3 + 2, to, :] = value.astype(bf16)

    chip_half = head // 2
    project(chip_half)
    ff_on(1)
    for kind in (0, 1):
        pass_copy(kind, 0).start()
    for k in (0, 1):
        tok_copy(1, k).wait_recv()
        tok_copy(2, k).start()
    for k in (0, 1):
        out_copy(1, k).start()
    for k in (0, 1):
        tok_copy(2, k).wait_recv()
    project(1 - chip_half)
    early = [
        pltpu.make_async_copy(normed, normed_out, local_sem.at[1]),
        pltpu.make_async_copy(qkv, qkv_out, local_sem.at[2]),
    ]
    for copy in early:
        copy.start()

    ones_row = (lax.broadcasted_iota(jnp.int32, (16, TOK), 0) == 0).astype(f32)
    for h in range(HEADS_HERE):
        values_t[h] = jnp.concatenate([qkv[h * 3 + 2].astype(f32).T, ones_row], axis=0).astype(bf16)

    def mix_copy(k, way):
        other, device = (
            (mate, here.partner()), (far, here.along("y", 2)), (far_mate, here.across()),
        )[way]
        src, dst = ((pair_out, pair_in), (last_out, last_in))[k]
        return remote(src.at[other], dst.at[head], mix_send.at[k, way], mix_recv.at[k, way], device)

    def mix_start(k):
        for j in range(4):
            own = slice(j * ROWS, j * ROWS + ROWS)
            if k == 0:
                pair_out[j] = jnp.concatenate([mixed[0, own, :], mixed[1, own, :]], axis=1).astype(bf16)
            else:
                last_out[j] = fold(mixed.at[2], j * ROWS)
        for way in (1, 2, 0):
            mix_copy(k, way).start()
        if k == 0:
            pair_in[head] = pair_out[head]
        else:
            last_in[head] = last_out[head]

    def ff_onward():
        for way, step in enumerate((1, 3)):
            for kind in (0, 1):
                ff_copy(kind, 2, step).wait_recv()
                onward_copy(kind, way).start()
        for step in (1, 3):
            for kind in (0, 1):
                pass_copy(kind, step).start()

    def out_on():
        for k in (0, 1):
            out_copy(1, k).wait_recv()
            out_copy(2, k).start()

    def attend(h, carry):
        def score(k):
            scores = dot_nt(qkv[h * 3 + 1], qkv[h * 3, k * QCHUNK : k * QCHUNK + QCHUNK, :])
            return scores, jnp.max(scores, axis=0, keepdims=True)

        ready = score(0)
        for k in range(CHUNKS):
            scores, top = ready
            if k + 1 < CHUNKS:
                ready = score(k + 1)
            weights = jnp.exp(scores - top).astype(bf16)
            outcome = dot_nn(values_t[h], weights)
            total = outcome[64:65, :]
            mixed[h, k * QCHUNK : k * QCHUNK + QCHUNK, :] = (outcome[0:64, :] / total).T
            lse[h * CHUNKS + k] = jnp.broadcast_to(top + jnp.log(total), (8, QCHUNK))
        pl.when(h == 0)(ff_onward)

        @pl.when(h == 1)
        def _():
            mix_start(0)
            out_on()

        return carry

    lax.fori_loop(0, HEADS_HERE, attend, 0)

    mix_start(1)
    for kind in (0, 1):
        for way in (0, 1):
            onward_copy(kind, way).wait_recv()
        pass_copy(kind, 2).start()
    for k in (0, 1):
        out_copy(0, k).wait_recv()
        out_copy(2, k).wait_recv()
    late = [
        pltpu.make_async_copy(lse, lse_out, local_sem.at[3]),
        pltpu.make_async_copy(mixed, mixed_keep, local_sem.at[4]),
        pltpu.make_async_copy(pair_out, pair_keep, local_sem.at[5]),
        pltpu.make_async_copy(last_out, last_keep, local_sem.at[9]),
        pltpu.make_async_copy(w_out_all, w_out_all_out, local_sem.at[6]),
        pltpu.make_async_copy(w_last_all, w_last_all_out, local_sem.at[8]),
    ]
    for copy in late:
        copy.start()
    for kind in (0, 1):
        for step in range(4):
            pass_copy(kind, step).wait_recv()
    for k in (0, 1):
        for way in range(3):
            mix_copy(k, way).wait_recv()
    last_copies = [
        pltpu.make_async_copy(pair_in, pair_in_out, local_sem.at[7]),
        pltpu.make_async_copy(last_in, last_in_out, local_sem.at[10]),
    ]
    for copy in last_copies:
        copy.start()
    sums.drain()
    half_copy.wait_send()
    for way in range(3):
        for k in (0, 1):
            out_copy(way, k).wait_send()
            tok_copy(way, k).wait_send()
        for k in (0, 1):
            mix_copy(k, way).wait_send()
    for kind in (0, 1):
        for phase in range(3):
            for step in (1, 3) if phase == 2 else (1, 2, 3):
                ff_copy(kind, phase, step).wait_send()
        for way in (0, 1):
            onward_copy(kind, way).wait_send()
        for step in range(4):
            pass_copy(kind, step).wait_send()
    for copy in early + late + last_copies:
        copy.wait()


VM = pl.BlockSpec(memory_space=pltpu.VMEM)
ANY = pl.BlockSpec(memory_space=pl.ANY)
DMA = pltpu.SemaphoreType.DMA


def shape(dims, kind=bf16):
    return jax.ShapeDtypeStruct(dims, kind)


def forward_call(*args):
    kept = (
        ((2, 784, D), bf16),
        ((9, TOK, 64), bf16),
        ((HEADS_HERE * CHUNKS, 8, QCHUNK), f32),
        ((HEADS_HERE, TOK, 64), f32),
        ((4, ROWS, 128), bf16),
        ((4, 200, 128), bf16),
        ((4, ROWS, 128), bf16),
        ((4, 200, 128), bf16),
        ((4, 192, D), bf16),
        ((4, 192, D), bf16),
    )
    return pl.pallas_call(
        forward_kernel,
        out_shape=(shape((8, D + UNITS), f32),)
        + tuple(shape(*k) for k in kept)
        + (shape((6, 4, 4, 4, 96, 128)),),
        in_specs=[VM] * 9,
        out_specs=(VM,) + (ANY,) * 11,
        scratch_shapes=[pltpu.VMEM(*k) for k in kept]
        + [
            pltpu.VMEM((4, ROWS, D), bf16),
            pltpu.VMEM((4, 8, D + UNITS), f32),
            pltpu.VMEM((10, 8, D + UNITS), f32),
            pltpu.VMEM((2, 24, D), f32),
            pltpu.VMEM((2, 24, UNITS), f32),
            pltpu.VMEM((2, 48, UNITS), f32),
            pltpu.VMEM((3, 96, 128), bf16),
            pltpu.VMEM((HEADS_HERE, 80, TOK), bf16),
            DMA((3, 2)), DMA((3, 2)), DMA((10,)), DMA((10,)), DMA((2,)),
            DMA((2, 3, 3)), DMA((2, 3, 3)), DMA((2, 4)), DMA((2, 4)),
            DMA((3, 2)), DMA((3, 2)), DMA((2, 3)), DMA((2, 3)), DMA((11,)), DMA((2, 2)), DMA((2, 2)),
        ],
        name="attention_forward",
        compiler_params=pltpu.CompilerParams(
            collective_id=0, has_side_effects=True, vmem_limit_bytes=VMEM_LIMIT
        ),
    )(*args)


SQRT_HALF = 0.7071067811865476
INV_SQRT_2PI = 0.3989422804014327


def feed_forward_kernel(
    cubes, params, tokens, cotangent, pair_in, last_in, w_out_all, weights,
    block_out, grad_middle, grad_branch, grad_pair, grad_last, small_grads, reduced_out,
    held, grads, arrived, reduced, normed2, outer, grad_normed2,
    load_sem, pair_send, pair_recv, keep_sem,
):
    here = Place()
    core, head = here.core, here.head

    def load(b):
        chips = pl.ds(b * 16, 16)
        return pltpu.make_async_copy(weights.at[:, chips], held.at[:, chips], load_sem.at[b])

    for b in range(BLOCKS):
        load(b).start()
    barrier = pltpu.get_barrier_semaphore()
    pl.semaphore_signal(barrier, inc=1, device_id=here.partner(), device_id_type=MESH)

    masked = row_mask(cubes, head)
    start = jnp.where(masked > 0.5, params[MASK : MASK + 1, 0:D], tokens[...].astype(f32))
    branch = jnp.zeros((ROWS, D), f32)
    for j in range(4):
        some = jnp.concatenate([pair_in[j], unfold(last_in[j])], axis=1)
        branch = branch + dot_nn(some, w_out_all[j])
    middle = start + branch + params[PROJ : PROJ + 1, 0:D]
    gain2 = params[GAIN2 : GAIN2 + 1, 0:D]
    unit2, _ = unit_of(middle)
    normed2[...] = (unit2 * gain2 + params[SHIFT2 : SHIFT2 + 1, 0:D]).astype(bf16)
    block_out[...] = middle
    outer[...] = jnp.zeros((ROWS, D), f32)
    grad_normed2[...] = jnp.zeros((ROWS, D), f32)
    pl.semaphore_wait(barrier, 1)
    mates = pl.ds((1 - core) * 3, 3)

    def pair_copy(b):
        chips = pl.ds(b * 16, 16)
        return remote(
            grads.at[mates, chips], arrived.at[:, chips], pair_send.at[b], pair_recv.at[b], here.partner()
        )

    def keep_copy(b):
        chips = pl.ds(b * 16, 16)
        return pltpu.make_async_copy(reduced.at[:, chips], reduced_out.at[:, chips], keep_sem.at[b])

    def add_pair(b):
        chips = pl.ds(b * 16, 16)
        pair_copy(b).wait_recv()
        for part in range(3):
            reduced[part, chips] = (
                grads[core * 3 + part, chips].astype(f32) + arrived[part, chips].astype(f32)
            ).astype(bf16)
        keep_copy(b).start()

    def some_units(b, carry):
        load(b).wait()
        chips = pl.ds(b * 16, 16)

        def weight(kind):
            return jnp.concatenate(
                [
                    held[s, chips, kind * 48 : kind * 48 + 48, :].reshape(2 * UNITS, 128)
                    for s in range(6)
                ],
                axis=1,
            )

        def keep(kind, grad):
            grad = grad.astype(bf16)
            for s in range(6):
                grads[s, chips, kind * 48 : kind * 48 + 48, :] = grad[
                    :, s * 128 : s * 128 + 128
                ].reshape(16, 48, 128)

        bias = jnp.concatenate(
            [params[pl.ds(2 * b + k, 1), D : D + UNITS] for k in (0, 1)], axis=1
        )
        inner = dot_nt(normed2[...], weight(0)) + bias
        below = 0.5 + 0.5 * lax.erf(inner * SQRT_HALF)
        active = (inner * below).astype(bf16)
        slope = below + inner * (INV_SQRT_2PI * jnp.exp(-0.5 * inner * inner))
        grad_active = dot_nt(cotangent[...], weight(1))
        grad_inner = (grad_active * slope).astype(bf16)
        bias_grad = jnp.sum(grad_inner.astype(f32), axis=0, keepdims=True)
        for k in (0, 1):
            small_grads[pl.ds(2 * b + k, 1), D : D + UNITS] = bias_grad[:, k * UNITS : k * UNITS + UNITS]
        outer[...] += dot_nn(active, weight(1))
        grad_normed2[...] += dot_nn(grad_inner, weight(0))
        keep(1, dot_tn(active, cotangent[...]))
        keep(0, dot_tn(grad_inner, normed2[...]))
        pair_copy(b).start()

        @pl.when(b > 0)
        def _():
            add_pair(b - 1)

        return carry

    lax.fori_loop(0, BLOCKS, some_units, 0)

    middle = block_out[...]
    block_out[...] = middle + outer[...] + params[FC2B : FC2B + 1, 0:D]
    unit2, inverse2 = unit_of(middle)
    grad_out = cotangent[...].astype(f32)
    back = grad_normed2[...]
    grad_mid = grad_out + unit_back(back * gain2, unit2, inverse2)
    grad_middle[...] = grad_mid
    low = grad_mid.astype(bf16)
    grad_branch[...] = low
    for j in range(4):
        some = dot_nt(low, w_out_all[j]).astype(bf16)
        grad_pair[j] = some[:, 0:128]
        grad_last[j] = some[:, 128:192]
    sums = [
        jnp.sum(v, axis=0, keepdims=True)
        for v in (grad_mid, back * unit2, back, grad_out)
    ]
    small_grads[:, 0:D] = jnp.concatenate(sums + [jnp.zeros((4, D), f32)], axis=0)
    add_pair(BLOCKS - 1)
    for b in range(BLOCKS):
        pair_copy(b).wait_send()
        keep_copy(b).wait()


def feed_forward_call(*args):
    return pl.pallas_call(
        feed_forward_kernel,
        out_shape=(
            shape((ROWS, D), f32),
            shape((ROWS, D), f32),
            shape((ROWS, D)),
            shape((4, ROWS, 128)),
            shape((4, ROWS, 64)),
            shape((8, D + UNITS), f32),
            shape((3, 64, 96, 128)),
        ),
        in_specs=[VM] * 7 + [ANY],
        out_specs=(VM,) * 6 + (ANY,),
        scratch_shapes=[
            pltpu.VMEM((6, 64, 96, 128), bf16),
            pltpu.VMEM((6, 64, 96, 128), bf16),
            pltpu.VMEM((3, 64, 96, 128), bf16),
            pltpu.VMEM((3, 64, 96, 128), bf16),
            pltpu.VMEM((ROWS, D), bf16),
            pltpu.VMEM((ROWS, D), f32),
            pltpu.VMEM((ROWS, D), f32),
            DMA((BLOCKS,)), DMA((BLOCKS,)), DMA((BLOCKS,)), DMA((BLOCKS,)),
        ],
        name="feed_forward",
        compiler_params=pltpu.CompilerParams(
            collective_id=1, has_side_effects=True, vmem_limit_bytes=VMEM_LIMIT
        ),
    )(*args)


def without(axes, axis):
    return tuple(a for a in axes if a != axis)


def backward_kernel(
    cubes, params, grad_pair, grad_last, grad_branch, small_grads, reduced,
    grad_middle_in, tokens_in, normed_in, qkv_in, lse_in, mixed_in, pair_in_, last_in_, w_qkv_in, w_last_in,
    tokens_grad, small_first, small_last, w_grads, w_fc1_grad, w_fc2_grad,
    grad_middle, tokens, normed, qkv, lse, mixed, mixed_pair, mixed_last, w_qkv, w_last, own_reduced,
    pair_back, last_back, mixed_wide, outer_back, queries, keys_t, grad_q, grad_kv, packed_back,
    branch_in, input_back, pair_out, pair_in, far_out, far_in,
    held, arrived, held_last, arrived_last,
    ff_in0, ff_sum1, ff_in1, ff_sum2, ff_in2, ff_last, ff_mate,
    w_src, w_in, w_z, w_z_in, w_y, w_y_in, w_all, column_sums,
    mix_send, mix_recv, br_send, br_recv, in_send, in_recv, sum_send, sum_recv, last_send, last_recv,
    ff_send, ff_recv, mate_sem, wx_send, wx_recv, wz_send, wz_recv, wy_send, wy_recv, wg_send, wg_recv,
    load_sem, last_out, last_in, value_out, value_in, head_send, head_recv,
):
    here = Place()
    core, head, at = here.core, here.head, here.at
    mate = head + 1 - 2 * core
    far = (head + 2) % 4
    far_mate = far + 1 - 2 * core
    slots = {axis: slot_of(axis, at[axis]) for axis in RING}

    def own_share(kind):
        axis = REDUCE[kind][0]
        return reduced.at[(slice(None),) + region({axis: slots[axis]}) + (pl.ds(kind * 48, 48),)]

    pairs = (
        (qkv_in, qkv), (lse_in, lse), (mixed_in, mixed), (tokens_in, tokens), (w_qkv_in, w_qkv),
        (normed_in, normed), (pair_in_, mixed_pair), (grad_middle_in, grad_middle),
        (own_share(0), own_reduced.at[0]), (own_share(1), own_reduced.at[1]), (w_last_in, w_last),
        (last_in_, mixed_last),
    )
    loads = [pltpu.make_async_copy(src, dst, load_sem.at[k]) for k, (src, dst) in enumerate(pairs)]
    for copy in loads:
        copy.start()
    greet(here)

    def mix_copy(k, way):
        other, device = (
            (mate, here.partner()), (far, here.along("y", 2)), (far_mate, here.across()),
        )[way]
        src, dst = ((grad_pair, pair_back), (grad_last, last_back))[k]
        return remote(src.at[other], dst.at[head], mix_send.at[k, way], mix_recv.at[k, way], device)

    for k in (0, 1):
        for way in (1, 2, 0):
            mix_copy(k, way).start()

    def peer_slot(axis, step):
        return slot_of(axis, (at[axis] + step) % 4)

    def ff_left(kind, phase):
        left = ("x", "z", "y")
        for done in REDUCE[kind][:phase]:
            left = without(left, done)
        return left

    def ff_copy(kind, phase, step):
        axis = REDUCE[kind][phase]
        where = tuple(
            peer_slot(axis, step) if a == axis else slice(None) for a in ff_left(kind, phase)
        )
        where = (slice(None),) + where
        if phase == 0:
            src = reduced.at[where + (pl.ds(kind * 48, 48),)]
        else:
            src = (ff_sum1, ff_sum2)[phase - 1].at[(kind,) + where]
        dst = (ff_in0, ff_in1, ff_in2)[phase]
        return remote(
            src, dst.at[kind, step - 1],
            ff_send.at[kind, phase, step - 1], ff_recv.at[kind, phase, step - 1],
            here.along(axis, step),
        )

    def ff_start(kind, phase):
        for step in (1, 2, 3):
            ff_copy(kind, phase, step).start()

    def ff_add(kind, phase):
        axis = REDUCE[kind][phase]
        where = tuple(slots[axis] if a == axis else slice(None) for a in ff_left(kind, phase))
        arrived_in = (ff_in0, ff_in1, ff_in2)[phase]
        for step in (1, 2, 3):
            ff_copy(kind, phase, step).wait_recv()
        if phase == 0:
            loads[8 + kind].wait()

        def some(part):
            if phase == 0:
                own = own_reduced[kind, part]
            else:
                own = (ff_sum1, ff_sum2)[phase - 1][(kind, part) + where]
            return ring_total(
                own.astype(f32), *[arrived_in[kind, k, part].astype(f32) for k in range(3)]
            )

        if phase == 0:
            @pl.loop(0, 3)
            def _(part):
                ff_sum1[kind, part] = some(part).astype(bf16)
        else:
            for part in range(3):
                total = some(part)
                if phase == 1:
                    ff_sum2[kind, part] = total.astype(bf16)
                else:
                    ff_last[kind, :, part * 128 : part * 128 + 128] = total

    for kind in (0, 1):
        ff_start(kind, 0)

    held[0] = small_grads[...]
    sums = SmallSum(here, held, arrived, sum_send, sum_recv)
    sums.start(0)

    beside = dict(at)
    beside["y"] = at["y"] + 1 - 2 * (at["y"] % 2)
    beside = here.device(beside, core)

    def first_axis(n):
        return "xz"[n % 2]

    def wx_copy(n, step):
        axis = first_axis(n)
        return remote(
            w_src.at[n, (at[axis] + step) % 4], w_in.at[n, step - 1],
            wx_send.at[n, step - 1], wx_recv.at[n, step - 1], here.along(axis, step),
        )

    def wz_copy(n, step):
        return remote(
            w_z.at[n], w_z_in.at[n, step - 1], wz_send.at[n, step - 1], wz_recv.at[n, step - 1],
            here.along(first_axis(n + 1), step),
        )

    def wy_copy(n):
        return remote(w_y.at[n], w_y_in.at[n], wy_send.at[n], wy_recv.at[n], beside)

    def wg_copy(n, step):
        axis = first_axis(n)
        spot = w_all.at[n, at[axis]]
        return remote(
            spot, spot, wg_send.at[n, step - 1], wg_recv.at[n, step - 1], here.along(axis, step)
        )

    def w_begin(n, grad):
        grad = grad.astype(bf16)
        for s in range(6):
            lanes = slice(s * 128, s * 128 + 128)
            first = s * 192
            for chunk in range(4):
                low, high = max(first, chunk * 288), min(first + 192, chunk * 288 + 288)
                if low < high:
                    w_src[n, chunk, low - chunk * 288 : high - chunk * 288, :] = grad[
                        low - first : high - first, lanes
                    ]
        for step in (1, 2, 3):
            wx_copy(n, step).start()

    def w_second(n):
        for step in (1, 2, 3):
            wx_copy(n, step).wait_recv()
        w_z[n] = ring_total(
            w_src[n, at[first_axis(n)]].astype(f32), *[w_in[n, k].astype(f32) for k in range(3)]
        ).astype(bf16)
        for step in (1, 2, 3):
            wz_copy(n, step).start()

    def w_third(n):
        for step in (1, 2, 3):
            wz_copy(n, step).wait_recv()
        w_y[n] = ring_total(
            w_z[n].astype(f32), *[w_z_in[n, k].astype(f32) for k in range(3)]
        ).astype(bf16)
        wy_copy(n).start()

    def w_fourth(n):
        wy_copy(n).wait_recv()
        w_all[n, at[first_axis(n)]] = (w_y[n].astype(f32) + w_y_in[n].astype(f32)).astype(bf16)
        for step in (1, 2, 3):
            wg_copy(n, step).start()

    def w_end(n):
        for step in (1, 2, 3):
            wg_copy(n, step).wait_recv()
        w_grads[n] = w_all[n]

    br_near = remote(grad_branch, branch_in.at[head], br_send.at[0], br_recv.at[0], here.partner())
    br_far = remote(grad_branch, branch_in.at[head], br_send.at[1], br_recv.at[1], here.along("y", 2))
    br_pass = remote(branch_in.at[far], branch_in.at[far], br_send.at[2], br_recv.at[2], here.partner())
    branch_in[head] = grad_branch[...]
    pair_back[head] = grad_pair[head]
    last_back[head] = grad_last[head]

    zeros = jnp.zeros((TOK, 64), bf16)
    loads[0].wait()
    for h in range(HEADS_HERE):
        query = qkv[h * 3]
        queries[h] = jnp.concatenate([zeros, query], axis=1)
        keys_t[h] = qkv[h * 3 + 1].astype(f32).T.astype(bf16)

    def outer_in(h):
        if h != 1:
            for way in range(3):
                mix_copy(h // 2, way).wait_recv()
        for j in range(4):
            block = last_back[j] if h == 2 else pair_back[j]
            lanes = slice(64, 128) if h == 1 else slice(0, 64)
            mixed_wide[j * ROWS : j * ROWS + ROWS, :] = block.astype(f32)[:, lanes]
        outer_back[h] = jnp.concatenate([mixed_wide[...].astype(bf16), zeros], axis=1)

    outer_in(0)
    br_far.start()
    br_near.start()
    for k in (1, 2, 3, 4, 5, 6, 7, 11):
        loads[k].wait()

    def branch_on():
        br_far.wait_recv()
        br_pass.start()

    def branch_end():
        br_near.wait_recv()
        br_pass.wait_recv()
        grad = jnp.zeros((192, D), f32)
        for j in range(4):
            some = jnp.concatenate([mixed_pair[j], unfold(mixed_last[j])], axis=1)
            grad = grad + dot_tn(some, branch_in[j])
        w_begin(0, grad)

    def sum_on(phase):
        total = sums.finish(phase)
        if phase < 3:
            sums.start(phase + 1)
        else:
            small_first[...] = total

    def ff_on(phase):
        for kind in (0, 1):
            ff_add(kind, phase)
            if phase < 2:
                ff_start(kind, phase + 1)

    chip = head // 2
    lane = lax.broadcasted_iota(jnp.int32, (TOK, 128), 1)

    def attend(h, carry):
        def score(k):
            chunk = slice(k * QCHUNK, k * QCHUNK + QCHUNK)
            scores = dot_nt(qkv[h * 3 + 1], qkv[h * 3, chunk, :])
            return scores, dot_nt(qkv[h * 3 + 2], outer_back[h, chunk, 0:64])

        ready = score(0)
        for k in range(CHUNKS):
            chunk = slice(k * QCHUNK, k * QCHUNK + QCHUNK)
            scores, grad_weights = ready
            if k + 1 < CHUNKS:
                ready = score(k + 1)
            given = outer_back[h, chunk, :]
            weights = jnp.exp(scores - lse[h * CHUNKS + k, 0:1, :])
            delta = jnp.sum(
                (given[:, 0:64].astype(f32) * mixed[h, chunk, :]).T, axis=0, keepdims=True
            )
            grad_scores = (weights * (grad_weights - delta)).astype(bf16)
            share = dot_nn(weights.astype(bf16), given) + dot_nn(grad_scores, queries[h, chunk, :])
            if k == 0:
                grad_kv[...] = share
            else:
                grad_kv[...] += share
            grad_q[chunk, 0:64] = dot_nn(keys_t[h], grad_scores).T * 0.125

        both = grad_kv[...]
        first = jnp.where(lane < 64, grad_q[...], both)
        packed_back[:, 0:128] = first.astype(bf16)
        packed_back[:, 128:192] = both[:, 0:64].astype(bf16)
        @pl.when(h < HEADS_HERE - 1)
        def _():
            for k, half in enumerate((1 - chip, chip)):
                share = dot_nn(
                    packed_back[pl.ds(pl.multiple_of(half * 784, 16), 784), :],
                    w_qkv[pl.ds(pl.multiple_of(h * 192, 16), 192), :],
                )
                for j in (0, 1):
                    some = share[j * ROWS : j * ROWS + ROWS]

                    @pl.when(h == 0)
                    def _():
                        input_back[half, j] = some

                    @pl.when(h > 0)
                    def _():
                        input_back[half, j] += some

                pl.when(h == HEADS_HERE - 2)(partial(pair_start, k, half))

        @pl.when(h == HEADS_HERE - 1)
        def _():
            for j in range(4):
                own = slice(j * ROWS, j * ROWS + ROWS)
                last_out[j] = first[own].astype(bf16)
                value_out[j] = fold(both, j * ROWS)
            for way in (1, 2, 0):
                for k in (0, 1):
                    head_copy(k, way).start()

        column_sums[pl.ds(h, 1), :] = jnp.sum(packed_back[...].astype(f32), axis=0, keepdims=True)

        w_grad = dot_tn(packed_back[...], normed[...])
        for n in range(HEADS_HERE):
            pl.when(h == n)(partial(w_begin, n + 1, w_grad))

        @pl.when(h == 0)
        def _():
            outer_in(1)
            sum_on(0)

        @pl.when(h == HEADS_HERE - 2)
        def _():
            pair_copies[0].wait_recv()
            far_out[...] = (input_back[1 - chip, core] + pair_in[0].astype(f32)).astype(bf16)
            far_copy.start()

        @pl.when(h == 1)
        def _():
            outer_in(2)
            sum_on(1)
            branch_on()

        return carry

    pair_copies = [
        remote(pair_out.at[k], pair_in.at[k], in_send.at[k], in_recv.at[k], here.partner()) for k in (0, 1)
    ]
    far_copy = remote(far_out, far_in, in_send.at[2], in_recv.at[2], here.along("y", 2))

    def head_copy(k, way):
        other, device = (
            (mate, here.partner()), (far, here.along("y", 2)), (far_mate, here.across()),
        )[way]
        src, dst = ((last_out, last_in), (value_out, value_in))[k]
        return remote(src.at[other], dst.at[head], head_send.at[k, way], head_recv.at[k, way], device)

    def pair_start(k, half):
        pair_out[k] = input_back[half, 1 - core].astype(bf16)
        pair_copies[k].start()

    lax.fori_loop(0, HEADS_HERE, attend, 0)

    ff_on(0)
    branch_end()
    w_second(1)
    w_second(2)
    sum_on(2)
    w_second(3)
    w_third(1)
    w_third(2)
    w_second(0)
    sum_on(3)

    masked = row_mask(cubes, head)
    start = jnp.where(masked > 0.5, params[MASK : MASK + 1, 0:D], tokens[...].astype(f32))
    unit1, inverse1 = unit_of(start)
    pair_copies[1].wait_recv()
    far_copy.wait_recv()
    last_in[head] = last_out[head]
    value_in[head] = value_out[head]
    loads[10].wait()
    back = input_back[chip, core] + pair_in[1].astype(f32) + far_in[...].astype(f32)
    for way in range(3):
        for k in (0, 1):
            head_copy(k, way).wait_recv()
    for j in range(4):
        some = jnp.concatenate([last_in[j], unfold(value_in[j])], axis=1)
        back = back + dot_nn(some, w_last[j])
    grad_start = grad_middle[...] + unit_back(
        back * params[GAIN1 : GAIN1 + 1, 0:D], unit1, inverse1
    )
    tokens_grad[...] = jnp.where(masked > 0.5, 0.0, grad_start)
    totals = [
        jnp.sum(v, axis=0, keepdims=True)
        for v in (back * unit1, back, jnp.where(masked > 0.5, grad_start, 0.0))
    ]
    held_last[0, :, 0:384] = jnp.concatenate(
        [v[:, k * 384 : k * 384 + 384] for v in totals for k in (0, 1)] + [jnp.zeros((2, 384), f32)],
        axis=0,
    )
    line = lax.broadcasted_iota(jnp.int32, (8, 192), 0)
    of_query = jnp.concatenate([column_sums[h : h + 1, 0:64] for h in range(HEADS_HERE)], axis=1)
    of_value = jnp.concatenate([column_sums[h : h + 1, 128:192] for h in range(HEADS_HERE)], axis=1)
    held_last[0, :, 384:576] = jnp.where(
        line == 2 * head, of_query, jnp.where(line == 2 * head + 1, of_value, 0.0)
    )
    held_last[0, :, 576:640] = jnp.zeros((8, 64), f32)
    last = SmallSum(here, held_last, arrived_last, last_send, last_recv)
    last.start(0)
    w_third(3)
    last.finish(0)
    last.start(1)
    w_third(0)
    w_fourth(1)
    w_fourth(2)
    ff_on(1)
    last.finish(1)
    last.start(2)
    w_fourth(3)
    w_fourth(0)
    ff_on(2)
    mate_copy = remote(
        ff_last.at[:, pl.ds(pl.multiple_of((1 - core) * 24, 8), 24), :], ff_mate,
        mate_sem.at[0], mate_sem.at[1], here.partner(),
    )
    mate_copy.start()
    last.finish(2)
    last.start(3)
    w_end(1)
    w_end(2)
    w_end(3)
    mate_copy.wait_recv()
    for kind, target in ((0, w_fc1_grad), (1, w_fc2_grad)):
        target[:, pl.ds(pl.multiple_of(core * UNITS, UNITS), UNITS)] = ff_last[
            kind, pl.ds(pl.multiple_of(core * 24, 8), 24), :
        ]
        target[:, pl.ds(pl.multiple_of((1 - core) * UNITS, UNITS), UNITS)] = ff_mate[kind]
    w_end(0)
    small_last[...] = last.finish(3)

    sums.drain()
    last.drain()
    for copy in [br_near, br_far, br_pass, far_copy, mate_copy] + pair_copies:
        copy.wait_send()
    for way in range(3):
        for k in (0, 1):
            head_copy(k, way).wait_send()
    for k in (0, 1):
        for way in range(3):
            mix_copy(k, way).wait_send()
    for kind in (0, 1):
        for phase in range(3):
            for step in (1, 2, 3):
                ff_copy(kind, phase, step).wait_send()
    for n in range(4):
        for step in (1, 2, 3):
            wx_copy(n, step).wait_send()
            wz_copy(n, step).wait_send()
            wg_copy(n, step).wait_send()
        wy_copy(n).wait_send()


def backward_call(*args):
    loaded = (
        ((ROWS, D), f32),
        ((ROWS, D), bf16),
        ((TOK, D), bf16),
        ((9, TOK, 64), bf16),
        ((HEADS_HERE * CHUNKS, 8, QCHUNK), f32),
        ((HEADS_HERE, TOK, 64), f32),
        ((4, ROWS, 128), bf16),
        ((4, 200, 128), bf16),
        ((576, D), bf16),
        ((4, 192, D), bf16),
    )
    return pl.pallas_call(
        backward_kernel,
        out_shape=(
            shape((ROWS, D), f32),
            shape((8, D + UNITS), f32),
            shape((8, 640), f32),
            shape((4, 4, 288, 128)),
            shape((24, D), f32),
            shape((24, D), f32),
        ),
        in_specs=[VM] * 6 + [ANY] * 11,
        out_specs=(VM,) * 6,
        scratch_shapes=[pltpu.VMEM(*k) for k in loaded]
        + [
            pltpu.VMEM((2, 3, 4, 4, 48, 128), bf16),
            pltpu.VMEM((4, ROWS, 128), bf16),
            pltpu.VMEM((4, ROWS, 64), bf16),
            pltpu.VMEM((TOK, 64), f32),
            pltpu.VMEM((HEADS_HERE, TOK, 128), bf16),
            pltpu.VMEM((HEADS_HERE, TOK, 128), bf16),
            pltpu.VMEM((HEADS_HERE, 64, TOK), bf16),
            pltpu.VMEM((TOK, 128), f32),
            pltpu.VMEM((TOK, 128), f32),
            pltpu.VMEM((TOK, 192), bf16),
            pltpu.VMEM((4, ROWS, D), bf16),
            pltpu.VMEM((2, 2, ROWS, D), f32),
            pltpu.VMEM((2, ROWS, D), bf16),
            pltpu.VMEM((2, ROWS, D), bf16),
            pltpu.VMEM((ROWS, D), bf16),
            pltpu.VMEM((ROWS, D), bf16),
            pltpu.VMEM((4, 8, D + UNITS), f32),
            pltpu.VMEM((10, 8, D + UNITS), f32),
            pltpu.VMEM((4, 8, 640), f32),
            pltpu.VMEM((10, 8, 640), f32),
            pltpu.VMEM((2, 3, 3, 4, 4, 48, 128), bf16),
            pltpu.VMEM((2, 3, 4, 4, 48, 128), bf16),
            pltpu.VMEM((2, 3, 3, 4, 48, 128), bf16),
            pltpu.VMEM((2, 3, 4, 48, 128), bf16),
            pltpu.VMEM((2, 3, 3, 48, 128), bf16),
            pltpu.VMEM((2, 48, UNITS), f32),
            pltpu.VMEM((2, 24, UNITS), f32),
            pltpu.VMEM((4, 4, 288, 128), bf16),
            pltpu.VMEM((4, 3, 288, 128), bf16),
            pltpu.VMEM((4, 288, 128), bf16),
            pltpu.VMEM((4, 3, 288, 128), bf16),
            pltpu.VMEM((4, 288, 128), bf16),
            pltpu.VMEM((4, 288, 128), bf16),
            pltpu.VMEM((4, 4, 288, 128), bf16),
            pltpu.VMEM((8, 192), f32),
            DMA((2, 3)), DMA((2, 3)), DMA((3,)), DMA((3,)), DMA((3,)), DMA((3,)),
            DMA((10,)), DMA((10,)), DMA((10,)), DMA((10,)),
            DMA((2, 3, 3)), DMA((2, 3, 3)), DMA((2,)),
            DMA((4, 3)), DMA((4, 3)), DMA((4, 3)), DMA((4, 3)), DMA((4,)), DMA((4,)), DMA((4, 3)), DMA((4, 3)),
            DMA((12,)),
            pltpu.VMEM((4, ROWS, 128), bf16),
            pltpu.VMEM((4, ROWS, 128), bf16),
            pltpu.VMEM((4, 200, 128), bf16),
            pltpu.VMEM((4, 200, 128), bf16),
            DMA((2, 3)), DMA((2, 3)),
        ],
        name="attention_backward",
        compiler_params=pltpu.CompilerParams(
            collective_id=2, has_side_effects=True, vmem_limit_bytes=VMEM_LIMIT
        ),
    )(*args)


def results_kernel(
    block_in, tokens_in, w_grads, w_fc1_in, w_fc2_in, first, last,
    block_out, tokens_grad, mask_grad, gain1_grad, shift1_grad, w_qkv_grad, qv_grad, w_out_grad,
    proj_grad, gain2_grad, shift2_grad, w_fc1_grad, fc1_grad, w_fc2_grad, fc2_grad,
):
    here = Place()
    pairs = (
        (block_in, block_out), (tokens_in, tokens_grad), (w_fc1_in, w_fc1_grad), (w_fc2_in, w_fc2_grad)
    )
    for src, dst in pairs:
        dst[...] = src[...]

    def pick(line, offset, count):
        column = lax.broadcasted_iota(jnp.int32, line.shape, 1) - offset
        spot = lax.broadcasted_iota(jnp.int32, (1, count), 1)
        out = jnp.zeros((1, count), f32)
        for j in range(count):
            one = jnp.sum(jnp.where(column == j, line, 0.0), axis=1, keepdims=True)
            out = jnp.where(spot == j, one, out)
        return out

    index = here.index
    for row, target in ((0, proj_grad), (1, gain2_grad), (2, shift2_grad), (3, fc2_grad)):
        target[...] = pick(first[row : row + 1, 0:D], index * 6, 6)
    fc1_grad[...] = pick(first[pl.ds(index // 16, 1), D : D + UNITS], (index % 16) * 24, 24)
    for k, target in enumerate((gain1_grad, shift1_grad, mask_grad)):
        target[...] = pick(last[pl.ds(2 * k + index // 64, 1), 0:384], (index % 64) * 6, 6)
    for k in (0, 1):
        qv_grad[k : k + 1, :] = last[pl.ds(2 * here.head + k, 1), 384:576]
    for n in range(4):
        for s in range(6):
            lanes = slice(s * 128, s * 128 + 128)
            start = s * 192
            for chunk in range(4):
                low, high = max(start, chunk * 288), min(start + 192, chunk * 288 + 288)
                if low < high:
                    got = w_grads[n, chunk, low - chunk * 288 : high - chunk * 288, :].astype(f32)
                    if n == 0:
                        w_out_grad[low - start : high - start, lanes] = got
                    else:
                        base = (n - 1) * 192 - start
                        w_qkv_grad[base + low : base + high, lanes] = got


def results_call(*args):
    six = shape((1, 6), f32)
    return pl.pallas_call(
        results_kernel,
        out_shape=(
            shape((ROWS, D), f32), shape((ROWS, D), f32), six, six, six, shape((576, D), f32),
            shape((2, 192), f32), shape((192, D), f32), six, six, six,
            shape((24, D), f32), shape((1, 24), f32), shape((24, D), f32), six,
        ),
        in_specs=[VM] * 7,
        out_specs=(VM,) * 15,
        name="results",
        compiler_params=pltpu.CompilerParams(vmem_limit_bytes=VMEM_LIMIT),
    )(*args)


def body(
    tokens, cube_mask, mask_token, norm1_gain, norm1_bias, w_qkv, qv_bias, w_out, proj_bias,
    norm2_gain, norm2_bias, w_fc1, fc1_bias, w_fc2, fc2_bias, cotangent,
):
    small = jnp.stack(
        [mask_token, norm1_gain, norm1_bias, proj_bias, norm2_gain, norm2_bias, fc2_bias, fc2_bias]
    )
    w_qkv_t = w_qkv.T
    (
        params, normed, qkv, lse, mixed, pair_out, last_out, pair_in, last_in, w_out_all, w_last_all, weights,
    ) = forward_call(
        small, fc1_bias[None], cube_mask, tokens, w_qkv_t, qv_bias, w_out, w_fc1.T, w_fc2,
    )
    block_out, grad_middle, grad_branch, grad_pair, grad_last, small_grads, reduced = feed_forward_call(
        cube_mask, params, tokens, cotangent, pair_in, last_in, w_out_all, weights.reshape(6, 64, 96, 128),
    )
    tokens_grad, small_first, small_last, w_grads, w_fc1_grad, w_fc2_grad = backward_call(
        cube_mask, params, grad_pair, grad_last, grad_branch, small_grads, reduced.reshape(3, 4, 4, 4, 96, 128),
        grad_middle, tokens, normed.reshape(TOK, D), qkv, lse, mixed, pair_out, last_out,
        w_qkv_t, w_last_all,
    )
    outs = list(
        results_call(block_out, tokens_grad, w_grads, w_fc1_grad, w_fc2_grad, small_first, small_last)
    )
    for k in (2, 3, 4, 8, 9, 10, 12, 14):
        outs[k] = outs[k].reshape(-1)
    outs[5] = outs[5].T
    outs[11] = outs[11].T
    return tuple(outs)


def solution(mesh):
    every = P(("clip", "head"))
    rows = P(("clip", "head"), None)
    columns = P(None, ("clip", "head"))
    in_specs = (
        rows, P("clip", None), every, every, every, P(None, "head"), P(None, "head"),
        P("head", None), every, every, every, columns, every, rows, every, rows,
    )
    out_specs = (
        rows, rows, every, every, every, P(None, "head"), P(None, "head"), P("head", None),
        every, every, every, columns, every, rows, every,
    )
    return jax.shard_map(body, mesh=mesh, in_specs=in_specs, out_specs=out_specs, check_vma=False)
```
